128 devices in a mesh: level: 4 (over x), dom: 32 (over z, y, core).
Axes of the slice: x: 4, y: 4, z: 4, core: 2. Of those that a mesh axis runs over, the one named last changes fastest.
Arguments:
- rhs: float32 [4, 32, 4, 64, 1024], P('level', 'dom'), may hold values from -6 to 6
- dinv: bfloat16 [4, 32, 4, 64, 4096], P('level', 'dom'), may hold values from -0.75 to 0.75
- lower_local: bfloat16 [4, 32, 3, 64, 3, 4096], P('level', 'dom'), may hold values from -0.41992188 to 0.41992188
- lower_nbrs: int32 [4, 32, 3, 64, 3], P('level', 'dom'), may hold values from 0 to 63
- upper_local: bfloat16 [4, 32, 3, 64, 3, 4096], P('level', 'dom'), may hold values from -0.41992188 to 0.41992188
- upper_nbrs: int32 [4, 32, 3, 64, 3], P('level', 'dom'), may hold values from 0 to 63
- lower_remote: bfloat16 [4, 32, 64, 3, 4096], P('level', 'dom'), may hold values from -0.59765625 to 0.59765625
- upper_remote: bfloat16 [4, 32, 64, 3, 4096], P('level', 'dom'), may hold values from -0.59765625 to 0.59765625
- remote_slots: int32 [4, 32, 64, 3], P('level', 'dom'), may hold values from 0 to 127
- send_list: int32 [4, 32, 32, 4], P('level', 'dom'), may hold values from 0 to 63
Outputs:
- preconditioned: bfloat16 [4, 32, 4, 64, 1024], P('level', 'dom')
The draws below stay inside these ranges and needn't reach their ends.
Inputs may be any that keep to these rules, and one draw needn't show every extreme that they name: `send_list`: A block may be listed several times.
All inputs are finite; a program needn't handle non-finite values.
Results may differ from the reference program's by a relative error of at most 0.04.
Values may be sent and summed in bfloat16 or wider, within the bound.
A program may use at most 192 MiB of HBM per device.

```python
import jax
import jax.numpy as jnp
from jax import lax

BS = 64
NVEC = 16
KL = 3
KR = 3
COLORS = 4
SEND = 4
NBC = 64
LEVELS = 4
PARTS_SIZE = 32
SLOTS = 128
FEAT = 1024
MAT = 4096


def plant(entries, key, least, high):
    longest = entries.shape.index(max(entries.shape))
    spots = []
    for shift in (0, 1):
        where = [jax.random.randint(jax.random.fold_in(key, axis), (), 0, length) for axis, length in enumerate(entries.shape)]
        where[longest] = (where[longest] + shift) % entries.shape[longest]
        spots.append(tuple(where))
    return entries.at[spots[0]].set(least).at[spots[1]].set(high)


def steps_of(own_key, shape, split, smallest, high):
    gain = 1.0
    for position, blocks in split:
        draws = jax.random.uniform(jax.random.fold_in(jax.random.fold_in(own_key, 6), position), (blocks,), jnp.float32, smallest / len(split), high / len(split))
        gain = gain * jnp.repeat(jnp.exp(draws), shape[position] // blocks).reshape((-1,) + (1,) * (len(shape) - 1 - position))
    return gain


def bell_draw(own_key, shape, spread, most, cuts=(), held_as=jnp.bfloat16):
    level = steps_of(own_key, shape, cuts, -0.22, 0.18) if cuts else 1.0
    array = jax.random.normal(own_key, shape, jnp.float32) * spread * level
    return jnp.minimum(jnp.maximum(array, -most), most).astype(held_as)


def setup_inputs(seed: int = 0) -> dict:
    arg_keys = jax.random.split(jax.random.key(seed), 11)
    rhs = bell_draw(arg_keys[0], (LEVELS, PARTS_SIZE, COLORS, NBC, FEAT), 1.0, 6.0, ((0, 4), (1, 32)), jnp.float32)
    dinv = bell_draw(arg_keys[1], (LEVELS, PARTS_SIZE, COLORS, NBC, MAT), BS ** -0.5, 0.75, ((0, 4), (1, 32)))
    lower_local = bell_draw(arg_keys[2], (LEVELS, PARTS_SIZE, COLORS - 1, NBC, KL, MAT), 0.07, 0.41992188, ((0, 4), (1, 32)))
    lower_nbrs = plant(jax.random.randint(arg_keys[3], (LEVELS, PARTS_SIZE, COLORS - 1, NBC, KL), 0, NBC), jax.random.fold_in(arg_keys[3], 1), 0, NBC - 1).astype(jnp.int32)
    upper_local = bell_draw(arg_keys[4], (LEVELS, PARTS_SIZE, COLORS - 1, NBC, KL, MAT), 0.07, 0.41992188, ((0, 4), (1, 32)))
    upper_nbrs = plant(jax.random.randint(arg_keys[5], (LEVELS, PARTS_SIZE, COLORS - 1, NBC, KL), 0, NBC), jax.random.fold_in(arg_keys[5], 1), 0, NBC - 1).astype(jnp.int32)
    lower_remote = bell_draw(arg_keys[6], (LEVELS, PARTS_SIZE, NBC, KR, MAT), 0.1, 0.59765625, ((0, 4), (1, 32)))
    upper_remote = bell_draw(arg_keys[7], (LEVELS, PARTS_SIZE, NBC, KR, MAT), 0.1, 0.59765625, ((0, 4), (1, 32)))
    remote_slots = plant(jax.random.randint(arg_keys[8], (LEVELS, PARTS_SIZE, NBC, KR), 0, SLOTS), jax.random.fold_in(arg_keys[8], 1), 0, SLOTS - 1).astype(jnp.int32)
    send_list = plant(jax.random.randint(arg_keys[9], (LEVELS, PARTS_SIZE, PARTS_SIZE, SEND), 0, NBC), jax.random.fold_in(arg_keys[9], 1), 0, NBC - 1).astype(jnp.int32)
    return dict(rhs=rhs, dinv=dinv, lower_local=lower_local, lower_nbrs=lower_nbrs, upper_local=upper_local, upper_nbrs=upper_nbrs, lower_remote=lower_remote, upper_remote=upper_remote, remote_slots=remote_slots, send_list=send_list)


HIGHEST_PRECISION = lax.Precision.HIGHEST


def pair_apply(matrices, vectors_in):
    vectors_in = lax.optimization_barrier(vectors_in)
    mat_full = matrices.astype(jnp.float32).reshape(matrices.shape[:-1] + (BS, BS))
    vec_full = vectors_in.astype(jnp.float32).reshape(vectors_in.shape[:-1] + (NVEC, BS))
    result = jnp.einsum('...oi,...vi->...vo', mat_full, vec_full, precision=HIGHEST_PRECISION)
    return result.reshape(result.shape[:-2] + (NVEC * BS,))


def take_rows(table, index):
    return jax.vmap(lambda table_one, index_one: table_one[index_one])(table, index)


def reference(rhs, dinv, lower_local, lower_nbrs, upper_local, upper_nbrs, lower_remote, upper_remote, remote_slots, send_list):
    features = NVEC * BS
    solved_levels = []
    for level_index in range(LEVELS):
        if level_index == 0:
            received = jnp.zeros((PARTS_SIZE, SLOTS, features), jnp.bfloat16)
        else:
            picked = take_rows(solved_levels[level_index - 1][:, COLORS - 1], send_list[level_index - 1])
            received = jnp.transpose(picked, (1, 0, 2, 3)).reshape(PARTS_SIZE, SLOTS, features)
        remote_rows = take_rows(received, remote_slots[level_index])
        columns = [(rhs[level_index, :, 0] - jnp.sum(pair_apply(lower_remote[level_index], remote_rows), axis=2)).astype(jnp.bfloat16)]
        for color_index in range(1, COLORS):
            near_rows = take_rows(columns[-1], lower_nbrs[level_index, :, color_index - 1])
            columns.append((rhs[level_index, :, color_index] - jnp.sum(pair_apply(lower_local[level_index, :, color_index - 1], near_rows), axis=2)).astype(jnp.bfloat16))
        solved_levels.append(jnp.stack(columns, axis=1))
    answers = [None] * LEVELS
    for level_index in range(LEVELS - 1, -1, -1):
        if level_index == LEVELS - 1:
            upward = jnp.zeros((PARTS_SIZE, NBC, features), jnp.float32)
        else:
            leading = answers[level_index + 1][:, 0]
            edge_terms = pair_apply(upper_remote[level_index + 1], jnp.broadcast_to(leading[:, :, None], (PARTS_SIZE, NBC, KR, features)))
            slot_sums = jax.vmap(lambda edge_one, index_one: jax.ops.segment_sum(edge_one.reshape(NBC * KR, features), index_one.reshape(NBC * KR), num_segments=SLOTS))(edge_terms, remote_slots[level_index + 1])
            per_owner = jnp.transpose(slot_sums.reshape(PARTS_SIZE, PARTS_SIZE, SEND, features), (1, 0, 2, 3))
            upward = jax.vmap(lambda value_one, index_one: jax.ops.segment_sum(value_one.reshape(PARTS_SIZE * SEND, features), index_one.reshape(PARTS_SIZE * SEND), num_segments=NBC))(per_owner, send_list[level_index])
        columns = [None] * COLORS
        top_rows = (solved_levels[level_index][:, COLORS - 1].astype(jnp.float32) - upward).astype(jnp.bfloat16)
        columns[COLORS - 1] = pair_apply(dinv[level_index, :, COLORS - 1], top_rows).astype(jnp.bfloat16)
        for color_index in range(COLORS - 2, -1, -1):
            near_rows = take_rows(columns[color_index + 1], upper_nbrs[level_index, :, color_index])
            reduced = (solved_levels[level_index][:, color_index].astype(jnp.float32) - jnp.sum(pair_apply(upper_local[level_index, :, color_index], near_rows), axis=2)).astype(jnp.bfloat16)
            columns[color_index] = pair_apply(dinv[level_index, :, color_index], reduced).astype(jnp.bfloat16)
        answers[level_index] = jnp.stack(columns, axis=1)
    return jnp.stack(answers, axis=0)
```

```python
import functools

import jax
import jax.numpy as jnp
from jax import lax
from jax.experimental import pallas as pl
from jax.experimental.pallas import tpu as pltpu
from jax.sharding import PartitionSpec as P

BS = 64
GROUP = 4
MESH = pl.DeviceIdType.MESH
BF16 = jnp.bfloat16
F32 = jnp.float32


def dot_rows(left, right):
    return lax.dot_general(left, right, (((1,), (1,)), ((), ())), preferred_element_type=F32)


def kernel(
    levels,
    parts,
    low_idx,
    up_idx,
    slot_idx,
    send_idx,
    edge_code,
    owner_code,
    rhs,
    w_low,
    w_up,
    w_lrem,
    w_urem,
    w_dinv,
    out,
    solved,
    table,
    rtable,
    boundary,
    upward,
    terms,
    edge_hot,
    owner_hot,
    send_f,
    recv_f,
    send_b,
    recv_b,
    sems,
):
    level = lax.axis_index("level")
    me = lax.axis_index("dom")
    colors, blocks = solved.shape[0], solved.shape[1]
    groups = blocks // GROUP
    rows_per_peer = send_f.shape[0] // parts

    barrier = pltpu.get_barrier_semaphore()

    def greet(step, _):
        peer = lax.rem(me + step, parts)

        @pl.when(level > 0)
        def _():
            pl.semaphore_signal(barrier, inc=1, device_id=(level - 1, peer), device_id_type=MESH)

        @pl.when(level < levels - 1)
        def _():
            pl.semaphore_signal(barrier, inc=1, device_id=(level + 1, peer), device_id_type=MESH)

        return 0

    lax.fori_loop(0, parts, greet, 0)

    low_half16 = lax.broadcasted_iota(jnp.int32, (16, 128), 1) < BS
    low_half8 = lax.broadcasted_iota(jnp.int32, (8, 128), 1) < BS
    zero16 = jnp.zeros((16, 128), F32)

    def doubled(packed):
        turned = pltpu.roll(packed, BS, 1)
        return jnp.concatenate(
            [jnp.where(low_half8, packed, turned), jnp.where(low_half8, turned, packed)], axis=0
        )

    def paired(rows):
        return jnp.where(low_half8, rows[:8], rows[8:])

    def gathered(idx, base, source, group):
        pieces = []
        for member in range(GROUP):
            at = base + (group * GROUP + member) * 3
            first, second, third = source[idx[at]], source[idx[at + 1]], source[idx[at + 2]]
            pieces.append(
                jnp.concatenate([jnp.where(low_half16, first, second), third], axis=1)
            )
        return jnp.concatenate(pieces, axis=0)

    def own_block(product, member):
        piece = product[member * 16 : member * 16 + 16, (member // 2) * 128 : (member // 2) * 128 + 128]
        turned = pltpu.roll(piece, BS, 1)
        return jnp.where(low_half16, piece, turned) if member % 2 == 0 else jnp.where(low_half16, turned, piece)

    def spread(members):
        pieces = []
        for member, value in enumerate(members):
            kept = jnp.where(low_half16, value, zero16) if member % 2 == 0 else jnp.where(low_half16, zero16, value)
            pair = [kept, zero16] if member < 2 else [zero16, kept]
            pieces.append(jnp.concatenate(pair, axis=1).astype(BF16))
        return jnp.concatenate(pieces, axis=0)

    def forward_step(weights, windex, idx, base, source, color):
        def body(group, _):
            product = dot_rows(gathered(idx, base, source, group), weights[windex + group])
            for member in range(GROUP):
                block = group * GROUP + member
                value = rhs[color, block] - own_block(product, member)
                solved[color, block] = value.astype(BF16)
            return 0

        lax.fori_loop(0, groups, body, 0, unroll=4)

    @pl.when(level == 0)
    def _():
        def body(block, _):
            solved[0, block] = rhs[0, block].astype(BF16)
            return 0

        lax.fori_loop(0, blocks, body, 0, unroll=8)

    @pl.when(level > 0)
    def _():
        pltpu.make_async_copy(recv_f, recv_f, sems.at[1]).wait()

        def body(pair, _):
            both = recv_f[pl.ds(pl.multiple_of(pair * 16, 16), 16), :].astype(F32)
            rtable[pair * 2] = doubled(both[:8]).astype(BF16)
            rtable[pair * 2 + 1] = doubled(both[8:]).astype(BF16)
            return 0

        lax.fori_loop(0, recv_f.shape[0] // 16, body, 0, unroll=8)
        forward_step(w_lrem, 0, slot_idx, 0, rtable, 0)

    def color_body(color, _):
        forward_step(w_low, (color - 1) * groups, low_idx, (color - 1) * blocks * 3, solved.at[color - 1], color)
        return 0

    lax.fori_loop(1, colors, color_body, 0)

    pl.semaphore_wait(
        barrier, parts * ((level > 0).astype(jnp.int32) + (level < levels - 1).astype(jnp.int32))
    )

    @pl.when(level < levels - 1)
    def _():
        def pack(block, _):
            boundary[block] = paired(solved[colors - 1, block].astype(F32))
            return 0

        lax.fori_loop(0, blocks, pack, 0, unroll=8)

        def body(pair, _):
            both = jnp.concatenate(
                [boundary[send_idx[pair * 2]], boundary[send_idx[pair * 2 + 1]]], axis=0
            )
            send_f[pl.ds(pl.multiple_of(pair * 16, 16), 16), :] = both.astype(BF16)
            return 0

        lax.fori_loop(0, send_f.shape[0] // 16, body, 0, unroll=8)

        def push(step, _):
            peer = lax.rem(me + step, parts)
            pltpu.make_async_remote_copy(
                src_ref=send_f.at[pl.ds(pl.multiple_of(peer * rows_per_peer, 16), rows_per_peer)],
                dst_ref=recv_f.at[pl.ds(pl.multiple_of(me * rows_per_peer, 16), rows_per_peer)],
                send_sem=sems.at[0],
                recv_sem=sems.at[1],
                device_id=(level + 1, peer),
                device_id_type=MESH,
            ).start()
            return 0

        lax.fori_loop(0, parts, push, 0)

    def hot_edge(chunk, _):
        rows = lax.broadcasted_iota(jnp.int32, (64, edge_hot.shape[1]), 0) + chunk * 64
        edge_hot[pl.ds(pl.multiple_of(chunk * 64, 64), 64), :] = jnp.where(
            rows == edge_code[...], 1.0, 0.0
        ).astype(BF16)
        return 0

    lax.fori_loop(0, edge_hot.shape[0] // 64, hot_edge, 0)

    def hot_owner(chunk, _):
        rows = lax.broadcasted_iota(jnp.int32, (64, owner_hot.shape[1]), 0) + chunk * 64
        owner_hot[pl.ds(pl.multiple_of(chunk * 64, 64), 64), :] = jnp.where(
            rows == owner_code[...], 1.0, 0.0
        ).astype(BF16)
        return 0

    lax.fori_loop(0, owner_hot.shape[0] // 64, hot_owner, 0)

    def finish(color, group, members):
        weights = w_dinv[color * groups + group]
        product = dot_rows(spread(members), jnp.concatenate([weights, weights], axis=0))
        outs = []
        for member in range(GROUP):
            value = product[member * 16 : member * 16 + 16]
            table[color, group * GROUP + member] = value.astype(BF16)
            outs.append(paired(value))
        out[color, pl.ds(pl.multiple_of(group * GROUP * 8, 32), GROUP * 8), :] = jnp.concatenate(
            outs, axis=0
        ).astype(BF16)

    @pl.when(level == levels - 1)
    def _():
        upward[...] = jnp.zeros_like(upward)

    @pl.when(level < levels - 1)
    def _():
        pltpu.make_async_copy(recv_b, recv_b, sems.at[3]).wait()
        upward[...] = jnp.dot(owner_hot[...], recv_b[...], preferred_element_type=F32)

    def last_color(group, _):
        members = []
        for member in range(GROUP):
            block = group * GROUP + member
            add = upward[pl.ds(pl.multiple_of(block * 8, 8), 8), :]
            members.append(solved[colors - 1, block].astype(F32) - doubled(add))
        finish(colors - 1, group, members)
        return 0

    lax.fori_loop(0, groups, last_color, 0, unroll=4)

    def back_color(step, _):
        color = colors - 2 - step
        source = table.at[color + 1]

        def body(group, _):
            product = dot_rows(
                gathered(up_idx, color * blocks * 3, source, group), w_up[color * groups + group]
            )
            members = [
                solved[color, group * GROUP + member].astype(F32) - own_block(product, member)
                for member in range(GROUP)
            ]
            finish(color, group, members)
            return 0

        lax.fori_loop(0, groups, body, 0, unroll=4)
        return 0

    lax.fori_loop(0, colors - 1, back_color, 0)

    @pl.when(level > 0)
    def _():
        def body(group, _):
            members = [table[0, group * GROUP + member].astype(F32) for member in range(GROUP)]
            product = dot_rows(spread(members), w_urem[group])
            pieces = []
            for member in range(GROUP):
                rows = product[member * 16 : member * 16 + 16]
                first, third = rows[:, :128], rows[:, 128:]
                turned = pltpu.roll(first, BS, 1)
                third_turned = pltpu.roll(third, BS, 1)
                pieces.append(jnp.where(low_half8, first[:8], turned[8:]))
                pieces.append(jnp.where(low_half8, turned[:8], first[8:]))
                pieces.append(jnp.where(low_half8, third[:8], third_turned[8:]))
            terms[pl.ds(pl.multiple_of(group * GROUP * 24, 96), GROUP * 24), :] = jnp.concatenate(
                pieces, axis=0
            ).astype(BF16)
            return 0

        lax.fori_loop(0, groups, body, 0, unroll=4)

        send_b[...] = jnp.dot(edge_hot[...], terms[...], preferred_element_type=F32).astype(BF16)

        def push(step, _):
            peer = lax.rem(me + step, parts)
            pltpu.make_async_remote_copy(
                src_ref=send_b.at[pl.ds(pl.multiple_of(peer * rows_per_peer, 16), rows_per_peer)],
                dst_ref=recv_b.at[pl.ds(pl.multiple_of(me * rows_per_peer, 16), rows_per_peer)],
                send_sem=sems.at[2],
                recv_sem=sems.at[3],
                device_id=(level - 1, peer),
                device_id_type=MESH,
            ).start()
            return 0

        lax.fori_loop(0, parts, push, 0)
        pltpu.make_async_copy(send_b, send_b, sems.at[2]).wait()

    @pl.when(level < levels - 1)
    def _():
        pltpu.make_async_copy(send_f, send_f, sems.at[0]).wait()


def per_device(
    levels,
    parts,
    rhs,
    dinv,
    lower_local,
    lower_nbrs,
    upper_local,
    upper_nbrs,
    lower_remote,
    upper_remote,
    remote_slots,
    send_list,
):
    colors, blocks, features = rhs.shape[2:]
    groups = blocks // GROUP
    slots = parts * send_list.shape[-1]

    def coupling_rows(matrices):
        count = matrices.shape[0]
        split = matrices.reshape(count, blocks, 3, BS, BS).transpose(0, 1, 3, 2, 4)
        flat = split.reshape(count * groups, GROUP * BS, 3 * BS)
        return jnp.pad(flat, ((0, 0), (0, 0), (0, BS)))

    w_low = coupling_rows(lower_local[0, 0])
    w_up = coupling_rows(upper_local[0, 0])
    w_lrem = coupling_rows(lower_remote[0])
    w_urem = (
        upper_remote[0, 0]
        .reshape(groups, GROUP, 3, BS, BS)
        .transpose(0, 2, 3, 1, 4)
        .reshape(groups, 3 * BS, GROUP * BS)
    )
    w_urem = jnp.pad(w_urem, ((0, 0), (0, BS), (0, 0)))
    w_dinv = (
        dinv[0, 0]
        .reshape(colors * groups, GROUP, BS, BS)
        .transpose(0, 2, 1, 3)
        .reshape(colors * groups, BS, GROUP * BS)
    )
    halves = rhs[0, 0].reshape(colors, blocks, 8, 2, BS).transpose(0, 1, 3, 2, 4)
    halves = halves.reshape(colors, blocks, 16, BS)
    right = jnp.concatenate([halves, halves], axis=-1)
    lanes = jnp.arange(8, dtype=jnp.int32)
    edge_code = (remote_slots.reshape(blocks * 3, 1) * 8 + lanes).reshape(1, blocks * 24)
    owner_code = (send_list.reshape(slots, 1) * 8 + lanes).reshape(1, slots * 8)

    smem = pl.BlockSpec(memory_space=pltpu.SMEM)
    vmem = pl.BlockSpec(memory_space=pltpu.VMEM)
    answer = pl.pallas_call(
        functools.partial(kernel, levels, parts),
        out_shape=jax.ShapeDtypeStruct((colors, blocks * 8, 128), BF16),
        in_specs=[smem] * 4 + [vmem] * 8,
        out_specs=vmem,
        scratch_shapes=[
            pltpu.VMEM((colors, blocks, 16, 128), BF16),
            pltpu.VMEM((colors, blocks, 16, 128), BF16),
            pltpu.VMEM((slots, 16, 128), BF16),
            pltpu.VMEM((blocks, 8, 128), F32),
            pltpu.VMEM((blocks * 8, 128), F32),
            pltpu.VMEM((blocks * 24, 128), BF16),
            pltpu.VMEM((slots * 8, blocks * 24), BF16),
            pltpu.VMEM((blocks * 8, slots * 8), BF16),
            pltpu.VMEM((slots * 8, 128), BF16),
            pltpu.VMEM((slots * 8, 128), BF16),
            pltpu.VMEM((slots * 8, 128), BF16),
            pltpu.VMEM((slots * 8, 128), BF16),
            pltpu.SemaphoreType.DMA((4,)),
        ],
        compiler_params=pltpu.CompilerParams(
            collective_id=0, has_side_effects=True, vmem_limit_bytes=60 * 1024 * 1024
        ),
        name="sweeps",
    )(
        lower_nbrs.reshape(-1),
        upper_nbrs.reshape(-1),
        remote_slots.reshape(-1),
        send_list.reshape(-1),
        edge_code,
        owner_code,
        right,
        w_low,
        w_up,
        w_lrem,
        w_urem,
        w_dinv,
    )
    return answer.reshape(1, 1, colors, blocks, features)


def solution(mesh):
    levels, parts = mesh.shape["level"], mesh.shape["dom"]
    return jax.shard_map(
        functools.partial(per_device, levels, parts),
        mesh=mesh,
        in_specs=(
            P("level", "dom", None, None, None),
            P("level", "dom", None, None, None),
            P("level", "dom", None, None, None, None),
            P("level", "dom", None, None, None),
            P("level", "dom", None, None, None, None),
            P("level", "dom", None, None, None),
            P("level", "dom", None, None, None),
            P("level", "dom", None, None, None),
            P("level", "dom", None, None),
            P("level", "dom", None, None),
        ),
        out_specs=P("level", "dom", None, None, None),
        check_vma=False,
    )
```

```python
import functools

import jax
import jax.numpy as jnp
from jax import lax
from jax.experimental import pallas as pl
from jax.experimental.pallas import tpu as pltpu
from jax.sharding import PartitionSpec as P

BS = 64
GROUP = 4
MESH = pl.DeviceIdType.MESH
BF16 = jnp.bfloat16
F32 = jnp.float32


def dot_rows(left, right):
    return lax.dot_general(left, right, (((1,), (1,)), ((), ())), preferred_element_type=F32)


def kernel(
    levels,
    parts,
    low_idx,
    up_idx,
    slot_idx,
    send_idx,
    rhs_hbm,
    low_hbm,
    up_hbm,
    lrem_hbm,
    urem_hbm,
    dinv_hbm,
    out,
    raw_rhs,
    raw,
    raw_urem,
    raw_dinv,
    weights,
    w_urem,
    w_dinv,
    rhs,
    mixed,
    solved,
    reduced,
    table,
    rtable,
    boundary,
    upward,
    terms,
    edge_code,
    owner_code,
    edge_hot,
    owner_hot,
    send_f,
    recv_f,
    send_b,
    recv_b,
    sems,
    load_sems,
):
    level = lax.axis_index("level")
    me = lax.axis_index("dom")
    colors, blocks = solved.shape[0], solved.shape[1]
    steps = colors - 1
    groups = blocks // GROUP
    per_peer = send_idx.shape[0]
    rows_per_peer = send_f.shape[0] // parts
    remote_piece = steps
    pieces = 2 * steps + 1

    def piece_source(piece):
        if piece < steps:
            return low_hbm.at[0, 0, piece]
        if piece == steps:
            return lrem_hbm.at[0, 0]
        return up_hbm.at[0, 0, piece - steps - 1]

    load_rhs = pltpu.make_async_copy(rhs_hbm.at[0, 0], raw_rhs, load_sems.at[pieces])
    load_urem = pltpu.make_async_copy(urem_hbm.at[0, 0], raw_urem, load_sems.at[pieces + 1])
    load_dinv = pltpu.make_async_copy(dinv_hbm.at[0, 0], raw_dinv, load_sems.at[pieces + 2])
    load_rhs.start()
    for piece in range(pieces):
        pltpu.make_async_copy(piece_source(piece), raw.at[piece], load_sems.at[piece]).start()
    load_dinv.start()
    load_urem.start()

    barrier = pltpu.get_barrier_semaphore()

    def greet(step, _):
        peer = lax.rem(me + step, parts)

        @pl.when(level > 0)
        def _():
            pl.semaphore_signal(barrier, inc=1, device_id=(level - 1, peer), device_id_type=MESH)

        @pl.when(level < levels - 1)
        def _():
            pl.semaphore_signal(barrier, inc=1, device_id=(level + 1, peer), device_id_type=MESH)

        return 0

    lax.fori_loop(0, parts, greet, 0)

    low_half16 = lax.broadcasted_iota(jnp.int32, (16, 128), 1) < BS
    low_half8 = lax.broadcasted_iota(jnp.int32, (8, 128), 1) < BS
    zero8 = jnp.zeros((8, 128), F32)
    zero16 = jnp.zeros((16, 128), BF16)

    def doubled(packed):
        turned = pltpu.roll(packed, BS, 1)
        return jnp.concatenate(
            [jnp.where(low_half8, packed, turned), jnp.where(low_half8, turned, packed)], axis=0
        )

    def paired(rows):
        return jnp.where(low_half8, rows[:8], rows[8:])

    def interleave(slot, first, second):
        first_turned = pltpu.roll(first, BS, 1)
        second_turned = pltpu.roll(second, BS, 1)
        mixed[slot, pl.ds(0, 8, stride=2), :] = jnp.where(low_half8, first, second_turned)
        mixed[slot, pl.ds(1, 8, stride=2), :] = jnp.where(low_half8, first_turned, second)

    def lines_of(source, first, quarter):
        lanes = slice(quarter * 1024, quarter * 1024 + 1024)
        part = source[pl.ds(pl.multiple_of(first, 16), 16), lanes]
        return part.astype(F32).reshape(16, 8, 128)

    def prepare_piece(piece, _):
        pltpu.make_async_copy(lrem_hbm.at[0, 0], raw.at[piece], load_sems.at[piece]).wait()

        def body(step, _):
            for quarter in range(4):
                lines = [lines_of(raw.at[piece, couple], step * 16, quarter) for couple in range(3)]
                for slot in range(16):
                    interleave(quarter * 32 + slot, lines[0][slot], lines[1][slot])
                    third = lines[2][slot]
                    turned = pltpu.roll(third, BS, 1)
                    at = quarter * 32 + 16 + slot
                    mixed[at, pl.ds(0, 8, stride=2), :] = jnp.where(low_half8, third, zero8)
                    mixed[at, pl.ds(1, 8, stride=2), :] = jnp.where(low_half8, turned, zero8)
                for slot in range(16):
                    group = piece * groups + step * GROUP + slot // GROUP
                    row = (slot % GROUP) * BS + quarter * 16
                    weights[group, row : row + 16, 0:128] = mixed[quarter * 32 + slot].astype(BF16)
                    weights[group, row : row + 16, 128:256] = mixed[quarter * 32 + 16 + slot].astype(BF16)
            return 0

        lax.fori_loop(0, blocks // 16, body, 0)
        return 0

    def prepare_rhs():
        load_rhs.wait()

        def body(step, _):
            color, first = step // (blocks // 8), lax.rem(step, blocks // 8) * 8
            lines = raw_rhs[color, pl.ds(pl.multiple_of(first, 8), 8), :].reshape(8, 8, 128)
            for slot in range(8):
                rhs[color, first + slot] = doubled(lines[slot])
            return 0

        lax.fori_loop(0, colors * blocks // 8, body, 0)

    def prepare_back():
        load_dinv.wait()

        def dinv_body(step, _):
            color, first = step // (blocks // 16), lax.rem(step, blocks // 16) * 16
            for quarter in range(4):
                lines = lines_of(raw_dinv.at[color], first, quarter)
                for pair in range(8):
                    interleave(quarter * 8 + pair, lines[2 * pair], lines[2 * pair + 1])
                for pair in range(8):
                    group = color * groups + first // GROUP + pair // 2
                    lanes = slice((pair % 2) * 128, (pair % 2) * 128 + 128)
                    value = mixed[quarter * 8 + pair].astype(BF16)
                    w_dinv[group, quarter * 16 : quarter * 16 + 16, lanes] = value
            return 0

        lax.fori_loop(0, colors * blocks // 16, dinv_body, 0)
        load_urem.wait()

        def urem_body(step, _):
            for quarter in range(4):
                for couple in range(3):
                    lines = lines_of(raw_urem.at[couple], step * 16, quarter)
                    for pair in range(8):
                        interleave(quarter * 24 + couple * 8 + pair, lines[2 * pair], lines[2 * pair + 1])
                    for pair in range(8):
                        group = step * GROUP + pair // 2
                        lanes = slice((pair % 2) * 128, (pair % 2) * 128 + 128)
                        value = mixed[quarter * 24 + couple * 8 + pair].astype(BF16)
                        row = couple * BS + quarter * 16
                        w_urem[group, row : row + 16, lanes] = value
                        if couple == 2:
                            w_urem[group, row + BS : row + BS + 16, lanes] = value
            return 0

        lax.fori_loop(0, blocks // 16, urem_body, 0)

        lane = lax.broadcasted_iota(jnp.int32, (8, 128), 1)
        for vector in range(edge_code.shape[1] // 128):
            code = jnp.zeros((8, 128), jnp.int32)
            for within in range(16):
                edge = vector * 16 + within
                code = jnp.where(lane // 8 == within, slot_idx[edge % 3, edge // 3] * 8 + lane % 8, code)
            edge_code[:, vector * 128 : vector * 128 + 128] = code
        for vector in range(owner_code.shape[1] // 128):
            code = jnp.zeros((8, 128), jnp.int32)
            for within in range(16):
                slot = vector * 16 + within
                code = jnp.where(
                    lane // 8 == within, send_idx[slot % per_peer, slot // per_peer] * 8 + lane % 8, code
                )
            owner_code[:, vector * 128 : vector * 128 + 128] = code

        def hot(target, codes):
            def body(chunk, _):
                rows = lax.broadcasted_iota(jnp.int32, (64, target.shape[1]), 0) + chunk * 64
                target[pl.ds(pl.multiple_of(chunk * 64, 64), 64), :] = jnp.where(
                    rows == codes[0:1, :], 1.0, 0.0
                ).astype(BF16)
                return 0

            lax.fori_loop(0, target.shape[0] // 64, body, 0)

        hot(edge_hot, edge_code)
        hot(owner_hot, owner_code)

    def product_of(indices, source, piece, group):
        members = []
        for member in range(GROUP):
            first, second, third = [source[at] for at in indices(group * GROUP + member)]
            members.append(jnp.concatenate([jnp.where(low_half16, first, second), third], axis=1))
        return dot_rows(jnp.concatenate(members, axis=0), weights[piece * groups + group])

    def own_block(product, member):
        lanes = slice((member // 2) * 128, (member // 2) * 128 + 128)
        piece = product[member * 16 : member * 16 + 16, lanes]
        turned = pltpu.roll(piece, BS, 1)
        if member % 2 == 0:
            return jnp.where(low_half16, piece, turned)
        return jnp.where(low_half16, turned, piece)

    def spread(source, group):
        members = []
        for member in range(GROUP):
            value = source[group * GROUP + member]
            if member % 2 == 0:
                kept = jnp.where(low_half16, value, zero16)
            else:
                kept = jnp.where(low_half16, zero16, value)
            pair = [kept, zero16] if member < 2 else [zero16, kept]
            members.append(jnp.concatenate(pair, axis=1))
        return jnp.concatenate(members, axis=0)

    def forward_step(piece, indices, source, color):
        def body(group, _):
            product = product_of(indices, source, piece, group)
            for member in range(GROUP):
                block = group * GROUP + member
                solved[color, block] = (rhs[color, block] - own_block(product, member)).astype(BF16)
            return 0

        lax.fori_loop(0, groups, body, 0, unroll=groups)

    def remote_indices(block):
        return [slot_idx[couple, block] for couple in range(3)]

    prepare_rhs()
    ahead = jnp.where(level == 0, 0, jnp.where(level == 1, steps + 1, pieces))
    lax.fori_loop(0, ahead, prepare_piece, 0)

    @pl.when(level >= 2)
    def _():
        prepare_back()

    @pl.when(level == 0)
    def _():
        def body(block, _):
            solved[0, block] = rhs[0, block].astype(BF16)
            return 0

        lax.fori_loop(0, blocks, body, 0, unroll=8)

    @pl.when(level > 0)
    def _():
        pltpu.make_async_copy(recv_f, recv_f, sems.at[1]).wait()

        def body(pair, _):
            both = recv_f[pl.ds(pl.multiple_of(pair * 16, 16), 16), :].astype(F32)
            rtable[pair * 2] = doubled(both[:8]).astype(BF16)
            rtable[pair * 2 + 1] = doubled(both[8:]).astype(BF16)
            return 0

        lax.fori_loop(0, recv_f.shape[0] // 16, body, 0, unroll=8)
        forward_step(remote_piece, remote_indices, rtable, 0)

    def color_body(color, _):
        @pl.when(level == 0)
        def _():
            prepare_piece(color - 1, 0)

        def indices(block):
            return [low_idx[color - 1, couple, block] for couple in range(3)]

        forward_step(color - 1, indices, solved.at[color - 1], color)
        return 0

    lax.fori_loop(1, colors, color_body, 0)

    pl.semaphore_wait(
        barrier, parts * ((level > 0).astype(jnp.int32) + (level < levels - 1).astype(jnp.int32))
    )

    @pl.when(level < levels - 1)
    def _():
        def pack(block, _):
            boundary[block] = paired(solved[colors - 1, block].astype(F32))
            return 0

        lax.fori_loop(0, blocks, pack, 0, unroll=8)

        def push(step, _):
            peer = lax.rem(me + step, parts)
            for pair in range(per_peer // 2):
                both = jnp.concatenate(
                    [boundary[send_idx[pair * 2, peer]], boundary[send_idx[pair * 2 + 1, peer]]], axis=0
                )
                send_f[pl.ds(pl.multiple_of(peer * rows_per_peer + pair * 16, 16), 16), :] = both.astype(BF16)
            pltpu.make_async_remote_copy(
                src_ref=send_f.at[pl.ds(pl.multiple_of(peer * rows_per_peer, 16), rows_per_peer)],
                dst_ref=recv_f.at[pl.ds(pl.multiple_of(me * rows_per_peer, 16), rows_per_peer)],
                send_sem=sems.at[0],
                recv_sem=sems.at[1],
                device_id=(level + 1, peer),
                device_id_type=MESH,
            ).start()
            return 0

        lax.fori_loop(0, parts, push, 0)

    behind = jnp.where(level == 0, steps, jnp.where(level == 1, steps + 1, pieces))
    lax.fori_loop(behind, pieces, prepare_piece, 0)

    @pl.when(level < 2)
    def _():
        prepare_back()

    def finish(color):
        def body(group, _):
            inverses = w_dinv[color * groups + group]
            product = dot_rows(spread(reduced, group), jnp.concatenate([inverses, inverses], axis=0))
            results = []
            for member in range(GROUP):
                value = product[member * 16 : member * 16 + 16]
                table[color, group * GROUP + member] = value.astype(BF16)
                results.append(paired(value))
            at = pl.ds(pl.multiple_of(group * GROUP * 8, GROUP * 8), GROUP * 8)
            out[color, at, :] = jnp.concatenate(results, axis=0).astype(BF16)
            return 0

        lax.fori_loop(0, groups, body, 0, unroll=groups)

    @pl.when(level == levels - 1)
    def _():
        upward[...] = jnp.zeros_like(upward)

    @pl.when(level < levels - 1)
    def _():
        pltpu.make_async_copy(recv_b, recv_b, sems.at[3]).wait()
        upward[...] = jnp.dot(owner_hot[...], recv_b[...], preferred_element_type=F32)

    def last_color(block, _):
        add = doubled(upward[pl.ds(pl.multiple_of(block * 8, 8), 8), :])
        reduced[block] = (solved[colors - 1, block].astype(F32) - add).astype(BF16)
        return 0

    lax.fori_loop(0, blocks, last_color, 0, unroll=16)

    def back_color(step, _):
        color = colors - 2 - step
        finish(color + 1)
        source = table.at[color + 1]

        def indices(block):
            return [up_idx[color, couple, block] for couple in range(3)]

        def body(group, _):
            product = product_of(indices, source, steps + 1 + color, group)
            for member in range(GROUP):
                block = group * GROUP + member
                value = solved[color, block].astype(F32) - own_block(product, member)
                reduced[block] = value.astype(BF16)
            return 0

        lax.fori_loop(0, groups, body, 0, unroll=groups)
        return 0

    lax.fori_loop(0, steps, back_color, 0)
    finish(0)

    @pl.when(level > 0)
    def _():
        def body(group, _):
            product = dot_rows(spread(table.at[0], group), w_urem[group])
            results = []
            for member in range(GROUP):
                rows = product[member * 16 : member * 16 + 16]
                both, third = rows[:, :128], rows[:, 128:]
                turned = pltpu.roll(both, BS, 1)
                results.append(jnp.where(low_half8, both[:8], turned[8:]))
                results.append(jnp.where(low_half8, turned[:8], both[8:]))
                results.append(paired(third))
            at = pl.ds(pl.multiple_of(group * GROUP * 24, 96), GROUP * 24)
            terms[at, :] = jnp.concatenate(results, axis=0).astype(BF16)
            return 0

        lax.fori_loop(0, groups, body, 0, unroll=groups)
        send_b[...] = jnp.dot(edge_hot[...], terms[...], preferred_element_type=F32).astype(BF16)

        def push(step, _):
            peer = lax.rem(me + step, parts)
            pltpu.make_async_remote_copy(
                src_ref=send_b.at[pl.ds(pl.multiple_of(peer * rows_per_peer, 16), rows_per_peer)],
                dst_ref=recv_b.at[pl.ds(pl.multiple_of(me * rows_per_peer, 16), rows_per_peer)],
                send_sem=sems.at[2],
                recv_sem=sems.at[3],
                device_id=(level - 1, peer),
                device_id_type=MESH,
            ).start()
            return 0

        lax.fori_loop(0, parts, push, 0)
        pltpu.make_async_copy(send_b, send_b, sems.at[2]).wait()

    @pl.when(level < levels - 1)
    def _():
        pltpu.make_async_copy(send_f, send_f, sems.at[0]).wait()


def per_device(
    levels,
    parts,
    rhs,
    dinv,
    lower_local,
    lower_nbrs,
    upper_local,
    upper_nbrs,
    lower_remote,
    upper_remote,
    remote_slots,
    send_list,
):
    colors, blocks, features = rhs.shape[2:]
    entries = dinv.shape[-1]
    steps, pieces = colors - 1, 2 * colors - 1
    groups = blocks // GROUP
    slots = parts * send_list.shape[-1]

    smem = pl.BlockSpec(memory_space=pltpu.SMEM)
    vmem = pl.BlockSpec(memory_space=pltpu.VMEM)
    hbm = pl.BlockSpec(memory_space=pl.ANY)
    answer = pl.pallas_call(
        functools.partial(kernel, levels, parts),
        out_shape=jax.ShapeDtypeStruct((colors, blocks * 8, 128), BF16),
        in_specs=[smem] * 4 + [hbm] * 6,
        out_specs=vmem,
        scratch_shapes=[
            pltpu.VMEM((colors, blocks, features), F32),
            pltpu.VMEM((pieces, 3, blocks, entries), BF16),
            pltpu.VMEM((3, blocks, entries), BF16),
            pltpu.VMEM((colors, blocks, entries), BF16),
            pltpu.VMEM((pieces * groups, GROUP * BS, 256), BF16),
            pltpu.VMEM((groups, 256, GROUP * BS), BF16),
            pltpu.VMEM((colors * groups, BS, GROUP * BS), BF16),
            pltpu.VMEM((colors, blocks, 16, 128), F32),
            pltpu.VMEM((128, 16, 128), F32),
            pltpu.VMEM((colors, blocks, 16, 128), BF16),
            pltpu.VMEM((blocks, 16, 128), BF16),
            pltpu.VMEM((colors, blocks, 16, 128), BF16),
            pltpu.VMEM((slots, 16, 128), BF16),
            pltpu.VMEM((blocks, 8, 128), F32),
            pltpu.VMEM((blocks * 8, 128), F32),
            pltpu.VMEM((blocks * 24, 128), BF16),
            pltpu.VMEM((8, blocks * 24), jnp.int32),
            pltpu.VMEM((8, slots * 8), jnp.int32),
            pltpu.VMEM((slots * 8, blocks * 24), BF16),
            pltpu.VMEM((blocks * 8, slots * 8), BF16),
            pltpu.VMEM((slots * 8, 128), BF16),
            pltpu.VMEM((slots * 8, 128), BF16),
            pltpu.VMEM((slots * 8, 128), BF16),
            pltpu.VMEM((slots * 8, 128), BF16),
            pltpu.SemaphoreType.DMA((4,)),
            pltpu.SemaphoreType.DMA((pieces + 3,)),
        ],
        compiler_params=pltpu.CompilerParams(
            collective_id=0, has_side_effects=True, vmem_limit_bytes=60 * 1024 * 1024
        ),
        name="sweeps",
    )(
        jnp.swapaxes(lower_nbrs[0, 0], 1, 2),
        jnp.swapaxes(upper_nbrs[0, 0], 1, 2),
        jnp.swapaxes(remote_slots[0, 0], 0, 1),
        jnp.swapaxes(send_list[0, 0], 0, 1),
        rhs,
        jnp.swapaxes(lower_local, 3, 4),
        jnp.swapaxes(upper_local, 3, 4),
        jnp.swapaxes(lower_remote, 2, 3),
        jnp.swapaxes(upper_remote, 2, 3),
        dinv,
    )
    return answer.reshape(1, 1, colors, blocks, features)


def solution(mesh):
    levels, parts = mesh.shape["level"], mesh.shape["dom"]
    return jax.shard_map(
        functools.partial(per_device, levels, parts),
        mesh=mesh,
        in_specs=(
            P("level", "dom", None, None, None),
            P("level", "dom", None, None, None),
            P("level", "dom", None, None, None, None),
            P("level", "dom", None, None, None),
            P("level", "dom", None, None, None, None),
            P("level", "dom", None, None, None),
            P("level", "dom", None, None, None),
            P("level", "dom", None, None, None),
            P("level", "dom", None, None),
            P("level", "dom", None, None),
        ),
        out_specs=P("level", "dom", None, None, None),
        check_vma=False,
    )
```

```python
import functools

import jax
import jax.numpy as jnp
from jax import lax
from jax.experimental import pallas as pl
from jax.experimental.pallas import tpu as pltpu
from jax.sharding import PartitionSpec as P

BS = 64
GROUP = 4
MESH = pl.DeviceIdType.MESH
BF16 = jnp.bfloat16
F32 = jnp.float32


def dot_rows(left, right):
    return lax.dot_general(left, right, (((1,), (1,)), ((), ())), preferred_element_type=F32)


def kernel(
    levels,
    parts,
    low_idx,
    up_idx,
    slot_idx,
    send_idx,
    rhs_hbm,
    low_hbm,
    up_hbm,
    lrem_hbm,
    urem_hbm,
    dinv_hbm,
    out,
    raw_rhs,
    raw,
    raw_urem,
    raw_dinv,
    weights,
    w_urem,
    w_dinv,
    rhs,
    mixed,
    solved,
    reduced,
    table,
    rtable,
    boundary,
    upward,
    terms,
    edge_code,
    owner_code,
    edge_hot,
    owner_hot,
    send_f,
    recv_f,
    send_b,
    recv_b,
    sems,
    load_sems,
):
    level = lax.axis_index("level")
    me = lax.axis_index("dom")
    colors, blocks = solved.shape[0], solved.shape[1]
    steps = colors - 1
    groups = blocks // GROUP
    per_peer = send_idx.shape[0]
    rows_per_peer = send_f.shape[0] // parts
    remote_piece = steps
    pieces = 2 * steps + 1

    def piece_source(piece):
        if piece < steps:
            return low_hbm.at[0, 0, piece]
        if piece == steps:
            return lrem_hbm.at[0, 0]
        return up_hbm.at[0, 0, piece - steps - 1]

    load_rhs = pltpu.make_async_copy(rhs_hbm.at[0, 0], raw_rhs, load_sems.at[pieces])
    load_urem = pltpu.make_async_copy(urem_hbm.at[0, 0], raw_urem, load_sems.at[pieces + 1])
    load_dinv = pltpu.make_async_copy(dinv_hbm.at[0, 0], raw_dinv, load_sems.at[pieces + 2])
    load_rhs.start()
    for piece in range(pieces):
        pltpu.make_async_copy(piece_source(piece), raw.at[piece], load_sems.at[piece]).start()
    load_dinv.start()
    load_urem.start()

    barrier = pltpu.get_barrier_semaphore()

    def greet(step, _):
        peer = lax.rem(me + step, parts)

        @pl.when(level > 0)
        def _():
            pl.semaphore_signal(barrier, inc=1, device_id=(level - 1, peer), device_id_type=MESH)

        @pl.when(level < levels - 1)
        def _():
            pl.semaphore_signal(barrier, inc=1, device_id=(level + 1, peer), device_id_type=MESH)

        return 0

    lax.fori_loop(0, parts, greet, 0)

    low_half16 = lax.broadcasted_iota(jnp.int32, (16, 128), 1) < BS
    low_half8 = lax.broadcasted_iota(jnp.int32, (8, 128), 1) < BS
    zero8 = jnp.zeros((8, 128), F32)
    zero16 = jnp.zeros((16, 128), BF16)

    def doubled(packed):
        turned = pltpu.roll(packed, BS, 1)
        return jnp.concatenate(
            [jnp.where(low_half8, packed, turned), jnp.where(low_half8, turned, packed)], axis=0
        )

    def paired(rows):
        return jnp.where(low_half8, rows[:8], rows[8:])

    def interleave(slot, first, second):
        first_turned = pltpu.roll(first, BS, 1)
        second_turned = pltpu.roll(second, BS, 1)
        mixed[slot, pl.ds(0, 8, stride=2), :] = jnp.where(low_half8, first, second_turned)
        mixed[slot, pl.ds(1, 8, stride=2), :] = jnp.where(low_half8, first_turned, second)

    def lines_of(source, first, quarter):
        lanes = slice(quarter * 1024, quarter * 1024 + 1024)
        part = source[pl.ds(pl.multiple_of(first, 16), 16), lanes]
        return part.astype(F32).reshape(16, 8, 128)

    def prepare_piece(piece, _):
        pltpu.make_async_copy(lrem_hbm.at[0, 0], raw.at[piece], load_sems.at[piece]).wait()

        def body(step, _):
            for quarter in range(4):
                lines = [lines_of(raw.at[piece, couple], step * 16, quarter) for couple in range(3)]
                for slot in range(16):
                    interleave(quarter * 32 + slot, lines[0][slot], lines[1][slot])
                    third = lines[2][slot]
                    turned = pltpu.roll(third, BS, 1)
                    at = quarter * 32 + 16 + slot
                    mixed[at, pl.ds(0, 8, stride=2), :] = jnp.where(low_half8, third, zero8)
                    mixed[at, pl.ds(1, 8, stride=2), :] = jnp.where(low_half8, turned, zero8)
                for slot in range(16):
                    group = piece * groups + step * GROUP + slot // GROUP
                    row = (slot % GROUP) * BS + quarter * 16
                    weights[group, row : row + 16, 0:128] = mixed[quarter * 32 + slot].astype(BF16)
                    weights[group, row : row + 16, 128:256] = mixed[quarter * 32 + 16 + slot].astype(BF16)
            return 0

        lax.fori_loop(0, blocks // 16, body, 0)
        return 0

    def prepare_rhs():
        load_rhs.wait()

        def body(step, _):
            color, first = step // (blocks // 8), lax.rem(step, blocks // 8) * 8
            lines = raw_rhs[color, pl.ds(pl.multiple_of(first, 8), 8), :].reshape(8, 8, 128)
            for slot in range(8):
                rhs[color, first + slot] = doubled(lines[slot])
            return 0

        lax.fori_loop(0, colors * blocks // 8, body, 0)

    def prepare_back():
        load_dinv.wait()

        def dinv_body(step, _):
            color, first = step // (blocks // 16), lax.rem(step, blocks // 16) * 16
            for quarter in range(4):
                lines = lines_of(raw_dinv.at[color], first, quarter)
                for pair in range(8):
                    interleave(quarter * 8 + pair, lines[2 * pair], lines[2 * pair + 1])
                for pair in range(8):
                    group = color * groups + first // GROUP + pair // 2
                    lanes = slice((pair % 2) * 128, (pair % 2) * 128 + 128)
                    value = mixed[quarter * 8 + pair].astype(BF16)
                    w_dinv[group, quarter * 16 : quarter * 16 + 16, lanes] = value
            return 0

        lax.fori_loop(0, colors * blocks // 16, dinv_body, 0)
        load_urem.wait()

        def urem_body(step, _):
            for quarter in range(4):
                for couple in range(3):
                    lines = lines_of(raw_urem.at[couple], step * 16, quarter)
                    for pair in range(8):
                        interleave(quarter * 24 + couple * 8 + pair, lines[2 * pair], lines[2 * pair + 1])
                    for pair in range(8):
                        group = step * GROUP + pair // 2
                        lanes = slice((pair % 2) * 128, (pair % 2) * 128 + 128)
                        value = mixed[quarter * 24 + couple * 8 + pair].astype(BF16)
                        row = couple * BS + quarter * 16
                        w_urem[group, row : row + 16, lanes] = value
                        if couple == 2:
                            w_urem[group, row + BS : row + BS + 16, lanes] = value
            return 0

        lax.fori_loop(0, blocks // 16, urem_body, 0)

        lane = lax.broadcasted_iota(jnp.int32, (8, 128), 1)
        for vector in range(edge_code.shape[1] // 128):
            code = jnp.zeros((8, 128), jnp.int32)
            for within in range(16):
                edge = vector * 16 + within
                code = jnp.where(lane // 8 == within, slot_idx[edge % 3, edge // 3] * 8 + lane % 8, code)
            edge_code[:, vector * 128 : vector * 128 + 128] = code
        for vector in range(owner_code.shape[1] // 128):
            code = jnp.zeros((8, 128), jnp.int32)
            for within in range(16):
                slot = vector * 16 + within
                code = jnp.where(
                    lane // 8 == within, send_idx[slot % per_peer, slot // per_peer] * 8 + lane % 8, code
                )
            owner_code[:, vector * 128 : vector * 128 + 128] = code

        def hot(target, codes):
            def body(chunk, _):
                rows = lax.broadcasted_iota(jnp.int32, (64, target.shape[1]), 0) + chunk * 64
                target[pl.ds(pl.multiple_of(chunk * 64, 64), 64), :] = jnp.where(
                    rows == codes[0:1, :], 1.0, 0.0
                ).astype(BF16)
                return 0

            lax.fori_loop(0, target.shape[0] // 64, body, 0)

        hot(edge_hot, edge_code)
        hot(owner_hot, owner_code)

    def product_of(indices, source, piece, group):
        members = []
        for member in range(GROUP):
            first, second, third = [source[at] for at in indices(group * GROUP + member)]
            members.append(jnp.concatenate([jnp.where(low_half16, first, second), third], axis=1))
        return dot_rows(jnp.concatenate(members, axis=0), weights[piece * groups + group])

    def own_block(product, member):
        lanes = slice((member // 2) * 128, (member // 2) * 128 + 128)
        piece = product[member * 16 : member * 16 + 16, lanes]
        turned = pltpu.roll(piece, BS, 1)
        if member % 2 == 0:
            return jnp.where(low_half16, piece, turned)
        return jnp.where(low_half16, turned, piece)

    def spread(source, group):
        members = []
        for member in range(GROUP):
            value = source[group * GROUP + member]
            if member % 2 == 0:
                kept = jnp.where(low_half16, value, zero16)
            else:
                kept = jnp.where(low_half16, zero16, value)
            pair = [kept, zero16] if member < 2 else [zero16, kept]
            members.append(jnp.concatenate(pair, axis=1))
        return jnp.concatenate(members, axis=0)

    def forward_step(piece, indices, source, color):
        def body(group, _):
            product = product_of(indices, source, piece, group)
            for member in range(GROUP):
                block = group * GROUP + member
                reduced[block] = (rhs[color, block] - own_block(product, member)).astype(BF16)
            return 0

        lax.fori_loop(0, groups, body, 0, unroll=groups)
        solved[color] = reduced[...]

    def remote_indices(block):
        return [slot_idx[couple, block] for couple in range(3)]

    prepare_rhs()
    ahead = jnp.where(level == 0, 0, jnp.where(level == 1, steps + 1, pieces))
    lax.fori_loop(0, ahead, prepare_piece, 0)

    @pl.when(level >= 2)
    def _():
        prepare_back()

    @pl.when(level == 0)
    def _():
        def body(block, _):
            solved[0, block] = rhs[0, block].astype(BF16)
            return 0

        lax.fori_loop(0, blocks, body, 0, unroll=8)

    @pl.when(level > 0)
    def _():
        pltpu.make_async_copy(recv_f, recv_f, sems.at[1]).wait()

        def body(pair, _):
            both = recv_f[pl.ds(pl.multiple_of(pair * 16, 16), 16), :].astype(F32)
            rtable[pair * 2] = doubled(both[:8]).astype(BF16)
            rtable[pair * 2 + 1] = doubled(both[8:]).astype(BF16)
            return 0

        lax.fori_loop(0, recv_f.shape[0] // 16, body, 0, unroll=8)
        forward_step(remote_piece, remote_indices, rtable, 0)

    def color_body(color, _):
        @pl.when(level == 0)
        def _():
            prepare_piece(color - 1, 0)

        def indices(block):
            return [low_idx[color - 1, couple, block] for couple in range(3)]

        forward_step(color - 1, indices, solved.at[color - 1], color)
        return 0

    lax.fori_loop(1, colors, color_body, 0)

    pl.semaphore_wait(
        barrier, parts * ((level > 0).astype(jnp.int32) + (level < levels - 1).astype(jnp.int32))
    )

    @pl.when(level < levels - 1)
    def _():
        def pack(block, _):
            boundary[block] = paired(solved[colors - 1, block].astype(F32))
            return 0

        lax.fori_loop(0, blocks, pack, 0, unroll=8)

        def push(step, _):
            peer = lax.rem(me + step, parts)
            for pair in range(per_peer // 2):
                both = jnp.concatenate(
                    [boundary[send_idx[pair * 2, peer]], boundary[send_idx[pair * 2 + 1, peer]]], axis=0
                )
                send_f[pl.ds(pl.multiple_of(peer * rows_per_peer + pair * 16, 16), 16), :] = both.astype(BF16)
            pltpu.make_async_remote_copy(
                src_ref=send_f.at[pl.ds(pl.multiple_of(peer * rows_per_peer, 16), rows_per_peer)],
                dst_ref=recv_f.at[pl.ds(pl.multiple_of(me * rows_per_peer, 16), rows_per_peer)],
                send_sem=sems.at[0],
                recv_sem=sems.at[1],
                device_id=(level + 1, peer),
                device_id_type=MESH,
            ).start()
            return 0

        lax.fori_loop(0, parts, push, 0)

    behind = jnp.where(level == 0, steps, jnp.where(level == 1, steps + 1, pieces))
    lax.fori_loop(behind, pieces, prepare_piece, 0)

    @pl.when(level < 2)
    def _():
        prepare_back()

    def finish(color):
        def body(group, _):
            inverses = w_dinv[color * groups + group]
            product = dot_rows(spread(reduced, group), jnp.concatenate([inverses, inverses], axis=0))
            results = []
            for member in range(GROUP):
                value = product[member * 16 : member * 16 + 16]
                table[color, group * GROUP + member] = value.astype(BF16)
                results.append(paired(value))
            at = pl.ds(pl.multiple_of(group * GROUP * 8, GROUP * 8), GROUP * 8)
            out[color, at, :] = jnp.concatenate(results, axis=0).astype(BF16)
            return 0

        lax.fori_loop(0, groups, body, 0, unroll=groups)

    @pl.when(level == levels - 1)
    def _():
        upward[...] = jnp.zeros_like(upward)

    @pl.when(level < levels - 1)
    def _():
        pltpu.make_async_copy(recv_b, recv_b, sems.at[3]).wait()
        upward[...] = jnp.dot(owner_hot[...], recv_b[...], preferred_element_type=F32)

    def last_color(block, _):
        add = doubled(upward[pl.ds(pl.multiple_of(block * 8, 8), 8), :])
        reduced[block] = (solved[colors - 1, block].astype(F32) - add).astype(BF16)
        return 0

    lax.fori_loop(0, blocks, last_color, 0, unroll=16)

    def back_color(step, _):
        color = colors - 2 - step
        finish(color + 1)
        source = table.at[color + 1]

        def indices(block):
            return [up_idx[color, couple, block] for couple in range(3)]

        def body(group, _):
            product = product_of(indices, source, steps + 1 + color, group)
            for member in range(GROUP):
                block = group * GROUP + member
                value = solved[color, block].astype(F32) - own_block(product, member)
                reduced[block] = value.astype(BF16)
            return 0

        lax.fori_loop(0, groups, body, 0, unroll=groups)
        return 0

    lax.fori_loop(0, steps, back_color, 0)
    finish(0)

    @pl.when(level > 0)
    def _():
        def body(group, _):
            product = dot_rows(spread(table.at[0], group), w_urem[group])
            results = []
            for member in range(GROUP):
                rows = product[member * 16 : member * 16 + 16]
                both, third = rows[:, :128], rows[:, 128:]
                turned = pltpu.roll(both, BS, 1)
                results.append(jnp.where(low_half8, both[:8], turned[8:]))
                results.append(jnp.where(low_half8, turned[:8], both[8:]))
                results.append(paired(third))
            at = pl.ds(pl.multiple_of(group * GROUP * 24, 96), GROUP * 24)
            terms[at, :] = jnp.concatenate(results, axis=0).astype(BF16)
            return 0

        lax.fori_loop(0, groups, body, 0, unroll=groups)
        send_b[...] = jnp.dot(edge_hot[...], terms[...], preferred_element_type=F32).astype(BF16)

        def push(step, _):
            peer = lax.rem(me + step, parts)
            pltpu.make_async_remote_copy(
                src_ref=send_b.at[pl.ds(pl.multiple_of(peer * rows_per_peer, 16), rows_per_peer)],
                dst_ref=recv_b.at[pl.ds(pl.multiple_of(me * rows_per_peer, 16), rows_per_peer)],
                send_sem=sems.at[2],
                recv_sem=sems.at[3],
                device_id=(level - 1, peer),
                device_id_type=MESH,
            ).start()
            return 0

        lax.fori_loop(0, parts, push, 0)
        pltpu.make_async_copy(send_b, send_b, sems.at[2]).wait()

    @pl.when(level < levels - 1)
    def _():
        pltpu.make_async_copy(send_f, send_f, sems.at[0]).wait()


def per_device(
    levels,
    parts,
    rhs,
    dinv,
    lower_local,
    lower_nbrs,
    upper_local,
    upper_nbrs,
    lower_remote,
    upper_remote,
    remote_slots,
    send_list,
):
    colors, blocks, features = rhs.shape[2:]
    entries = dinv.shape[-1]
    steps, pieces = colors - 1, 2 * colors - 1
    groups = blocks // GROUP
    slots = parts * send_list.shape[-1]

    smem = pl.BlockSpec(memory_space=pltpu.SMEM)
    vmem = pl.BlockSpec(memory_space=pltpu.VMEM)
    hbm = pl.BlockSpec(memory_space=pl.ANY)
    answer = pl.pallas_call(
        functools.partial(kernel, levels, parts),
        out_shape=jax.ShapeDtypeStruct((colors, blocks * 8, 128), BF16),
        in_specs=[smem] * 4 + [hbm] * 6,
        out_specs=vmem,
        scratch_shapes=[
            pltpu.VMEM((colors, blocks, features), F32),
            pltpu.VMEM((pieces, 3, blocks, entries), BF16),
            pltpu.VMEM((3, blocks, entries), BF16),
            pltpu.VMEM((colors, blocks, entries), BF16),
            pltpu.VMEM((pieces * groups, GROUP * BS, 256), BF16),
            pltpu.VMEM((groups, 256, GROUP * BS), BF16),
            pltpu.VMEM((colors * groups, BS, GROUP * BS), BF16),
            pltpu.VMEM((colors, blocks, 16, 128), F32),
            pltpu.VMEM((128, 16, 128), F32),
            pltpu.VMEM((colors, blocks, 16, 128), BF16),
            pltpu.VMEM((blocks, 16, 128), BF16),
            pltpu.VMEM((colors, blocks, 16, 128), BF16),
            pltpu.VMEM((slots, 16, 128), BF16),
            pltpu.VMEM((blocks, 8, 128), F32),
            pltpu.VMEM((blocks * 8, 128), F32),
            pltpu.VMEM((blocks * 24, 128), BF16),
            pltpu.VMEM((8, blocks * 24), jnp.int32),
            pltpu.VMEM((8, slots * 8), jnp.int32),
            pltpu.VMEM((slots * 8, blocks * 24), BF16),
            pltpu.VMEM((blocks * 8, slots * 8), BF16),
            pltpu.VMEM((slots * 8, 128), BF16),
            pltpu.VMEM((slots * 8, 128), BF16),
            pltpu.VMEM((slots * 8, 128), BF16),
            pltpu.VMEM((slots * 8, 128), BF16),
            pltpu.SemaphoreType.DMA((4,)),
            pltpu.SemaphoreType.DMA((pieces + 3,)),
        ],
        compiler_params=pltpu.CompilerParams(
            collective_id=0, has_side_effects=True, vmem_limit_bytes=60 * 1024 * 1024
        ),
        name="sweeps",
    )(
        jnp.swapaxes(lower_nbrs[0, 0], 1, 2),
        jnp.swapaxes(upper_nbrs[0, 0], 1, 2),
        jnp.swapaxes(remote_slots[0, 0], 0, 1),
        jnp.swapaxes(send_list[0, 0], 0, 1),
        rhs,
        jnp.swapaxes(lower_local, 3, 4),
        jnp.swapaxes(upper_local, 3, 4),
        jnp.swapaxes(lower_remote, 2, 3),
        jnp.swapaxes(upper_remote, 2, 3),
        dinv,
    )
    return answer.reshape(1, 1, colors, blocks, features)


def solution(mesh):
    levels, parts = mesh.shape["level"], mesh.shape["dom"]
    return jax.shard_map(
        functools.partial(per_device, levels, parts),
        mesh=mesh,
        in_specs=(
            P("level", "dom", None, None, None),
            P("level", "dom", None, None, None),
            P("level", "dom", None, None, None, None),
            P("level", "dom", None, None, None),
            P("level", "dom", None, None, None, None),
            P("level", "dom", None, None, None),
            P("level", "dom", None, None, None),
            P("level", "dom", None, None, None),
            P("level", "dom", None, None),
            P("level", "dom", None, None),
        ),
        out_specs=P("level", "dom", None, None, None),
        check_vma=False,
    )
```

```python
import functools

import jax
import jax.numpy as jnp
from jax import lax
from jax.experimental import pallas as pl
from jax.experimental.pallas import tpu as pltpu
from jax.sharding import PartitionSpec as P

BS = 64
GROUP = 4
MESH = pl.DeviceIdType.MESH
BF16 = jnp.bfloat16
F32 = jnp.float32


def dot_rows(left, right):
    return lax.dot_general(left, right, (((1,), (1,)), ((), ())), preferred_element_type=F32)


def far_first(parts):
    if parts != 32:
        return [(0, 0, step) for step in range(parts)], (1, 1, parts)
    hops = lambda step: min(step, 4 - step)
    steps = [(z, y, core) for z in range(4) for y in range(4) for core in range(2)]
    steps.sort(key=lambda at: -(hops(at[0]) + hops(at[1]) + 0.5 * at[2]))
    return steps, (4, 4, 2)


def kernel(
    levels,
    parts,
    low_idx,
    up_idx,
    slot_idx,
    send_idx,
    rhs_hbm,
    low_hbm,
    up_hbm,
    lrem_hbm,
    urem_hbm,
    dinv_hbm,
    out,
    raw_rhs,
    raw,
    raw_urem,
    raw_dinv,
    flat,
    mats,
    mat_urem,
    w_dinv,
    mat_dinv,
    identity,
    rhs,
    mixed,
    solved,
    reduced,
    base,
    table,
    rtable,
    boundary,
    upward,
    terms,
    edge_code,
    owner_code,
    edge_hot,
    owner_hot,
    send_f,
    recv_f,
    send_b,
    recv_b,
    sems,
    load_sems,
):
    level = lax.axis_index("level")
    me = lax.axis_index("dom")
    colors, blocks = solved.shape[0], solved.shape[1]
    steps = colors - 1
    groups = blocks // GROUP
    per_peer = send_idx.shape[0]
    rows_per_peer = send_f.shape[0] // parts
    offsets, sides = far_first(parts)
    at_z, at_y, at_core = me // (sides[1] * sides[2]), lax.rem(me // sides[2], sides[1]), lax.rem(me, sides[2])
    peers = [
        (lax.rem(at_z + z, sides[0]) * sides[1] + lax.rem(at_y + y, sides[1])) * sides[2]
        + lax.rem(at_core + core, sides[2])
        for z, y, core in offsets
    ]
    remote_piece = steps
    pieces = 2 * steps + 1

    def piece_source(piece):
        if piece < steps:
            return low_hbm.at[0, 0, piece]
        if piece == steps:
            return lrem_hbm.at[0, 0]
        return up_hbm.at[0, 0, piece - steps - 1]

    load_rhs = pltpu.make_async_copy(rhs_hbm.at[0, 0], raw_rhs, load_sems.at[pieces])
    load_urem = pltpu.make_async_copy(urem_hbm.at[0, 0], raw_urem, load_sems.at[pieces + 1])
    load_dinv = pltpu.make_async_copy(dinv_hbm.at[0, 0], raw_dinv, load_sems.at[pieces + 2])
    load_rhs.start()
    for piece in range(steps + 1):
        pltpu.make_async_copy(piece_source(piece), raw.at[piece], load_sems.at[piece]).start()
    load_dinv.start()
    load_urem.start()
    for piece in range(steps + 1, pieces):
        pltpu.make_async_copy(piece_source(piece), raw.at[piece], load_sems.at[piece]).start()

    barrier = pltpu.get_barrier_semaphore()

    def greet(step, _):
        peer = lax.rem(me + step, parts)

        @pl.when(level > 0)
        def _():
            pl.semaphore_signal(barrier, inc=1, device_id=(level - 1, peer), device_id_type=MESH)

        @pl.when(level < levels - 1)
        def _():
            pl.semaphore_signal(barrier, inc=1, device_id=(level + 1, peer), device_id_type=MESH)

        return 0

    lax.fori_loop(0, parts, greet, 0)

    low_half16 = lax.broadcasted_iota(jnp.int32, (16, 128), 1) < BS
    low_half8 = lax.broadcasted_iota(jnp.int32, (8, 128), 1) < BS
    zero8 = jnp.zeros((8, 128), F32)
    zero16 = jnp.zeros((16, 128), BF16)

    def doubled(packed):
        turned = pltpu.roll(packed, BS, 1)
        return jnp.concatenate(
            [jnp.where(low_half8, packed, turned), jnp.where(low_half8, turned, packed)], axis=0
        )

    def paired(rows):
        return jnp.where(low_half8, rows[:8], rows[8:])

    def interleave(slot, first, second):
        first_turned = pltpu.roll(first, BS, 1)
        second_turned = pltpu.roll(second, BS, 1)
        mixed[slot, pl.ds(0, 8, stride=2), :] = jnp.where(low_half8, first, second_turned)
        mixed[slot, pl.ds(1, 8, stride=2), :] = jnp.where(low_half8, first_turned, second)

    def lines_of(source, first, quarter):
        lanes = slice(quarter * 1024, quarter * 1024 + 1024)
        part = source[pl.ds(pl.multiple_of(first, 16), 16), lanes]
        return part.astype(F32).reshape(16, 8, 128)

    def await_piece(piece):
        pltpu.make_async_copy(lrem_hbm.at[0, 0], raw.at[piece], load_sems.at[piece]).wait()

    def flatten_piece(piece):
        await_piece(piece)

        def body(step, _):
            for quarter in range(4):
                lines = [lines_of(raw.at[piece, couple], step * 16, quarter) for couple in range(3)]
                for slot in range(16):
                    interleave(quarter * 32 + slot, lines[0][slot], lines[1][slot])
                    third = lines[2][slot]
                    turned = pltpu.roll(third, BS, 1)
                    at = quarter * 32 + 16 + slot
                    mixed[at, pl.ds(0, 8, stride=2), :] = jnp.where(low_half8, third, zero8)
                    mixed[at, pl.ds(1, 8, stride=2), :] = jnp.where(low_half8, turned, zero8)
                for slot in range(16):
                    group = step * GROUP + slot // GROUP
                    row = (slot % GROUP) * BS + quarter * 16
                    flat[group, row : row + 16, 0:128] = mixed[quarter * 32 + slot].astype(BF16)
                    flat[group, row : row + 16, 128:256] = mixed[quarter * 32 + 16 + slot].astype(BF16)
            return 0

        lax.fori_loop(0, blocks // 16, body, 0)

    def turned(rows):
        return dot_rows(identity[...], rows).astype(BF16)

    def prepare_lower(piece, _):
        flatten_piece(piece)

        def body(group, _):
            mats[piece * groups + group] = turned(flat[group])
            return 0

        lax.fori_loop(0, groups, body, 0, unroll=4)
        return 0

    member_lane = lax.broadcasted_iota(jnp.int32, (BS, GROUP * BS), 1) // BS

    def prepare_upper(color, _):
        piece = steps + 1 + color
        flatten_piece(piece)

        def body(group, _):
            inverses = w_dinv[color * groups + group]
            apart = [
                jnp.where(member_lane == member, inverses, jnp.zeros_like(inverses))
                for member in range(GROUP)
            ]
            product = dot_rows(turned(flat[group]), jnp.concatenate(apart, axis=0))
            mats[piece * groups + group] = product.astype(BF16)
            return 0

        lax.fori_loop(0, groups, body, 0, unroll=4)
        return 0

    def prepare_rhs():
        load_rhs.wait()

        def body(step, _):
            color, first = step // (blocks // 8), lax.rem(step, blocks // 8) * 8
            lines = raw_rhs[color, pl.ds(pl.multiple_of(first, 8), 8), :].reshape(8, 8, 128)
            for slot in range(8):
                rhs[color, first + slot] = doubled(lines[slot])
            return 0

        lax.fori_loop(0, colors * blocks // 8, body, 0, unroll=2)

    def prepare_sums():
        load_dinv.wait()

        def dinv_body(step, _):
            color, first = step // (blocks // 16), lax.rem(step, blocks // 16) * 16
            for quarter in range(4):
                lines = lines_of(raw_dinv.at[color], first, quarter)
                for pair in range(8):
                    interleave(quarter * 8 + pair, lines[2 * pair], lines[2 * pair + 1])
                for pair in range(8):
                    group = color * groups + first // GROUP + pair // 2
                    lanes = slice((pair % 2) * 128, (pair % 2) * 128 + 128)
                    value = mixed[quarter * 8 + pair].astype(BF16)
                    w_dinv[group, quarter * 16 : quarter * 16 + 16, lanes] = value
            return 0

        lax.fori_loop(0, colors * blocks // 16, dinv_body, 0)

        def dinv_turn(group, _):
            inverses = w_dinv[group]
            mat_dinv[group] = turned(jnp.concatenate([inverses, inverses], axis=0))
            return 0

        lax.fori_loop(0, colors * groups, dinv_turn, 0, unroll=4)
        load_urem.wait()

        def urem_body(step, _):
            for quarter in range(4):
                for couple in range(3):
                    lines = lines_of(raw_urem.at[couple], step * 16, quarter)
                    for pair in range(8):
                        interleave(quarter * 24 + couple * 8 + pair, lines[2 * pair], lines[2 * pair + 1])
                    for pair in range(8):
                        group = step * GROUP + pair // 2
                        lanes = slice((pair % 2) * 128, (pair % 2) * 128 + 128)
                        value = mixed[quarter * 24 + couple * 8 + pair].astype(BF16)
                        row = couple * BS + quarter * 16
                        flat[group, row : row + 16, lanes] = value
                        if couple == 2:
                            flat[group, row + BS : row + BS + 16, lanes] = value
            return 0

        lax.fori_loop(0, blocks // 16, urem_body, 0)

        def urem_turn(group, _):
            mat_urem[group] = turned(flat[group])
            return 0

        lax.fori_loop(0, groups, urem_turn, 0, unroll=4)

        lane = lax.broadcasted_iota(jnp.int32, (8, 128), 1)
        for vector in range(edge_code.shape[1] // 128):
            code = jnp.zeros((8, 128), jnp.int32)
            for within in range(16):
                edge = vector * 16 + within
                code = jnp.where(lane // 8 == within, slot_idx[0, edge % 3, 0, edge // 3] * 8 + lane % 8, code)
            edge_code[:, vector * 128 : vector * 128 + 128] = code
        for vector in range(owner_code.shape[1] // 128):
            code = jnp.zeros((8, 128), jnp.int32)
            for within in range(16):
                slot = vector * 16 + within
                code = jnp.where(
                    lane // 8 == within, send_idx[slot % per_peer, slot // per_peer] * 8 + lane % 8, code
                )
            owner_code[:, vector * 128 : vector * 128 + 128] = code

        def hot(target, codes):
            def body(chunk, _):
                rows = lax.broadcasted_iota(jnp.int32, (64, target.shape[1]), 0) + chunk * 64
                target[pl.ds(pl.multiple_of(chunk * 64, 64), 64), :] = jnp.where(
                    rows == codes[0:1, :], 1.0, 0.0
                ).astype(BF16)
                return 0

            lax.fori_loop(0, target.shape[0] // 64, body, 0)

        hot(edge_hot, edge_code)
        hot(owner_hot, owner_code)

    def gathered(indices, source, group):
        members = []
        for member in range(GROUP):
            first, second, third = [source[at] for at in indices(group * GROUP + member)]
            members.append(jnp.concatenate([jnp.where(low_half16, first, second), third], axis=1))
        return jnp.concatenate(members, axis=0)

    def own_block(product, member):
        lanes = slice((member // 2) * 128, (member // 2) * 128 + 128)
        piece = product[member * 16 : member * 16 + 16, lanes]
        turned = pltpu.roll(piece, BS, 1)
        if member % 2 == 0:
            return jnp.where(low_half16, piece, turned)
        return jnp.where(low_half16, turned, piece)

    def spread(source, group):
        members = []
        for member in range(GROUP):
            value = source[group * GROUP + member]
            if member % 2 == 0:
                kept = jnp.where(low_half16, value, zero16)
            else:
                kept = jnp.where(low_half16, zero16, value)
            pair = [kept, zero16] if member < 2 else [zero16, kept]
            members.append(jnp.concatenate(pair, axis=1))
        return jnp.concatenate(members, axis=0)

    def forward_step(multiply, indices, source, color):
        def body(group, _):
            product = multiply(gathered(indices, source, group), group)
            for member in range(GROUP):
                block = group * GROUP + member
                reduced[block] = (rhs[color, block] - own_block(product, member)).astype(BF16)
            return 0

        lax.fori_loop(0, groups, body, 0, unroll=groups)
        solved[color] = reduced[...]

    def by_piece(piece):
        return lambda rows, group: jnp.dot(
            rows, mats[piece * groups + group], preferred_element_type=F32
        )

    def remote_indices(block):
        return [slot_idx[0, couple, 0, block] for couple in range(3)]

    def lower_indices(color):
        return lambda block: [low_idx[0, color - 1, couple, 0, block] for couple in range(3)]

    prepare_rhs()

    @pl.when(level == 0)
    def _():
        def body(block, _):
            solved[0, block] = rhs[0, block].astype(BF16)
            return 0

        lax.fori_loop(0, blocks, body, 0, unroll=8)

        def color_body(color, _):
            flatten_piece(color - 1)
            forward_step(
                lambda rows, group: dot_rows(rows, flat[group]),
                lower_indices(color),
                solved.at[color - 1],
                color,
            )
            return 0

        lax.fori_loop(1, colors, color_body, 0)

    identity[...] = jnp.where(
        lax.broadcasted_iota(jnp.int32, (256, 256), 0) == lax.broadcasted_iota(jnp.int32, (256, 256), 1),
        1.0,
        0.0,
    ).astype(BF16)

    @pl.when(level > 0)
    def _():
        lax.fori_loop(0, steps + 1, prepare_lower, 0)

    @pl.when(level >= 2)
    def _():
        prepare_sums()

    lax.fori_loop(0, jnp.where(level == levels - 1, steps, 0), prepare_upper, 0)

    @pl.when(level > 0)
    def _():
        pltpu.make_async_copy(recv_f, recv_f, sems.at[1]).wait()

        def body(pair, _):
            both = recv_f[pl.ds(pl.multiple_of(pair * 16, 16), 16), :].astype(F32)
            rtable[pair * 2] = doubled(both[:8]).astype(BF16)
            rtable[pair * 2 + 1] = doubled(both[8:]).astype(BF16)
            return 0

        lax.fori_loop(0, recv_f.shape[0] // 16, body, 0, unroll=8)
        forward_step(by_piece(remote_piece), remote_indices, rtable, 0)

        def color_body(color, _):
            forward_step(by_piece(color - 1), lower_indices(color), solved.at[color - 1], color)
            return 0

        lax.fori_loop(1, colors, color_body, 0)

    pl.semaphore_wait(
        barrier, parts * ((level > 0).astype(jnp.int32) + (level < levels - 1).astype(jnp.int32))
    )

    @pl.when(level < levels - 1)
    def _():
        def pack(block, _):
            boundary[block] = paired(solved[colors - 1, block].astype(F32))
            return 0

        lax.fori_loop(0, blocks, pack, 0, unroll=8)

        for peer in peers:
            for pair in range(per_peer // 2):
                both = jnp.concatenate(
                    [boundary[send_idx[pair * 2, peer]], boundary[send_idx[pair * 2 + 1, peer]]], axis=0
                )
                send_f[pl.ds(pl.multiple_of(peer * rows_per_peer + pair * 16, 16), 16), :] = both.astype(BF16)
            pltpu.make_async_remote_copy(
                src_ref=send_f.at[pl.ds(pl.multiple_of(peer * rows_per_peer, 16), rows_per_peer)],
                dst_ref=recv_f.at[pl.ds(pl.multiple_of(me * rows_per_peer, 16), rows_per_peer)],
                send_sem=sems.at[0],
                recv_sem=sems.at[1],
                device_id=(level + 1, peer),
                device_id_type=MESH,
            ).start()

    @pl.when(level == 0)
    def _():
        await_piece(remote_piece)

    @pl.when(level < 2)
    def _():
        prepare_sums()

    lax.fori_loop(0, jnp.where(level == levels - 1, 0, steps), prepare_upper, 0)

    def scale(color, source, put):
        def body(group, _):
            product = jnp.dot(
                spread(source, group), mat_dinv[color * groups + group], preferred_element_type=F32
            )
            for member in range(GROUP):
                put(group * GROUP + member, product[member * 16 : member * 16 + 16])
            return 0

        lax.fori_loop(0, groups, body, 0, unroll=groups)

    def scale_solved(color, _):
        def put(block, value):
            base[color, block] = value

        scale(color, solved.at[color], put)
        return 0

    lax.fori_loop(0, steps, scale_solved, 0)

    def store_out(color):
        def body(group, _):
            values = [paired(table[color, group * GROUP + member].astype(F32)) for member in range(GROUP)]
            at = pl.ds(pl.multiple_of(group * GROUP * 8, GROUP * 8), GROUP * 8)
            out[color, at, :] = jnp.concatenate(values, axis=0).astype(BF16)
            return 0

        lax.fori_loop(0, groups, body, 0, unroll=4)

    @pl.when(level == levels - 1)
    def _():
        upward[...] = jnp.zeros_like(upward)

    @pl.when(level < levels - 1)
    def _():
        pltpu.make_async_copy(recv_b, recv_b, sems.at[3]).wait()
        upward[...] = jnp.dot(owner_hot[...], recv_b[...], preferred_element_type=F32)

    def last_color(block, _):
        add = doubled(upward[pl.ds(pl.multiple_of(block * 8, 8), 8), :])
        reduced[block] = (solved[colors - 1, block].astype(F32) - add).astype(BF16)
        return 0

    lax.fori_loop(0, blocks, last_color, 0, unroll=16)

    def put_last(block, value):
        table[colors - 1, block] = value.astype(BF16)

    scale(colors - 1, reduced, put_last)

    def back_color(step, _):
        color = colors - 2 - step
        source = table.at[color + 1]
        multiply = by_piece(steps + 1 + color)

        def indices(block):
            return [up_idx[0, color, couple, 0, block] for couple in range(3)]

        def body(group, _):
            product = multiply(gathered(indices, source, group), group)
            for member in range(GROUP):
                block = group * GROUP + member
                reduced[block] = (base[color, block] - own_block(product, member)).astype(BF16)
            return 0

        lax.fori_loop(0, groups, body, 0, unroll=groups)
        table[color] = reduced[...]
        return 0

    lax.fori_loop(0, steps, back_color, 0)

    @pl.when(level > 0)
    def _():
        def body(group, _):
            product = jnp.dot(
                spread(table.at[0], group), mat_urem[group], preferred_element_type=F32
            )
            results = []
            for member in range(GROUP):
                rows = product[member * 16 : member * 16 + 16]
                both, third = rows[:, :128], rows[:, 128:]
                turned = pltpu.roll(both, BS, 1)
                results.append(jnp.where(low_half8, both[:8], turned[8:]))
                results.append(jnp.where(low_half8, turned[:8], both[8:]))
                results.append(paired(third))
            at = pl.ds(pl.multiple_of(group * GROUP * 24, 96), GROUP * 24)
            terms[at, :] = jnp.concatenate(results, axis=0).astype(BF16)
            return 0

        lax.fori_loop(0, groups, body, 0, unroll=groups)
        send_b[...] = jnp.dot(edge_hot[...], terms[...], preferred_element_type=F32).astype(BF16)

        for peer in peers:
            pltpu.make_async_remote_copy(
                src_ref=send_b.at[pl.ds(pl.multiple_of(peer * rows_per_peer, 16), rows_per_peer)],
                dst_ref=recv_b.at[pl.ds(pl.multiple_of(me * rows_per_peer, 16), rows_per_peer)],
                send_sem=sems.at[2],
                recv_sem=sems.at[3],
                device_id=(level - 1, peer),
                device_id_type=MESH,
            ).start()

    def color_out(color, _):
        store_out(color)
        return 0

    lax.fori_loop(0, colors, color_out, 0)

    @pl.when(level > 0)
    def _():
        pltpu.make_async_copy(send_b, send_b, sems.at[2]).wait()

    @pl.when(level < levels - 1)
    def _():
        pltpu.make_async_copy(send_f, send_f, sems.at[0]).wait()


def per_device(
    levels,
    parts,
    rhs,
    dinv,
    lower_local,
    lower_nbrs,
    upper_local,
    upper_nbrs,
    lower_remote,
    upper_remote,
    remote_slots,
    send_list,
):
    colors, blocks, features = rhs.shape[2:]
    entries = dinv.shape[-1]
    steps, pieces = colors - 1, 2 * colors - 1
    groups = blocks // GROUP
    slots = parts * send_list.shape[-1]

    smem = pl.BlockSpec(memory_space=pltpu.SMEM)
    vmem = pl.BlockSpec(memory_space=pltpu.VMEM)
    hbm = pl.BlockSpec(memory_space=pl.ANY)
    answer = pl.pallas_call(
        functools.partial(kernel, levels, parts),
        out_shape=jax.ShapeDtypeStruct((colors, blocks * 8, 128), BF16),
        in_specs=[smem] * 4 + [hbm] * 6,
        out_specs=vmem,
        scratch_shapes=[
            pltpu.VMEM((colors, blocks, features), F32),
            pltpu.VMEM((pieces, 3, blocks, entries), BF16),
            pltpu.VMEM((3, blocks, entries), BF16),
            pltpu.VMEM((colors, blocks, entries), BF16),
            pltpu.VMEM((groups, GROUP * BS, 256), BF16),
            pltpu.VMEM((pieces * groups, 256, GROUP * BS), BF16),
            pltpu.VMEM((groups, GROUP * BS, 256), BF16),
            pltpu.VMEM((colors * groups, BS, GROUP * BS), BF16),
            pltpu.VMEM((colors * groups, GROUP * BS, 2 * BS), BF16),
            pltpu.VMEM((256, 256), BF16),
            pltpu.VMEM((colors, blocks, 16, 128), F32),
            pltpu.VMEM((128, 16, 128), F32),
            pltpu.VMEM((colors, blocks, 16, 128), BF16),
            pltpu.VMEM((blocks, 16, 128), BF16),
            pltpu.VMEM((steps, blocks, 16, 128), F32),
            pltpu.VMEM((colors, blocks, 16, 128), BF16),
            pltpu.VMEM((slots, 16, 128), BF16),
            pltpu.VMEM((blocks, 8, 128), F32),
            pltpu.VMEM((blocks * 8, 128), F32),
            pltpu.VMEM((blocks * 24, 128), BF16),
            pltpu.VMEM((8, blocks * 24), jnp.int32),
            pltpu.VMEM((8, slots * 8), jnp.int32),
            pltpu.VMEM((slots * 8, blocks * 24), BF16),
            pltpu.VMEM((blocks * 8, slots * 8), BF16),
            pltpu.VMEM((slots * 8, 128), BF16),
            pltpu.VMEM((slots * 8, 128), BF16),
            pltpu.VMEM((slots * 8, 128), BF16),
            pltpu.VMEM((slots * 8, 128), BF16),
            pltpu.SemaphoreType.DMA((4,)),
            pltpu.SemaphoreType.DMA((pieces + 3,)),
        ],
        compiler_params=pltpu.CompilerParams(
            collective_id=0, has_side_effects=True, vmem_limit_bytes=60 * 1024 * 1024
        ),
        name="sweeps",
    )(
        jnp.transpose(lower_nbrs, (0, 2, 4, 1, 3)),
        jnp.transpose(upper_nbrs, (0, 2, 4, 1, 3)),
        jnp.transpose(remote_slots, (0, 3, 1, 2)),
        jnp.swapaxes(send_list[0, 0], 0, 1),
        rhs,
        jnp.swapaxes(lower_local, 3, 4),
        jnp.swapaxes(upper_local, 3, 4),
        jnp.swapaxes(lower_remote, 2, 3),
        jnp.swapaxes(upper_remote, 2, 3),
        dinv,
    )
    return answer.reshape(1, 1, colors, blocks, features)


def solution(mesh):
    levels, parts = mesh.shape["level"], mesh.shape["dom"]
    return jax.shard_map(
        functools.partial(per_device, levels, parts),
        mesh=mesh,
        in_specs=(
            P("level", "dom", None, None, None),
            P("level", "dom", None, None, None),
            P("level", "dom", None, None, None, None),
            P("level", "dom", None, None, None),
            P("level", "dom", None, None, None, None),
            P("level", "dom", None, None, None),
            P("level", "dom", None, None, None),
            P("level", "dom", None, None, None),
            P("level", "dom", None, None),
            P("level", "dom", None, None),
        ),
        out_specs=P("level", "dom", None, None, None),
        check_vma=False,
    )
```

```python
import functools

import jax
import jax.numpy as jnp
from jax import lax
from jax.experimental import pallas as pl
from jax.experimental.pallas import tpu as pltpu
from jax.sharding import PartitionSpec as P

BS = 64
GROUP = 4
DEPTH = 3 * BS
MESH = pl.DeviceIdType.MESH
BF16 = jnp.bfloat16
F32 = jnp.float32


def dot_rows(left, right):
    return lax.dot_general(left, right, (((1,), (1,)), ((), ())), preferred_element_type=F32)


def far_first(parts):
    if parts != 32:
        return [(0, 0, step) for step in range(parts)], (1, 1, parts)
    hops = lambda step: min(step, 4 - step)
    steps = [(z, y, core) for z in range(4) for y in range(4) for core in range(2)]
    steps.sort(key=lambda at: -(hops(at[0]) + hops(at[1]) + 0.5 * at[2]))
    return steps, (4, 4, 2)


def kernel(
    levels,
    parts,
    low_idx,
    up_idx,
    slot_idx,
    send_idx,
    rhs_hbm,
    low_hbm,
    up_hbm,
    lrem_hbm,
    urem_hbm,
    dinv_hbm,
    out,
    raw_rhs,
    raw,
    raw_urem,
    raw_dinv,
    flat,
    mats,
    mat_urem,
    w_dinv,
    mat_dinv,
    identity,
    rhs,
    mixed,
    solved,
    reduced,
    base,
    table,
    rtable,
    boundary,
    upward,
    terms,
    edge_code,
    owner_code,
    edge_hot,
    owner_hot,
    send_f,
    recv_f,
    send_b,
    recv_b,
    sems,
    load_sems,
):
    level = lax.axis_index("level")
    me = lax.axis_index("dom")
    colors, blocks = solved.shape[0], solved.shape[1]
    steps = colors - 1
    groups = blocks // GROUP
    per_peer = send_idx.shape[0]
    rows_per_peer = send_f.shape[0] // parts
    offsets, sides = far_first(parts)
    at_z, at_y, at_core = me // (sides[1] * sides[2]), lax.rem(me // sides[2], sides[1]), lax.rem(me, sides[2])
    peers = [
        (lax.rem(at_z + z, sides[0]) * sides[1] + lax.rem(at_y + y, sides[1])) * sides[2]
        + lax.rem(at_core + core, sides[2])
        for z, y, core in offsets
    ]
    remote_piece = steps
    pieces = 2 * steps + 1

    def piece_source(piece):
        if piece < steps:
            return low_hbm.at[0, 0, piece]
        if piece == steps:
            return lrem_hbm.at[0, 0]
        return up_hbm.at[0, 0, piece - steps - 1]

    load_rhs = pltpu.make_async_copy(rhs_hbm.at[0, 0], raw_rhs, load_sems.at[pieces])
    load_urem = pltpu.make_async_copy(urem_hbm.at[0, 0], raw_urem, load_sems.at[pieces + 1])
    load_dinv = pltpu.make_async_copy(dinv_hbm.at[0, 0], raw_dinv, load_sems.at[pieces + 2])
    load_rhs.start()
    for piece in range(steps + 1):
        pltpu.make_async_copy(piece_source(piece), raw.at[piece], load_sems.at[piece]).start()
    load_dinv.start()
    load_urem.start()
    for piece in range(steps + 1, pieces):
        pltpu.make_async_copy(piece_source(piece), raw.at[piece], load_sems.at[piece]).start()

    barrier = pltpu.get_barrier_semaphore()

    def greet(step, _):
        peer = lax.rem(me + step, parts)

        @pl.when(level > 0)
        def _():
            pl.semaphore_signal(barrier, inc=1, device_id=(level - 1, peer), device_id_type=MESH)

        @pl.when(level < levels - 1)
        def _():
            pl.semaphore_signal(barrier, inc=1, device_id=(level + 1, peer), device_id_type=MESH)

        return 0

    lax.fori_loop(0, parts, greet, 0)

    low_half16 = lax.broadcasted_iota(jnp.int32, (16, 128), 1) < BS
    low_half8 = lax.broadcasted_iota(jnp.int32, (8, 128), 1) < BS
    zero16 = jnp.zeros((16, 128), BF16)

    def doubled(packed):
        turned = pltpu.roll(packed, BS, 1)
        return jnp.concatenate(
            [jnp.where(low_half8, packed, turned), jnp.where(low_half8, turned, packed)], axis=0
        )

    def paired(rows):
        return jnp.where(low_half8, rows[:8], rows[8:])

    def interleave(slot, first, second):
        first_turned = pltpu.roll(first, BS, 1)
        second_turned = pltpu.roll(second, BS, 1)
        mixed[slot, pl.ds(0, 8, stride=2), :] = jnp.where(low_half8, first, second_turned)
        mixed[slot, pl.ds(1, 8, stride=2), :] = jnp.where(low_half8, first_turned, second)

    def lines_of(source, first, quarter):
        lanes = slice(quarter * 1024, quarter * 1024 + 1024)
        part = source[pl.ds(pl.multiple_of(first, 16), 16), lanes]
        return part.astype(F32).reshape(16, 8, 128)

    def await_piece(piece):
        pltpu.make_async_copy(lrem_hbm.at[0, 0], raw.at[piece], load_sems.at[piece]).wait()

    def flatten_piece(piece):
        await_piece(piece)

        def body(step, _):
            for quarter in range(4):
                lines = [lines_of(raw.at[piece, couple], step * 16, quarter) for couple in range(3)]
                for slot in range(16):
                    interleave(quarter * 32 + slot, lines[0][slot], lines[1][slot])
                    third = lines[2][slot]
                    turned = pltpu.roll(third, BS, 1)
                    at = quarter * 32 + 16 + slot
                    mixed[at, pl.ds(0, 8, stride=2), :] = third
                    mixed[at, pl.ds(1, 8, stride=2), :] = turned
                for slot in range(16):
                    group = step * GROUP + slot // GROUP
                    row = (slot % GROUP) * BS + quarter * 16
                    flat[group, row : row + 16, 0:128] = mixed[quarter * 32 + slot].astype(BF16)
                    flat[group, row : row + 16, 128:DEPTH] = mixed[
                        quarter * 32 + 16 + slot, :, : DEPTH - 128
                    ].astype(BF16)
            return 0

        lax.fori_loop(0, blocks // 16, body, 0)

    def turned(rows):
        return dot_rows(identity[: rows.shape[1], : rows.shape[1]], rows).astype(BF16)

    def prepare_lower(piece, _):
        flatten_piece(piece)

        def body(group, _):
            mats[piece * groups + group] = turned(flat[group, :, :DEPTH])
            return 0

        lax.fori_loop(0, groups, body, 0, unroll=4)
        return 0

    member_lane = lax.broadcasted_iota(jnp.int32, (BS, GROUP * BS), 1) // BS

    def prepare_upper(color, _):
        piece = steps + 1 + color
        flatten_piece(piece)

        def body(group, _):
            inverses = w_dinv[color * groups + group]
            apart = [
                jnp.where(member_lane == member, inverses, jnp.zeros_like(inverses))
                for member in range(GROUP)
            ]
            product = dot_rows(turned(flat[group, :, :DEPTH]), jnp.concatenate(apart, axis=0))
            mats[piece * groups + group] = product.astype(BF16)
            return 0

        lax.fori_loop(0, groups, body, 0, unroll=4)
        return 0

    def prepare_rhs():
        load_rhs.wait()

        def body(step, _):
            color, first = step // (blocks // 8), lax.rem(step, blocks // 8) * 8
            lines = raw_rhs[color, pl.ds(pl.multiple_of(first, 8), 8), :].reshape(8, 8, 128)
            for slot in range(8):
                rhs[color, first + slot] = doubled(lines[slot])
            return 0

        lax.fori_loop(0, colors * blocks // 8, body, 0, unroll=8)

    def prepare_sums():
        load_dinv.wait()

        def dinv_body(step, _):
            color, first = step // (blocks // 16), lax.rem(step, blocks // 16) * 16
            for quarter in range(4):
                lines = lines_of(raw_dinv.at[color], first, quarter)
                for pair in range(8):
                    interleave(quarter * 8 + pair, lines[2 * pair], lines[2 * pair + 1])
                for pair in range(8):
                    group = color * groups + first // GROUP + pair // 2
                    lanes = slice((pair % 2) * 128, (pair % 2) * 128 + 128)
                    value = mixed[quarter * 8 + pair].astype(BF16)
                    w_dinv[group, quarter * 16 : quarter * 16 + 16, lanes] = value
            return 0

        lax.fori_loop(0, colors * blocks // 16, dinv_body, 0)

        def dinv_turn(group, _):
            inverses = w_dinv[group]
            mat_dinv[group] = turned(jnp.concatenate([inverses, inverses], axis=0))
            return 0

        lax.fori_loop(0, colors * groups, dinv_turn, 0, unroll=4)
        load_urem.wait()

        def urem_body(step, _):
            for quarter in range(4):
                for couple in range(3):
                    lines = lines_of(raw_urem.at[couple], step * 16, quarter)
                    for pair in range(8):
                        interleave(quarter * 24 + couple * 8 + pair, lines[2 * pair], lines[2 * pair + 1])
                    for pair in range(8):
                        group = step * GROUP + pair // 2
                        lanes = slice((pair % 2) * 128, (pair % 2) * 128 + 128)
                        value = mixed[quarter * 24 + couple * 8 + pair].astype(BF16)
                        row = couple * BS + quarter * 16
                        flat[group, row : row + 16, lanes] = value
                        if couple == 2:
                            flat[group, row + BS : row + BS + 16, lanes] = value
            return 0

        lax.fori_loop(0, blocks // 16, urem_body, 0)

        def urem_turn(group, _):
            mat_urem[group] = turned(flat[group])
            return 0

        lax.fori_loop(0, groups, urem_turn, 0, unroll=4)

        lane = lax.broadcasted_iota(jnp.int32, (8, 128), 1)
        for vector in range(edge_code.shape[1] // 128):
            code = jnp.zeros((8, 128), jnp.int32)
            for within in range(16):
                edge = vector * 16 + within
                code = jnp.where(lane // 8 == within, slot_idx[0, edge % 3, 0, edge // 3] * 8 + lane % 8, code)
            edge_code[:, vector * 128 : vector * 128 + 128] = code
        for vector in range(owner_code.shape[1] // 128):
            code = jnp.zeros((8, 128), jnp.int32)
            for within in range(16):
                slot = vector * 16 + within
                code = jnp.where(
                    lane // 8 == within, send_idx[slot % per_peer, slot // per_peer] * 8 + lane % 8, code
                )
            owner_code[:, vector * 128 : vector * 128 + 128] = code

        def hot(target, codes):
            def body(chunk, _):
                rows = lax.broadcasted_iota(jnp.int32, (64, target.shape[1]), 0) + chunk * 64
                target[pl.ds(pl.multiple_of(chunk * 64, 64), 64), :] = jnp.where(
                    rows == codes[0:1, :], 1.0, 0.0
                ).astype(BF16)
                return 0

            lax.fori_loop(0, target.shape[0] // 64, body, 0)

        hot(edge_hot, edge_code)
        hot(owner_hot, owner_code)

    def gathered(indices, source, group):
        members = []
        for member in range(GROUP):
            first, second, third = [source[at] for at in indices(group * GROUP + member)]
            members.append(
                jnp.concatenate([jnp.where(low_half16, first, second), third[:, :BS]], axis=1)
            )
        return jnp.concatenate(members, axis=0)

    def own_block(product, member):
        lanes = slice((member // 2) * 128, (member // 2) * 128 + 128)
        piece = product[member * 16 : member * 16 + 16, lanes]
        turned = pltpu.roll(piece, BS, 1)
        if member % 2 == 0:
            return jnp.where(low_half16, piece, turned)
        return jnp.where(low_half16, turned, piece)

    def spread(source, group):
        members = []
        for member in range(GROUP):
            value = source[group * GROUP + member]
            if member % 2 == 0:
                kept = jnp.where(low_half16, value, zero16)
            else:
                kept = jnp.where(low_half16, zero16, value)
            pair = [kept, zero16] if member < 2 else [zero16, kept]
            members.append(jnp.concatenate(pair, axis=1))
        return jnp.concatenate(members, axis=0)

    def forward_step(multiply, indices, source, color):
        def body(group, _):
            product = multiply(gathered(indices, source, group), group)
            for member in range(GROUP):
                block = group * GROUP + member
                reduced[block] = (rhs[color, block] - own_block(product, member)).astype(BF16)
            return 0

        lax.fori_loop(0, groups, body, 0, unroll=groups)
        solved[color] = reduced[...]

    def by_piece(piece):
        return lambda rows, group: jnp.dot(
            rows, mats[piece * groups + group], preferred_element_type=F32
        )

    def remote_indices(block):
        return [slot_idx[0, couple, 0, block] for couple in range(3)]

    def lower_indices(color):
        return lambda block: [low_idx[0, color - 1, couple, 0, block] for couple in range(3)]

    prepare_rhs()

    @pl.when(level == 0)
    def _():
        def body(block, _):
            solved[0, block] = rhs[0, block].astype(BF16)
            return 0

        lax.fori_loop(0, blocks, body, 0, unroll=8)

        def color_body(color, _):
            flatten_piece(color - 1)
            forward_step(
                lambda rows, group: dot_rows(rows, flat[group, :, :DEPTH]),
                lower_indices(color),
                solved.at[color - 1],
                color,
            )
            return 0

        lax.fori_loop(1, colors, color_body, 0)

    identity[...] = jnp.where(
        lax.broadcasted_iota(jnp.int32, (256, 256), 0) == lax.broadcasted_iota(jnp.int32, (256, 256), 1),
        1.0,
        0.0,
    ).astype(BF16)

    @pl.when(level > 0)
    def _():
        lax.fori_loop(0, steps + 1, prepare_lower, 0)

    @pl.when(level >= 2)
    def _():
        prepare_sums()

    lax.fori_loop(0, jnp.where(level == levels - 1, steps, 0), prepare_upper, 0)

    @pl.when(level > 0)
    def _():
        pltpu.make_async_copy(recv_f, recv_f, sems.at[1]).wait()

        def body(pair, _):
            both = recv_f[pl.ds(pl.multiple_of(pair * 16, 16), 16), :].astype(F32)
            rtable[pair * 2] = doubled(both[:8]).astype(BF16)
            rtable[pair * 2 + 1] = doubled(both[8:]).astype(BF16)
            return 0

        lax.fori_loop(0, recv_f.shape[0] // 16, body, 0, unroll=8)
        forward_step(by_piece(remote_piece), remote_indices, rtable, 0)

        def color_body(color, _):
            forward_step(by_piece(color - 1), lower_indices(color), solved.at[color - 1], color)
            return 0

        lax.fori_loop(1, colors, color_body, 0)

    pl.semaphore_wait(
        barrier, parts * ((level > 0).astype(jnp.int32) + (level < levels - 1).astype(jnp.int32))
    )

    @pl.when(level < levels - 1)
    def _():
        def pack(block, _):
            boundary[block] = paired(solved[colors - 1, block].astype(F32))
            return 0

        lax.fori_loop(0, blocks, pack, 0, unroll=8)

        for peer in peers:
            for pair in range(per_peer // 2):
                both = jnp.concatenate(
                    [boundary[send_idx[pair * 2, peer]], boundary[send_idx[pair * 2 + 1, peer]]], axis=0
                )
                send_f[pl.ds(pl.multiple_of(peer * rows_per_peer + pair * 16, 16), 16), :] = both.astype(BF16)
            pltpu.make_async_remote_copy(
                src_ref=send_f.at[pl.ds(pl.multiple_of(peer * rows_per_peer, 16), rows_per_peer)],
                dst_ref=recv_f.at[pl.ds(pl.multiple_of(me * rows_per_peer, 16), rows_per_peer)],
                send_sem=sems.at[0],
                recv_sem=sems.at[1],
                device_id=(level + 1, peer),
                device_id_type=MESH,
            ).start()

    @pl.when(level == 0)
    def _():
        await_piece(remote_piece)

    @pl.when(level < 2)
    def _():
        prepare_sums()

    lax.fori_loop(0, jnp.where(level == levels - 1, 0, steps), prepare_upper, 0)

    def scale(color, source, put):
        def body(group, _):
            product = jnp.dot(
                spread(source, group), mat_dinv[color * groups + group], preferred_element_type=F32
            )
            for member in range(GROUP):
                put(group * GROUP + member, product[member * 16 : member * 16 + 16])
            return 0

        lax.fori_loop(0, groups, body, 0, unroll=groups)

    def scale_solved(color, _):
        def put(block, value):
            base[color, block] = value

        scale(color, solved.at[color], put)
        return 0

    lax.fori_loop(0, steps, scale_solved, 0)

    def store_out(color):
        for first in range(0, blocks, 16):
            values = [paired(table[color, first + slot].astype(F32))[None] for slot in range(16)]
            rows = jnp.concatenate(values, axis=0).reshape(16, 16 * BS)
            out[color, first : first + 16, :] = rows.astype(BF16)

    @pl.when(level == levels - 1)
    def _():
        upward[...] = jnp.zeros_like(upward)

    @pl.when(level < levels - 1)
    def _():
        pltpu.make_async_copy(recv_b, recv_b, sems.at[3]).wait()
        upward[...] = jnp.dot(owner_hot[...], recv_b[...], preferred_element_type=F32)

    def last_color(block, _):
        add = doubled(upward[pl.ds(pl.multiple_of(block * 8, 8), 8), :])
        reduced[block] = (solved[colors - 1, block].astype(F32) - add).astype(BF16)
        return 0

    lax.fori_loop(0, blocks, last_color, 0, unroll=16)

    def put_last(block, value):
        table[colors - 1, block] = value.astype(BF16)

    scale(colors - 1, reduced, put_last)

    def back_color(step, _):
        color = colors - 2 - step
        source = table.at[color + 1]
        store_out(color + 1)
        multiply = by_piece(steps + 1 + color)

        def indices(block):
            return [up_idx[0, color, couple, 0, block] for couple in range(3)]

        def body(group, _):
            product = multiply(gathered(indices, source, group), group)
            for member in range(GROUP):
                block = group * GROUP + member
                reduced[block] = (base[color, block] - own_block(product, member)).astype(BF16)
            return 0

        lax.fori_loop(0, groups, body, 0, unroll=groups)
        table[color] = reduced[...]
        return 0

    lax.fori_loop(0, steps, back_color, 0)

    @pl.when(level > 0)
    def _():
        def body(group, _):
            product = jnp.dot(
                spread(table.at[0], group), mat_urem[group], preferred_element_type=F32
            )
            results = []
            for member in range(GROUP):
                rows = product[member * 16 : member * 16 + 16]
                both, third = rows[:, :128], rows[:, 128:]
                turned = pltpu.roll(both, BS, 1)
                results.append(jnp.where(low_half8, both[:8], turned[8:]))
                results.append(jnp.where(low_half8, turned[:8], both[8:]))
                results.append(paired(third))
            at = pl.ds(pl.multiple_of(group * GROUP * 24, 96), GROUP * 24)
            terms[at, :] = jnp.concatenate(results, axis=0).astype(BF16)
            return 0

        lax.fori_loop(0, groups, body, 0, unroll=groups)
        send_b[...] = jnp.dot(edge_hot[...], terms[...], preferred_element_type=F32).astype(BF16)

        for peer in peers:
            pltpu.make_async_remote_copy(
                src_ref=send_b.at[pl.ds(pl.multiple_of(peer * rows_per_peer, 16), rows_per_peer)],
                dst_ref=recv_b.at[pl.ds(pl.multiple_of(me * rows_per_peer, 16), rows_per_peer)],
                send_sem=sems.at[2],
                recv_sem=sems.at[3],
                device_id=(level - 1, peer),
                device_id_type=MESH,
            ).start()

    store_out(0)

    @pl.when(level > 0)
    def _():
        pltpu.make_async_copy(send_b, send_b, sems.at[2]).wait()

    @pl.when(level < levels - 1)
    def _():
        pltpu.make_async_copy(send_f, send_f, sems.at[0]).wait()


def per_device(
    levels,
    parts,
    rhs,
    dinv,
    lower_local,
    lower_nbrs,
    upper_local,
    upper_nbrs,
    lower_remote,
    upper_remote,
    remote_slots,
    send_list,
):
    colors, blocks, features = rhs.shape[2:]
    entries = dinv.shape[-1]
    steps, pieces = colors - 1, 2 * colors - 1
    groups = blocks // GROUP
    slots = parts * send_list.shape[-1]

    smem = pl.BlockSpec(memory_space=pltpu.SMEM)
    vmem = pl.BlockSpec(memory_space=pltpu.VMEM)
    hbm = pl.BlockSpec(memory_space=pl.ANY)
    answer = pl.pallas_call(
        functools.partial(kernel, levels, parts),
        out_shape=jax.ShapeDtypeStruct((colors, blocks, features), BF16),
        in_specs=[smem] * 4 + [hbm] * 6,
        out_specs=vmem,
        scratch_shapes=[
            pltpu.VMEM((colors, blocks, features), F32),
            pltpu.VMEM((pieces, 3, blocks, entries), BF16),
            pltpu.VMEM((3, blocks, entries), BF16),
            pltpu.VMEM((colors, blocks, entries), BF16),
            pltpu.VMEM((groups, GROUP * BS, 256), BF16),
            pltpu.VMEM((pieces * groups, DEPTH, GROUP * BS), BF16),
            pltpu.VMEM((groups, GROUP * BS, 256), BF16),
            pltpu.VMEM((colors * groups, BS, GROUP * BS), BF16),
            pltpu.VMEM((colors * groups, GROUP * BS, 2 * BS), BF16),
            pltpu.VMEM((256, 256), BF16),
            pltpu.VMEM((colors, blocks, 16, 128), F32),
            pltpu.VMEM((128, 16, 128), F32),
            pltpu.VMEM((colors, blocks, 16, 128), BF16),
            pltpu.VMEM((blocks, 16, 128), BF16),
            pltpu.VMEM((steps, blocks, 16, 128), F32),
            pltpu.VMEM((colors, blocks, 16, 128), BF16),
            pltpu.VMEM((slots, 16, 128), BF16),
            pltpu.VMEM((blocks, 8, 128), F32),
            pltpu.VMEM((blocks * 8, 128), F32),
            pltpu.VMEM((blocks * 24, 128), BF16),
            pltpu.VMEM((8, blocks * 24), jnp.int32),
            pltpu.VMEM((8, slots * 8), jnp.int32),
            pltpu.VMEM((slots * 8, blocks * 24), BF16),
            pltpu.VMEM((blocks * 8, slots * 8), BF16),
            pltpu.VMEM((slots * 8, 128), BF16),
            pltpu.VMEM((slots * 8, 128), BF16),
            pltpu.VMEM((slots * 8, 128), BF16),
            pltpu.VMEM((slots * 8, 128), BF16),
            pltpu.SemaphoreType.DMA((4,)),
            pltpu.SemaphoreType.DMA((pieces + 3,)),
        ],
        compiler_params=pltpu.CompilerParams(
            collective_id=0, has_side_effects=True, vmem_limit_bytes=60 * 1024 * 1024
        ),
        name="sweeps",
    )(
        jnp.transpose(lower_nbrs, (0, 2, 4, 1, 3)),
        jnp.transpose(upper_nbrs, (0, 2, 4, 1, 3)),
        jnp.transpose(remote_slots, (0, 3, 1, 2)),
        jnp.swapaxes(send_list[0, 0], 0, 1),
        rhs,
        jnp.swapaxes(lower_local, 3, 4),
        jnp.swapaxes(upper_local, 3, 4),
        jnp.swapaxes(lower_remote, 2, 3),
        jnp.swapaxes(upper_remote, 2, 3),
        dinv,
    )
    return answer[None, None]


def solution(mesh):
    levels, parts = mesh.shape["level"], mesh.shape["dom"]
    return jax.shard_map(
        functools.partial(per_device, levels, parts),
        mesh=mesh,
        in_specs=(
            P("level", "dom", None, None, None),
            P("level", "dom", None, None, None),
            P("level", "dom", None, None, None, None),
            P("level", "dom", None, None, None),
            P("level", "dom", None, None, None, None),
            P("level", "dom", None, None, None),
            P("level", "dom", None, None, None),
            P("level", "dom", None, None, None),
            P("level", "dom", None, None),
            P("level", "dom", None, None),
        ),
        out_specs=P("level", "dom", None, None, None),
        check_vma=False,
    )
```

```python
import functools

import jax
import jax.numpy as jnp
from jax import lax
from jax.experimental import pallas as pl
from jax.experimental.pallas import tpu as pltpu
from jax.sharding import PartitionSpec as P

BS = 64
GROUP = 4
DEPTH = 3 * BS
MESH = pl.DeviceIdType.MESH
BF16 = jnp.bfloat16
F32 = jnp.float32


def dot_rows(left, right):
    return lax.dot_general(left, right, (((1,), (1,)), ((), ())), preferred_element_type=F32)


def far_first(parts):
    if parts != 32:
        return [(0, 0, step) for step in range(parts)], (1, 1, parts)
    hops = lambda step: min(step, 4 - step)
    steps = [(z, y, core) for z in range(4) for y in range(4) for core in range(2)]
    steps.sort(key=lambda at: -(hops(at[0]) + hops(at[1]) + 0.5 * at[2]))
    return steps, (4, 4, 2)


def kernel(
    levels,
    parts,
    low_idx,
    up_idx,
    slot_idx,
    send_idx,
    rhs_hbm,
    low_hbm,
    up_hbm,
    lrem_hbm,
    urem_hbm,
    dinv_hbm,
    out,
    raw_rhs,
    raw,
    raw_urem,
    raw_dinv,
    flat,
    mats,
    mat_urem,
    w_dinv,
    mat_dinv,
    identity,
    rhs,
    mixed,
    solved,
    reduced,
    table,
    rtable,
    upward,
    terms,
    edge_code,
    owner_code,
    edge_hot,
    owner_hot,
    send_f,
    recv_f,
    send_b,
    recv_b,
    sems,
    load_sems,
):
    level = lax.axis_index("level")
    me = lax.axis_index("dom")
    colors, blocks = solved.shape[1], solved.shape[2]
    steps = colors - 1
    groups = blocks // GROUP
    per_peer = send_idx.shape[0]
    rows_per_peer = send_f.shape[1] // parts
    offsets, sides = far_first(parts)
    at_z, at_y, at_core = me // (sides[1] * sides[2]), lax.rem(me // sides[2], sides[1]), lax.rem(me, sides[2])
    peers = [
        (lax.rem(at_z + z, sides[0]) * sides[1] + lax.rem(at_y + y, sides[1])) * sides[2]
        + lax.rem(at_core + core, sides[2])
        for z, y, core in offsets
    ]
    remote_piece = steps
    pieces = 2 * steps + 1

    def piece_source(piece):
        if piece < steps:
            return low_hbm.at[0, 0, piece]
        if piece == steps:
            return lrem_hbm.at[0, 0]
        return up_hbm.at[0, 0, piece - steps - 1]

    load_rhs = pltpu.make_async_copy(rhs_hbm.at[0, 0], raw_rhs, load_sems.at[pieces])
    load_urem = pltpu.make_async_copy(urem_hbm.at[0, 0], raw_urem, load_sems.at[pieces + 1])
    load_dinv = pltpu.make_async_copy(dinv_hbm.at[0, 0], raw_dinv, load_sems.at[pieces + 2])
    load_rhs.start()
    for piece in range(steps + 1):
        pltpu.make_async_copy(piece_source(piece), raw.at[piece], load_sems.at[piece]).start()
    load_dinv.start()
    load_urem.start()
    for piece in range(steps + 1, pieces):
        pltpu.make_async_copy(piece_source(piece), raw.at[piece], load_sems.at[piece]).start()

    barrier = pltpu.get_barrier_semaphore()

    def greet(step, _):
        peer = lax.rem(me + step, parts)

        @pl.when(level > 0)
        def _():
            pl.semaphore_signal(barrier, inc=1, device_id=(level - 1, peer), device_id_type=MESH)

        @pl.when(level < levels - 1)
        def _():
            pl.semaphore_signal(barrier, inc=1, device_id=(level + 1, peer), device_id_type=MESH)

        return 0

    lax.fori_loop(0, parts, greet, 0)

    low_half8 = lax.broadcasted_iota(jnp.int32, (8, 128), 1) < BS
    top_half8 = lax.broadcasted_iota(jnp.int32, (8, 128), 0) < 4
    zero8 = jnp.zeros((8, 128), F32)

    def interleave(slot, first, second):
        first_turned = pltpu.roll(first, BS, 1)
        second_turned = pltpu.roll(second, BS, 1)
        mixed[slot, pl.ds(0, 8, stride=2), :] = jnp.where(low_half8, first, second_turned)
        mixed[slot, pl.ds(1, 8, stride=2), :] = jnp.where(low_half8, first_turned, second)

    def lines_of(source, first, quarter):
        lanes = slice(quarter * 1024, quarter * 1024 + 1024)
        part = source[pl.ds(pl.multiple_of(first, 16), 16), lanes]
        return part.astype(F32).reshape(16, 8, 128)

    def await_piece(piece):
        pltpu.make_async_copy(lrem_hbm.at[0, 0], raw.at[piece], load_sems.at[piece]).wait()

    def flatten_piece(piece, target):
        await_piece(piece)

        def body(step, _):
            for quarter in range(4):
                lines = [lines_of(raw.at[piece, couple], step * 16, quarter) for couple in range(3)]
                for slot in range(16):
                    interleave(quarter * 32 + slot, lines[0][slot], lines[1][slot])
                    third = lines[2][slot]
                    turned = pltpu.roll(third, BS, 1)
                    at = quarter * 32 + 16 + slot
                    mixed[at, pl.ds(0, 8, stride=2), :] = third
                    mixed[at, pl.ds(1, 8, stride=2), :] = turned
                for slot in range(16):
                    group = target * groups + step * GROUP + slot // GROUP
                    row = (slot % GROUP) * BS + quarter * 16
                    flat[group, row : row + 16, 0:128] = mixed[quarter * 32 + slot].astype(BF16)
                    flat[group, row : row + 16, 128:DEPTH] = mixed[
                        quarter * 32 + 16 + slot, :, : DEPTH - 128
                    ].astype(BF16)
            return 0

        lax.fori_loop(0, blocks // 16, body, 0)

    def turned(rows):
        return dot_rows(identity[: rows.shape[1], : rows.shape[1]], rows).astype(BF16)

    def prepare_lower(piece, _):
        flatten_piece(piece, 0)

        def body(group, _):
            mats[piece * groups + group] = turned(flat[group, :, :DEPTH])
            return 0

        lax.fori_loop(0, groups, body, 0, unroll=4)
        return 0

    member_lane = lax.broadcasted_iota(jnp.int32, (BS, GROUP * BS), 1) // BS

    def prepare_upper(color, _):
        piece = steps + 1 + color
        flatten_piece(piece, 0)

        def body(group, _):
            inverses = w_dinv[color * groups + group]
            apart = [
                jnp.where(member_lane == member, inverses, jnp.zeros_like(inverses))
                for member in range(GROUP)
            ]
            product = dot_rows(turned(flat[group, :, :DEPTH]), jnp.concatenate(apart, axis=0))
            mats[piece * groups + group] = product.astype(BF16)
            return 0

        lax.fori_loop(0, groups, body, 0, unroll=4)
        return 0

    def prepare_rhs():
        load_rhs.wait()

        def body(step, _):
            color, first = step // (blocks // 8), lax.rem(step, blocks // 8) * 8
            lines = raw_rhs[color, pl.ds(pl.multiple_of(first, 8), 8), :].reshape(8, 8, 128)
            for slot in range(8):
                line = lines[slot]
                turn = pltpu.roll(line, BS, 1)
                even = jnp.where(low_half8, line, turn)
                odd = pltpu.roll(jnp.where(low_half8, turn, line), 4, 0)
                rhs[0, color, first + slot] = jnp.where(top_half8, even, odd)
                rhs[1, color, first + slot] = jnp.where(top_half8, odd, even)
            return 0

        lax.fori_loop(0, colors * blocks // 8, body, 0, unroll=8)

    def prepare_sums():
        load_dinv.wait()

        def dinv_body(step, _):
            color, first = step // (blocks // 16), lax.rem(step, blocks // 16) * 16
            for quarter in range(4):
                lines = lines_of(raw_dinv.at[color], first, quarter)
                for pair in range(8):
                    interleave(quarter * 8 + pair, lines[2 * pair], lines[2 * pair + 1])
                for pair in range(8):
                    group = color * groups + first // GROUP + pair // 2
                    lanes = slice((pair % 2) * 128, (pair % 2) * 128 + 128)
                    value = mixed[quarter * 8 + pair].astype(BF16)
                    w_dinv[group, quarter * 16 : quarter * 16 + 16, lanes] = value
            return 0

        lax.fori_loop(0, colors * blocks // 16, dinv_body, 0)

        def dinv_turn(group, _):
            inverses = w_dinv[group]
            mat_dinv[group] = turned(jnp.concatenate([inverses, inverses], axis=0))
            return 0

        lax.fori_loop(0, colors * groups, dinv_turn, 0, unroll=4)
        load_urem.wait()

        def urem_body(step, _):
            for quarter in range(4):
                for couple in range(3):
                    lines = lines_of(raw_urem.at[couple], step * 16, quarter)
                    for pair in range(8):
                        interleave(quarter * 24 + couple * 8 + pair, lines[2 * pair], lines[2 * pair + 1])
                    for pair in range(8):
                        group = step * GROUP + pair // 2
                        lanes = slice((pair % 2) * 128, (pair % 2) * 128 + 128)
                        value = mixed[quarter * 24 + couple * 8 + pair].astype(BF16)
                        row = couple * BS + quarter * 16
                        flat[group, row : row + 16, lanes] = value
                        if couple == 2:
                            flat[group, row + BS : row + BS + 16, lanes] = value
            return 0

        lax.fori_loop(0, blocks // 16, urem_body, 0)

        def urem_turn(group, _):
            mat_urem[group] = turned(flat[group])
            return 0

        lax.fori_loop(0, groups, urem_turn, 0, unroll=4)

        lane = lax.broadcasted_iota(jnp.int32, (8, 128), 1)

        def spell(number_of):
            code = jnp.zeros((8, 128), jnp.int32)
            for within in range(16):
                code = jnp.where(lane // 8 == within, number_of(within), code)
            return code

        per_term = blocks // 16
        for parity, couples in enumerate(((0, 1, 2), (1, 0, 2))):
            for vector in range(3 * per_term):
                couple, first = couples[vector // per_term], vector % per_term * 16
                slot = spell(lambda within: slot_idx[0, couple, 0, first + within])
                place = jnp.where(slot % 2 == parity, slot // 2 * 8 + lane % 8, -1)
                edge_code[parity, :, vector * 128 : vector * 128 + 128] = place
            for vector in range(owner_code.shape[2] // 128):
                pairs = per_peer // 2

                def owner(within):
                    at = vector * 16 + within
                    return send_idx[at % pairs * 2 + parity, at // pairs]

                place = spell(owner) * 8 + lane % 8
                owner_code[parity, :, vector * 128 : vector * 128 + 128] = place

        def hot(target, codes):
            def body(chunk, _):
                rows = lax.broadcasted_iota(jnp.int32, (64, target.shape[1]), 0) + chunk * 64
                target[pl.ds(pl.multiple_of(chunk * 64, 64), 64), :] = jnp.where(
                    rows == codes[0:1, :], 1.0, 0.0
                ).astype(BF16)
                return 0

            lax.fori_loop(0, target.shape[0] // 64, body, 0)

        for parity in range(2):
            hot(edge_hot.at[parity], edge_code.at[parity])
            hot(owner_hot.at[parity], owner_code.at[parity])

    def gathered(indices, source, group):
        firsts, thirds = [], []
        for member in range(GROUP):
            first, second, third = [source[at] for at in indices(group * GROUP + member)]
            firsts.append(jnp.where(low_half8, first, second))
            thirds.append(third)
        third = jnp.concatenate(thirds, axis=0)[:, :BS]
        return jnp.concatenate([jnp.concatenate(firsts, axis=0), third], axis=1).astype(BF16)

    def own_block(product, member):
        lanes = slice((member // 2) * 128, (member // 2) * 128 + 128)
        piece = product[member * 8 : member * 8 + 8, lanes]
        turn = pltpu.roll(piece, BS, 1)
        if member % 2 == 0:
            return jnp.where(low_half8, piece, turn)
        return jnp.where(low_half8, turn, piece)

    def spread(source, group):
        members = []
        for member in range(GROUP):
            value = source[group * GROUP + member]
            if member % 2 == 0:
                kept = jnp.where(low_half8, value, zero8)
            else:
                kept = jnp.where(low_half8, zero8, value)
            pair = [kept, zero8] if member < 2 else [zero8, kept]
            members.append(jnp.concatenate(pair, axis=1))
        return jnp.concatenate(members, axis=0).astype(BF16)

    def forward_step(multiply, indices, source, half, color):
        def body(group, _):
            product = multiply(gathered(indices, source, group), group)
            for member in range(GROUP):
                block = group * GROUP + member
                reduced[block] = rhs[half, color, block] - own_block(product, member)
            return 0

        lax.fori_loop(0, groups, body, 0, unroll=groups)
        solved[half, color] = reduced[...]

    def by_piece(piece):
        return lambda rows, group: jnp.dot(
            rows, mats[piece * groups + group], preferred_element_type=F32
        )

    def remote_indices(block):
        return [slot_idx[0, couple, 0, block] for couple in range(3)]

    def lower_indices(color):
        return lambda block: [low_idx[0, color - 1, couple, 0, block] for couple in range(3)]

    prepare_rhs()

    @pl.when(level == 0)
    def _():
        flatten_piece(0, 0)

    identity[...] = jnp.where(
        lax.broadcasted_iota(jnp.int32, (256, 256), 0) == lax.broadcasted_iota(jnp.int32, (256, 256), 1),
        1.0,
        0.0,
    ).astype(BF16)

    @pl.when(level > 0)
    def _():
        lax.fori_loop(0, steps + 1, prepare_lower, 0)

    @pl.when(level >= 2)
    def _():
        prepare_sums()

    lax.fori_loop(0, jnp.where(level == levels - 1, steps, 0), prepare_upper, 0)

    pl.semaphore_wait(
        barrier, parts * ((level > 0).astype(jnp.int32) + (level < levels - 1).astype(jnp.int32))
    )

    def peer_rows(peer):
        return pl.ds(pl.multiple_of(peer * rows_per_peer, 16), rows_per_peer)

    def forward_half(half, _):
        @pl.when(level == 0)
        def _():
            solved[half, 0] = rhs[half, 0]

            def color_body(color, _):
                @pl.when((half == 0) & (color > 1))
                def _():
                    flatten_piece(color - 1, color - 1)

                forward_step(
                    lambda rows, group: dot_rows(rows, flat[(color - 1) * groups + group, :, :DEPTH]),
                    lower_indices(color),
                    solved.at[half, color - 1],
                    half,
                    color,
                )
                return 0

            lax.fori_loop(1, colors, color_body, 0)

        @pl.when(level > 0)
        def _():
            pltpu.make_async_copy(recv_f.at[half], recv_f.at[half], sems.at[2 + half]).wait()

            def body(pair, _):
                both = recv_f[half, pl.ds(pl.multiple_of(pair * 16, 16), 16), :].astype(F32)
                for side in range(2):
                    line = both[side * 8 : side * 8 + 8]
                    turn = pltpu.roll(line, BS, 1)
                    rtable[pair * 4 + side * 2] = jnp.where(low_half8, line, turn)
                    rtable[pair * 4 + side * 2 + 1] = jnp.where(low_half8, turn, line)
                return 0

            lax.fori_loop(0, recv_f.shape[1] // 16, body, 0, unroll=8)
            forward_step(by_piece(remote_piece), remote_indices, rtable, half, 0)

            def color_body(color, _):
                forward_step(
                    by_piece(color - 1), lower_indices(color), solved.at[half, color - 1], half, color
                )
                return 0

            lax.fori_loop(1, colors, color_body, 0)

        @pl.when(level < levels - 1)
        def _():
            for peer in peers:
                lines = []
                for pair in range(per_peer // 2):
                    even, odd = reduced[send_idx[pair * 2, peer]], reduced[send_idx[pair * 2 + 1, peer]]
                    lines.append(jnp.where(low_half8, even, odd))
                send_f[half, peer_rows(peer), :] = jnp.concatenate(lines, axis=0).astype(BF16)
                pltpu.make_async_remote_copy(
                    src_ref=send_f.at[half, peer_rows(peer)],
                    dst_ref=recv_f.at[half, peer_rows(me)],
                    send_sem=sems.at[half],
                    recv_sem=sems.at[2 + half],
                    device_id=(level + 1, peer),
                    device_id_type=MESH,
                ).start()

        return 0

    lax.fori_loop(0, 2, forward_half, 0)

    @pl.when(level == 0)
    def _():
        await_piece(remote_piece)

    @pl.when(level < 2)
    def _():
        prepare_sums()

    lax.fori_loop(0, jnp.where(level == levels - 1, 0, steps), prepare_upper, 0)

    def scale(color, source, put):
        def body(group, _):
            product = jnp.dot(
                spread(source, group), mat_dinv[color * groups + group], preferred_element_type=F32
            )
            for member in range(GROUP):
                put(group * GROUP + member, product[member * 8 : member * 8 + 8])
            return 0

        lax.fori_loop(0, groups, body, 0, unroll=groups)

    def scale_solved(at, _):
        half, color = at // steps, lax.rem(at, steps)

        def put(block, value):
            rhs[half, color, block] = value

        scale(color, solved.at[half, color], put)
        return 0

    lax.fori_loop(0, 2 * steps, scale_solved, 0)

    def store_out(color):
        for first in range(0, blocks, 16):
            values = []
            for slot in range(16):
                zero_half, one_half = table[0, color, first + slot], table[1, color, first + slot]
                even = jnp.where(top_half8, zero_half, one_half)
                odd = pltpu.roll(jnp.where(top_half8, one_half, zero_half), 4, 0)
                values.append(jnp.where(low_half8, even, odd)[None])
            rows = jnp.concatenate(values, axis=0).reshape(16, 16 * BS)
            out[color, first : first + 16, :] = rows.astype(BF16)

    low_lanes = lax.broadcasted_iota(jnp.int32, upward.shape, 1) < BS
    low_sums = lax.broadcasted_iota(jnp.int32, send_b.shape[1:], 1) < BS

    def backward_half(half, _):
        @pl.when(level == levels - 1)
        def _():
            upward[...] = jnp.zeros_like(upward)

        @pl.when(level < levels - 1)
        def _():
            pltpu.make_async_copy(recv_b.at[half], recv_b.at[half], sems.at[6 + half]).wait()
            even = jnp.dot(owner_hot[0], recv_b[half], preferred_element_type=F32)
            odd = jnp.dot(owner_hot[1], recv_b[half], preferred_element_type=F32)
            upward[...] = jnp.where(low_lanes, even, odd)

        def last_color(block, _):
            parts_of = upward[pl.ds(pl.multiple_of(block * 8, 8), 8), :]
            reduced[block] = solved[half, colors - 1, block] - (parts_of + pltpu.roll(parts_of, BS, 1))
            return 0

        lax.fori_loop(0, blocks, last_color, 0, unroll=16)

        def put_last(block, value):
            table[half, colors - 1, block] = value

        scale(colors - 1, reduced, put_last)

        def back_color(step, _):
            color = colors - 2 - step
            source = table.at[half, color + 1]
            store_out(color + 1)
            multiply = by_piece(steps + 1 + color)

            def indices(block):
                return [up_idx[0, color, couple, 0, block] for couple in range(3)]

            def body(group, _):
                product = multiply(gathered(indices, source, group), group)
                for member in range(GROUP):
                    block = group * GROUP + member
                    reduced[block] = rhs[half, color, block] - own_block(product, member)
                return 0

            lax.fori_loop(0, groups, body, 0, unroll=groups)
            table[half, color] = reduced[...]
            return 0

        lax.fori_loop(0, steps, back_color, 0)

        @pl.when(level > 0)
        def _():
            def body(group, _):
                product = jnp.dot(
                    spread(reduced, group), mat_urem[group], preferred_element_type=F32
                )
                both, third = product[:, :128], product[:, 128:]
                for term, value in enumerate((both, pltpu.roll(both, BS, 1), third)):
                    at = term * blocks * 8 + group * GROUP * 8
                    terms[pl.ds(pl.multiple_of(at, GROUP * 8), GROUP * 8), :] = value.astype(BF16)
                return 0

            lax.fori_loop(0, groups, body, 0, unroll=groups)
            even = jnp.dot(edge_hot[0], terms[...], preferred_element_type=F32)
            odd = jnp.dot(edge_hot[1], terms[...], preferred_element_type=F32)
            send_b[half] = jnp.where(low_sums, even, odd).astype(BF16)
            for peer in peers:
                pltpu.make_async_remote_copy(
                    src_ref=send_b.at[half, peer_rows(peer)],
                    dst_ref=recv_b.at[half, peer_rows(me)],
                    send_sem=sems.at[4 + half],
                    recv_sem=sems.at[6 + half],
                    device_id=(level - 1, peer),
                    device_id_type=MESH,
                ).start()

        return 0

    lax.fori_loop(0, 2, backward_half, 0)
    store_out(0)

    for half in range(2):

        @pl.when(level > 0)
        def _():
            pltpu.make_async_copy(send_b.at[half], send_b.at[half], sems.at[4 + half]).wait()

        @pl.when(level < levels - 1)
        def _():
            pltpu.make_async_copy(send_f.at[half], send_f.at[half], sems.at[half]).wait()


def per_device(
    levels,
    parts,
    rhs,
    dinv,
    lower_local,
    lower_nbrs,
    upper_local,
    upper_nbrs,
    lower_remote,
    upper_remote,
    remote_slots,
    send_list,
):
    colors, blocks, features = rhs.shape[2:]
    entries = dinv.shape[-1]
    steps, pieces = colors - 1, 2 * colors - 1
    groups = blocks // GROUP
    slots = parts * send_list.shape[-1]

    smem = pl.BlockSpec(memory_space=pltpu.SMEM)
    vmem = pl.BlockSpec(memory_space=pltpu.VMEM)
    hbm = pl.BlockSpec(memory_space=pl.ANY)
    answer = pl.pallas_call(
        functools.partial(kernel, levels, parts),
        out_shape=jax.ShapeDtypeStruct((colors, blocks, features), BF16),
        in_specs=[smem] * 4 + [hbm] * 6,
        out_specs=vmem,
        scratch_shapes=[
            pltpu.VMEM((colors, blocks, features), F32),
            pltpu.VMEM((pieces, 3, blocks, entries), BF16),
            pltpu.VMEM((3, blocks, entries), BF16),
            pltpu.VMEM((colors, blocks, entries), BF16),
            pltpu.VMEM((steps * groups, GROUP * BS, 256), BF16),
            pltpu.VMEM((pieces * groups, DEPTH, GROUP * BS), BF16),
            pltpu.VMEM((groups, GROUP * BS, 256), BF16),
            pltpu.VMEM((colors * groups, BS, GROUP * BS), BF16),
            pltpu.VMEM((colors * groups, GROUP * BS, 2 * BS), BF16),
            pltpu.VMEM((256, 256), BF16),
            pltpu.VMEM((2, colors, blocks, 8, 128), F32),
            pltpu.VMEM((128, 16, 128), F32),
            pltpu.VMEM((2, colors, blocks, 8, 128), F32),
            pltpu.VMEM((blocks, 8, 128), F32),
            pltpu.VMEM((2, colors, blocks, 8, 128), F32),
            pltpu.VMEM((slots, 8, 128), F32),
            pltpu.VMEM((blocks * 8, 128), F32),
            pltpu.VMEM((blocks * 24, 128), BF16),
            pltpu.VMEM((2, 8, blocks * 24), jnp.int32),
            pltpu.VMEM((2, 8, slots * 4), jnp.int32),
            pltpu.VMEM((2, slots * 4, blocks * 24), BF16),
            pltpu.VMEM((2, blocks * 8, slots * 4), BF16),
            pltpu.VMEM((2, slots * 4, 128), BF16),
            pltpu.VMEM((2, slots * 4, 128), BF16),
            pltpu.VMEM((2, slots * 4, 128), BF16),
            pltpu.VMEM((2, slots * 4, 128), BF16),
            pltpu.SemaphoreType.DMA((8,)),
            pltpu.SemaphoreType.DMA((pieces + 3,)),
        ],
        compiler_params=pltpu.CompilerParams(
            collective_id=0, has_side_effects=True, vmem_limit_bytes=60 * 1024 * 1024
        ),
        name="sweeps",
    )(
        jnp.transpose(lower_nbrs, (0, 2, 4, 1, 3)),
        jnp.transpose(upper_nbrs, (0, 2, 4, 1, 3)),
        jnp.transpose(remote_slots, (0, 3, 1, 2)),
        jnp.swapaxes(send_list[0, 0], 0, 1),
        rhs,
        jnp.swapaxes(lower_local, 3, 4),
        jnp.swapaxes(upper_local, 3, 4),
        jnp.swapaxes(lower_remote, 2, 3),
        jnp.swapaxes(upper_remote, 2, 3),
        dinv,
    )
    return answer[None, None]


def solution(mesh):
    levels, parts = mesh.shape["level"], mesh.shape["dom"]
    return jax.shard_map(
        functools.partial(per_device, levels, parts),
        mesh=mesh,
        in_specs=(
            P("level", "dom", None, None, None),
            P("level", "dom", None, None, None),
            P("level", "dom", None, None, None, None),
            P("level", "dom", None, None, None),
            P("level", "dom", None, None, None, None),
            P("level", "dom", None, None, None),
            P("level", "dom", None, None, None),
            P("level", "dom", None, None, None),
            P("level", "dom", None, None),
            P("level", "dom", None, None),
        ),
        out_specs=P("level", "dom", None, None, None),
        check_vma=False,
    )
```

```python
import functools

import jax
import jax.numpy as jnp
from jax import lax
from jax.experimental import pallas as pl
from jax.experimental.pallas import tpu as pltpu
from jax.sharding import PartitionSpec as P

BS = 64
GROUP = 4
DEPTH = 3 * BS
MESH = pl.DeviceIdType.MESH
BF16 = jnp.bfloat16
F32 = jnp.float32


def dot_rows(left, right):
    return lax.dot_general(left, right, (((1,), (1,)), ((), ())), preferred_element_type=F32)


def far_first(parts):
    if parts != 32:
        return [(0, 0, step) for step in range(parts)], (1, 1, parts)
    hops = lambda step: min(step, 4 - step)
    steps = [(z, y, core) for z in range(4) for y in range(4) for core in range(2)]
    steps.sort(key=lambda at: -(hops(at[0]) + hops(at[1]) + 0.5 * at[2]))
    return steps, (4, 4, 2)


def kernel(
    levels,
    parts,
    low_idx,
    up_idx,
    slot_idx,
    send_idx,
    rhs_hbm,
    low_hbm,
    up_hbm,
    lrem_hbm,
    urem_hbm,
    dinv_hbm,
    out,
    raw_rhs,
    raw,
    raw_urem,
    raw_dinv,
    flat,
    mats,
    mat_urem,
    w_dinv,
    mat_dinv,
    identity,
    rhs,
    mixed,
    solved,
    reduced,
    table,
    rtable,
    upward,
    terms,
    edge_code,
    owner_code,
    edge_hot,
    owner_hot,
    send_f,
    recv_f,
    send_b,
    recv_b,
    sems,
    load_sems,
):
    level = lax.axis_index("level")
    me = lax.axis_index("dom")
    colors, blocks = solved.shape[1], solved.shape[2]
    steps = colors - 1
    groups = blocks // GROUP
    per_peer = send_idx.shape[0]
    rows_per_peer = send_f.shape[1] // parts
    offsets, sides = far_first(parts)
    at_z, at_y, at_core = me // (sides[1] * sides[2]), lax.rem(me // sides[2], sides[1]), lax.rem(me, sides[2])
    peers = [
        (lax.rem(at_z + z, sides[0]) * sides[1] + lax.rem(at_y + y, sides[1])) * sides[2]
        + lax.rem(at_core + core, sides[2])
        for z, y, core in offsets
    ]
    remote_piece = steps
    pieces = 2 * steps + 1

    def piece_source(piece):
        if piece < steps:
            return low_hbm.at[0, 0, piece]
        if piece == steps:
            return lrem_hbm.at[0, 0]
        return up_hbm.at[0, 0, piece - steps - 1]

    load_rhs = pltpu.make_async_copy(rhs_hbm.at[0, 0], raw_rhs, load_sems.at[pieces])
    load_urem = pltpu.make_async_copy(urem_hbm.at[0, 0], raw_urem, load_sems.at[pieces + 1])
    load_dinv = pltpu.make_async_copy(dinv_hbm.at[0, 0], raw_dinv, load_sems.at[pieces + 2])
    load_rhs.start()
    for piece in range(steps + 1):
        pltpu.make_async_copy(piece_source(piece), raw.at[piece], load_sems.at[piece]).start()
    load_dinv.start()
    load_urem.start()
    for piece in range(steps + 1, pieces):
        pltpu.make_async_copy(piece_source(piece), raw.at[piece], load_sems.at[piece]).start()

    barrier = pltpu.get_barrier_semaphore()

    def greet(step, _):
        peer = lax.rem(me + step, parts)

        @pl.when(level > 0)
        def _():
            pl.semaphore_signal(barrier, inc=1, device_id=(level - 1, peer), device_id_type=MESH)

        @pl.when(level < levels - 1)
        def _():
            pl.semaphore_signal(barrier, inc=1, device_id=(level + 1, peer), device_id_type=MESH)

        return 0

    lax.fori_loop(0, parts, greet, 0)

    low_half8 = lax.broadcasted_iota(jnp.int32, (8, 128), 1) < BS
    top_half8 = lax.broadcasted_iota(jnp.int32, (8, 128), 0) < 4
    zero8 = jnp.zeros((8, 128), F32)

    def interleave(slot, first, second):
        first_turned = pltpu.roll(first, BS, 1)
        second_turned = pltpu.roll(second, BS, 1)
        mixed[slot, pl.ds(0, 8, stride=2), :] = jnp.where(low_half8, first, second_turned)
        mixed[slot, pl.ds(1, 8, stride=2), :] = jnp.where(low_half8, first_turned, second)

    def lines_of(source, first, quarter):
        lanes = slice(quarter * 1024, quarter * 1024 + 1024)
        part = source[pl.ds(pl.multiple_of(first, 16), 16), lanes]
        return part.astype(F32).reshape(16, 8, 128)

    def await_piece(piece):
        pltpu.make_async_copy(lrem_hbm.at[0, 0], raw.at[piece], load_sems.at[piece]).wait()

    def flatten_piece(piece, target):
        await_piece(piece)

        def body(step, _):
            for quarter in range(4):
                lines = [lines_of(raw.at[piece, couple], step * 16, quarter) for couple in range(3)]
                for slot in range(16):
                    interleave(quarter * 32 + slot, lines[0][slot], lines[1][slot])
                    third = lines[2][slot]
                    turned = pltpu.roll(third, BS, 1)
                    at = quarter * 32 + 16 + slot
                    mixed[at, pl.ds(0, 8, stride=2), :] = third
                    mixed[at, pl.ds(1, 8, stride=2), :] = turned
                for slot in range(16):
                    group = target * groups + step * GROUP + slot // GROUP
                    row = (slot % GROUP) * BS + quarter * 16
                    flat[group, row : row + 16, 0:128] = mixed[quarter * 32 + slot].astype(BF16)
                    flat[group, row : row + 16, 128:DEPTH] = mixed[
                        quarter * 32 + 16 + slot, :, : DEPTH - 128
                    ].astype(BF16)
            return 0

        lax.fori_loop(0, blocks // 16, body, 0)

    def turned(rows):
        return dot_rows(identity[: rows.shape[1], : rows.shape[1]], rows).astype(BF16)

    def prepare_lower(piece, _):
        flatten_piece(piece, 0)

        def body(group, _):
            mats[piece * groups + group] = turned(flat[group, :, :DEPTH])
            return 0

        lax.fori_loop(0, groups, body, 0, unroll=4)
        return 0

    member_lane = lax.broadcasted_iota(jnp.int32, (BS, GROUP * BS), 1) // BS

    def prepare_upper(color, _):
        piece = steps + 1 + color
        flatten_piece(piece, 0)

        def body(group, _):
            inverses = w_dinv[color * groups + group]
            apart = [
                jnp.where(member_lane == member, inverses, jnp.zeros_like(inverses))
                for member in range(GROUP)
            ]
            product = dot_rows(turned(flat[group, :, :DEPTH]), jnp.concatenate(apart, axis=0))
            mats[piece * groups + group] = product.astype(BF16)
            return 0

        lax.fori_loop(0, groups, body, 0, unroll=4)
        return 0

    def prepare_rhs():
        load_rhs.wait()

        def body(step, _):
            color, first = step // (blocks // 8), lax.rem(step, blocks // 8) * 8
            lines = raw_rhs[color, pl.ds(pl.multiple_of(first, 8), 8), :].reshape(8, 8, 128)
            for slot in range(8):
                line = lines[slot]
                turn = pltpu.roll(line, BS, 1)
                even = jnp.where(low_half8, line, turn)
                odd = pltpu.roll(jnp.where(low_half8, turn, line), 4, 0)
                rhs[0, color, first + slot] = jnp.where(top_half8, even, odd)
                rhs[1, color, first + slot] = jnp.where(top_half8, odd, even)
            return 0

        lax.fori_loop(0, colors * blocks // 8, body, 0, unroll=8)

    def prepare_sums():
        load_dinv.wait()

        def dinv_body(step, _):
            color, first = step // (blocks // 16), lax.rem(step, blocks // 16) * 16
            for quarter in range(4):
                lines = lines_of(raw_dinv.at[color], first, quarter)
                for pair in range(8):
                    interleave(quarter * 8 + pair, lines[2 * pair], lines[2 * pair + 1])
                for pair in range(8):
                    group = color * groups + first // GROUP + pair // 2
                    lanes = slice((pair % 2) * 128, (pair % 2) * 128 + 128)
                    value = mixed[quarter * 8 + pair].astype(BF16)
                    w_dinv[group, quarter * 16 : quarter * 16 + 16, lanes] = value
            return 0

        lax.fori_loop(0, colors * blocks // 16, dinv_body, 0)

        def dinv_turn(group, _):
            inverses = w_dinv[group]
            mat_dinv[group] = turned(jnp.concatenate([inverses, inverses], axis=0))
            return 0

        lax.fori_loop(0, colors * groups, dinv_turn, 0, unroll=4)
        load_urem.wait()

        def urem_body(step, _):
            for quarter in range(4):
                for couple in range(3):
                    lines = lines_of(raw_urem.at[couple], step * 16, quarter)
                    for pair in range(8):
                        interleave(quarter * 24 + couple * 8 + pair, lines[2 * pair], lines[2 * pair + 1])
                    for pair in range(8):
                        group = step * GROUP + pair // 2
                        lanes = slice((pair % 2) * 128, (pair % 2) * 128 + 128)
                        value = mixed[quarter * 24 + couple * 8 + pair].astype(BF16)
                        row = couple * BS + quarter * 16
                        flat[group, row : row + 16, lanes] = value
                        if couple == 2:
                            flat[group, row + BS : row + BS + 16, lanes] = value
            return 0

        lax.fori_loop(0, blocks // 16, urem_body, 0)

        def urem_turn(group, _):
            mat_urem[group] = turned(flat[group])
            return 0

        lax.fori_loop(0, groups, urem_turn, 0, unroll=4)

        lane = lax.broadcasted_iota(jnp.int32, (8, 128), 1)

        def spell(number_of):
            code = jnp.zeros((8, 128), jnp.int32)
            for within in range(16):
                code = jnp.where(lane // 8 == within, number_of(within), code)
            return code

        per_term = blocks // 16
        for parity, couples in enumerate(((0, 1, 2), (1, 0, 2))):
            for vector in range(3 * per_term):
                couple, first = couples[vector // per_term], vector % per_term * 16
                slot = spell(lambda within: slot_idx[0, couple, 0, first + within])
                place = jnp.where(slot % 2 == parity, slot // 2 * 8 + lane % 8, -1)
                edge_code[parity, :, vector * 128 : vector * 128 + 128] = place
            for vector in range(owner_code.shape[2] // 128):
                pairs = per_peer // 2

                def owner(within):
                    at = vector * 16 + within
                    return send_idx[at % pairs * 2 + parity, at // pairs]

                place = spell(owner) * 8 + lane % 8
                owner_code[parity, :, vector * 128 : vector * 128 + 128] = place

        def hot(target, codes):
            def body(chunk, _):
                rows = lax.broadcasted_iota(jnp.int32, (64, target.shape[1]), 0) + chunk * 64
                target[pl.ds(pl.multiple_of(chunk * 64, 64), 64), :] = jnp.where(
                    rows == codes[0:1, :], 1.0, 0.0
                ).astype(BF16)
                return 0

            lax.fori_loop(0, target.shape[0] // 64, body, 0)

        for parity in range(2):
            hot(edge_hot.at[parity], edge_code.at[parity])

        @pl.when(level < levels - 1)
        def _():
            for parity in range(2):
                hot(owner_hot.at[parity], owner_code.at[parity])

    def gathered(indices, source, group):
        firsts, thirds = [], []
        for member in range(GROUP):
            first, second, third = [source[at] for at in indices(group * GROUP + member)]
            firsts.append(jnp.where(low_half8, first, second))
            thirds.append(third)
        third = jnp.concatenate(thirds, axis=0)[:, :BS]
        return jnp.concatenate([jnp.concatenate(firsts, axis=0), third], axis=1).astype(BF16)

    def own_block(product, member):
        lanes = slice((member // 2) * 128, (member // 2) * 128 + 128)
        piece = product[member * 8 : member * 8 + 8, lanes]
        turn = pltpu.roll(piece, BS, 1)
        if member % 2 == 0:
            return jnp.where(low_half8, piece, turn)
        return jnp.where(low_half8, turn, piece)

    def spread(source, group):
        members = []
        for member in range(GROUP):
            value = source[group * GROUP + member]
            if member % 2 == 0:
                kept = jnp.where(low_half8, value, zero8)
            else:
                kept = jnp.where(low_half8, zero8, value)
            pair = [kept, zero8] if member < 2 else [zero8, kept]
            members.append(jnp.concatenate(pair, axis=1))
        return jnp.concatenate(members, axis=0).astype(BF16)

    def forward_step(multiply, indices, source, half, color):
        def body(group, _):
            product = multiply(gathered(indices, source, group), group)
            for member in range(GROUP):
                block = group * GROUP + member
                reduced[block] = rhs[half, color, block] - own_block(product, member)
            return 0

        lax.fori_loop(0, groups, body, 0, unroll=groups)
        solved[half, color] = reduced[...]

    def by_piece(piece):
        return lambda rows, group: jnp.dot(
            rows, mats[piece * groups + group], preferred_element_type=F32
        )

    def remote_indices(block):
        return [slot_idx[0, couple, 0, block] for couple in range(3)]

    def lower_indices(color):
        return lambda block: [low_idx[0, color - 1, couple, 0, block] for couple in range(3)]

    prepare_rhs()

    @pl.when(level == 0)
    def _():
        flatten_piece(0, 0)

    identity[...] = jnp.where(
        lax.broadcasted_iota(jnp.int32, (256, 256), 0) == lax.broadcasted_iota(jnp.int32, (256, 256), 1),
        1.0,
        0.0,
    ).astype(BF16)

    ahead = jnp.where(level == 0, 0, jnp.where(level == levels - 1, pieces, steps + 1))
    lax.fori_loop(0, ahead, prepare_lower, 0)

    @pl.when(level >= 2)
    def _():
        prepare_sums()

    pl.semaphore_wait(
        barrier, parts * ((level > 0).astype(jnp.int32) + (level < levels - 1).astype(jnp.int32))
    )

    def peer_rows(peer):
        return pl.ds(pl.multiple_of(peer * rows_per_peer, 16), rows_per_peer)

    def forward_half(half, _):
        @pl.when(level == 0)
        def _():
            solved[half, 0] = rhs[half, 0]

            def color_body(color, _):
                @pl.when((half == 0) & (color > 1))
                def _():
                    flatten_piece(color - 1, color - 1)

                forward_step(
                    lambda rows, group: dot_rows(rows, flat[(color - 1) * groups + group, :, :DEPTH]),
                    lower_indices(color),
                    solved.at[half, color - 1],
                    half,
                    color,
                )
                return 0

            lax.fori_loop(1, colors, color_body, 0)

        @pl.when(level > 0)
        def _():
            pltpu.make_async_copy(recv_f.at[half], recv_f.at[half], sems.at[2 + half]).wait()

            def body(pair, _):
                both = recv_f[half, pl.ds(pl.multiple_of(pair * 16, 16), 16), :].astype(F32)
                for side in range(2):
                    line = both[side * 8 : side * 8 + 8]
                    turn = pltpu.roll(line, BS, 1)
                    rtable[pair * 4 + side * 2] = jnp.where(low_half8, line, turn)
                    rtable[pair * 4 + side * 2 + 1] = jnp.where(low_half8, turn, line)
                return 0

            lax.fori_loop(0, recv_f.shape[1] // 16, body, 0, unroll=8)
            forward_step(by_piece(remote_piece), remote_indices, rtable, half, 0)

            def color_body(color, _):
                forward_step(
                    by_piece(color - 1), lower_indices(color), solved.at[half, color - 1], half, color
                )
                return 0

            lax.fori_loop(1, colors, color_body, 0)

        @pl.when(level < levels - 1)
        def _():
            for peer in peers:
                lines = []
                for pair in range(per_peer // 2):
                    even, odd = reduced[send_idx[pair * 2, peer]], reduced[send_idx[pair * 2 + 1, peer]]
                    lines.append(jnp.where(low_half8, even, odd))
                send_f[half, peer_rows(peer), :] = jnp.concatenate(lines, axis=0).astype(BF16)
                pltpu.make_async_remote_copy(
                    src_ref=send_f.at[half, peer_rows(peer)],
                    dst_ref=recv_f.at[half, peer_rows(me)],
                    send_sem=sems.at[half],
                    recv_sem=sems.at[2 + half],
                    device_id=(level + 1, peer),
                    device_id_type=MESH,
                ).start()

        return 0

    lax.fori_loop(0, 2, forward_half, 0)

    @pl.when(level == 0)
    def _():
        await_piece(remote_piece)

    @pl.when(level < 2)
    def _():
        prepare_sums()

    lax.fori_loop(0, jnp.where(level == levels - 1, 0, steps), prepare_upper, 0)

    def scale(color, source, put):
        def body(group, _):
            product = jnp.dot(
                spread(source, group), mat_dinv[color * groups + group], preferred_element_type=F32
            )
            for member in range(GROUP):
                put(group * GROUP + member, product[member * 8 : member * 8 + 8])
            return 0

        lax.fori_loop(0, groups, body, 0, unroll=groups)

    def scale_solved(at, _):
        half, color = at // steps, lax.rem(at, steps)

        def put(block, value):
            rhs[half, color, block] = value

        scale(color, solved.at[half, color], put)
        return 0

    @pl.when(level < levels - 1)
    def _():
        lax.fori_loop(0, 2 * steps, scale_solved, 0)

    @pl.when(level == levels - 1)
    def _():
        for half in range(2):
            for color in range(steps):
                rhs[half, color] = solved[half, color]


    def store_out(color):
        for first in range(0, blocks, 16):
            values = []
            for slot in range(16):
                zero_half, one_half = table[0, color, first + slot], table[1, color, first + slot]
                even = jnp.where(top_half8, zero_half, one_half)
                odd = pltpu.roll(jnp.where(top_half8, one_half, zero_half), 4, 0)
                values.append(jnp.where(low_half8, even, odd)[None])
            rows = jnp.concatenate(values, axis=0).reshape(16, 16 * BS)
            out[color, first : first + 16, :] = rows.astype(BF16)

    low_lanes = lax.broadcasted_iota(jnp.int32, upward.shape, 1) < BS
    low_sums = lax.broadcasted_iota(jnp.int32, send_b.shape[1:], 1) < BS

    def backward_half(half, _):
        @pl.when(level == levels - 1)
        def _():
            reduced[...] = solved[half, colors - 1]

        @pl.when(level < levels - 1)
        def _():
            pltpu.make_async_copy(recv_b.at[half], recv_b.at[half], sems.at[6 + half]).wait()
            even = jnp.dot(owner_hot[0], recv_b[half], preferred_element_type=F32)
            odd = jnp.dot(owner_hot[1], recv_b[half], preferred_element_type=F32)
            upward[...] = jnp.where(low_lanes, even, odd)

            def last_color(block, _):
                parts_of = upward[pl.ds(pl.multiple_of(block * 8, 8), 8), :]
                reduced[block] = solved[half, colors - 1, block] - (parts_of + pltpu.roll(parts_of, BS, 1))
                return 0

            lax.fori_loop(0, blocks, last_color, 0, unroll=blocks)

        def put_last(block, value):
            table[half, colors - 1, block] = value

        scale(colors - 1, reduced, put_last)

        def back_color(step, _):
            color = colors - 2 - step
            source = table.at[half, color + 1]
            store_out(color + 1)
            multiply = by_piece(steps + 1 + color)

            def indices(block):
                return [up_idx[0, color, couple, 0, block] for couple in range(3)]

            def body(group, _):
                product = multiply(gathered(indices, source, group), group)
                for member in range(GROUP):
                    block = group * GROUP + member
                    reduced[block] = rhs[half, color, block] - own_block(product, member)
                return 0

            lax.fori_loop(0, groups, body, 0, unroll=groups)

            @pl.when(level < levels - 1)
            def _():
                table[half, color] = reduced[...]

            @pl.when(level == levels - 1)
            def _():
                def put(block, value):
                    table[half, color, block] = value

                scale(color, reduced, put)

            return 0

        lax.fori_loop(0, steps, back_color, 0)

        @pl.when(level > 0)
        def _():
            def body(group, _):
                product = jnp.dot(
                    spread(table.at[half, 0], group), mat_urem[group], preferred_element_type=F32
                )
                both, third = product[:, :128], product[:, 128:]
                for term, value in enumerate((both, pltpu.roll(both, BS, 1), third)):
                    at = term * blocks * 8 + group * GROUP * 8
                    terms[pl.ds(pl.multiple_of(at, GROUP * 8), GROUP * 8), :] = value.astype(BF16)
                return 0

            lax.fori_loop(0, groups, body, 0, unroll=groups)
            even = jnp.dot(edge_hot[0], terms[...], preferred_element_type=F32)
            odd = jnp.dot(edge_hot[1], terms[...], preferred_element_type=F32)
            send_b[half] = jnp.where(low_sums, even, odd).astype(BF16)
            for peer in peers:
                pltpu.make_async_remote_copy(
                    src_ref=send_b.at[half, peer_rows(peer)],
                    dst_ref=recv_b.at[half, peer_rows(me)],
                    send_sem=sems.at[4 + half],
                    recv_sem=sems.at[6 + half],
                    device_id=(level - 1, peer),
                    device_id_type=MESH,
                ).start()

        return 0

    lax.fori_loop(0, 2, backward_half, 0)
    store_out(0)

    for half in range(2):

        @pl.when(level > 0)
        def _():
            pltpu.make_async_copy(send_b.at[half], send_b.at[half], sems.at[4 + half]).wait()

        @pl.when(level < levels - 1)
        def _():
            pltpu.make_async_copy(send_f.at[half], send_f.at[half], sems.at[half]).wait()


def per_device(
    levels,
    parts,
    rhs,
    dinv,
    lower_local,
    lower_nbrs,
    upper_local,
    upper_nbrs,
    lower_remote,
    upper_remote,
    remote_slots,
    send_list,
):
    colors, blocks, features = rhs.shape[2:]
    entries = dinv.shape[-1]
    steps, pieces = colors - 1, 2 * colors - 1
    groups = blocks // GROUP
    slots = parts * send_list.shape[-1]

    smem = pl.BlockSpec(memory_space=pltpu.SMEM)
    vmem = pl.BlockSpec(memory_space=pltpu.VMEM)
    hbm = pl.BlockSpec(memory_space=pl.ANY)
    answer = pl.pallas_call(
        functools.partial(kernel, levels, parts),
        out_shape=jax.ShapeDtypeStruct((colors, blocks, features), BF16),
        in_specs=[smem] * 4 + [hbm] * 6,
        out_specs=vmem,
        scratch_shapes=[
            pltpu.VMEM((colors, blocks, features), F32),
            pltpu.VMEM((pieces, 3, blocks, entries), BF16),
            pltpu.VMEM((3, blocks, entries), BF16),
            pltpu.VMEM((colors, blocks, entries), BF16),
            pltpu.VMEM((steps * groups, GROUP * BS, 256), BF16),
            pltpu.VMEM((pieces * groups, DEPTH, GROUP * BS), BF16),
            pltpu.VMEM((groups, GROUP * BS, 256), BF16),
            pltpu.VMEM((colors * groups, BS, GROUP * BS), BF16),
            pltpu.VMEM((colors * groups, GROUP * BS, 2 * BS), BF16),
            pltpu.VMEM((256, 256), BF16),
            pltpu.VMEM((2, colors, blocks, 8, 128), F32),
            pltpu.VMEM((128, 16, 128), F32),
            pltpu.VMEM((2, colors, blocks, 8, 128), F32),
            pltpu.VMEM((blocks, 8, 128), F32),
            pltpu.VMEM((2, colors, blocks, 8, 128), F32),
            pltpu.VMEM((slots, 8, 128), F32),
            pltpu.VMEM((blocks * 8, 128), F32),
            pltpu.VMEM((blocks * 24, 128), BF16),
            pltpu.VMEM((2, 8, blocks * 24), jnp.int32),
            pltpu.VMEM((2, 8, slots * 4), jnp.int32),
            pltpu.VMEM((2, slots * 4, blocks * 24), BF16),
            pltpu.VMEM((2, blocks * 8, slots * 4), BF16),
            pltpu.VMEM((2, slots * 4, 128), BF16),
            pltpu.VMEM((2, slots * 4, 128), BF16),
            pltpu.VMEM((2, slots * 4, 128), BF16),
            pltpu.VMEM((2, slots * 4, 128), BF16),
            pltpu.SemaphoreType.DMA((8,)),
            pltpu.SemaphoreType.DMA((pieces + 3,)),
        ],
        compiler_params=pltpu.CompilerParams(
            collective_id=0, has_side_effects=True, vmem_limit_bytes=60 * 1024 * 1024
        ),
        name="sweeps",
    )(
        jnp.transpose(lower_nbrs, (0, 2, 4, 1, 3)),
        jnp.transpose(upper_nbrs, (0, 2, 4, 1, 3)),
        jnp.transpose(remote_slots, (0, 3, 1, 2)),
        jnp.swapaxes(send_list[0, 0], 0, 1),
        rhs,
        jnp.swapaxes(lower_local, 3, 4),
        jnp.swapaxes(upper_local, 3, 4),
        jnp.swapaxes(lower_remote, 2, 3),
        jnp.swapaxes(upper_remote, 2, 3),
        dinv,
    )
    return answer[None, None]


def solution(mesh):
    levels, parts = mesh.shape["level"], mesh.shape["dom"]
    return jax.shard_map(
        functools.partial(per_device, levels, parts),
        mesh=mesh,
        in_specs=(
            P("level", "dom", None, None, None),
            P("level", "dom", None, None, None),
            P("level", "dom", None, None, None, None),
            P("level", "dom", None, None, None),
            P("level", "dom", None, None, None, None),
            P("level", "dom", None, None, None),
            P("level", "dom", None, None, None),
            P("level", "dom", None, None, None),
            P("level", "dom", None, None),
            P("level", "dom", None, None),
        ),
        out_specs=P("level", "dom", None, None, None),
        check_vma=False,
    )
```

```python
import functools

import jax
import jax.numpy as jnp
from jax import lax
from jax.experimental import pallas as pl
from jax.experimental.pallas import tpu as pltpu
from jax.sharding import PartitionSpec as P

BS = 64
GROUP = 4
DEPTH = 3 * BS
MESH = pl.DeviceIdType.MESH
BF16 = jnp.bfloat16
F32 = jnp.float32


def dot_rows(left, right):
    return lax.dot_general(left, right, (((1,), (1,)), ((), ())), preferred_element_type=F32)


def far_first(parts):
    if parts != 32:
        return [(0, 0, step) for step in range(parts)], (1, 1, parts)
    hops = lambda step: min(step, 4 - step)
    steps = [(z, y, core) for z in range(4) for y in range(4) for core in range(2)]
    steps.sort(key=lambda at: -(hops(at[0]) + hops(at[1]) + 0.5 * at[2]))
    return steps, (4, 4, 2)


def kernel(
    levels,
    parts,
    low_idx,
    up_idx,
    slot_idx,
    send_idx,
    rhs_hbm,
    low_hbm,
    up_hbm,
    lrem_hbm,
    urem_hbm,
    dinv_hbm,
    out,
    raw_rhs,
    raw,
    raw_urem,
    raw_dinv,
    flat,
    mats,
    mat_urem,
    w_dinv,
    mat_dinv,
    identity,
    rhs,
    mixed,
    solved,
    reduced,
    table,
    rtable,
    upward,
    terms,
    edge_code,
    owner_code,
    edge_hot,
    owner_hot,
    send_f,
    recv_f,
    send_b,
    recv_b,
    sems,
    load_sems,
):
    level = lax.axis_index("level")
    me = lax.axis_index("dom")
    colors, blocks = solved.shape[1], solved.shape[2]
    steps = colors - 1
    groups = blocks // GROUP
    per_peer = send_idx.shape[0]
    rows_per_peer = send_f.shape[1] // parts
    offsets, sides = far_first(parts)
    at_z, at_y, at_core = me // (sides[1] * sides[2]), lax.rem(me // sides[2], sides[1]), lax.rem(me, sides[2])
    peers = [
        (lax.rem(at_z + z, sides[0]) * sides[1] + lax.rem(at_y + y, sides[1])) * sides[2]
        + lax.rem(at_core + core, sides[2])
        for z, y, core in offsets
    ]
    remote_piece = steps
    pieces = 2 * steps + 1

    def piece_source(piece):
        if piece < steps:
            return low_hbm.at[0, 0, piece]
        if piece == steps:
            return lrem_hbm.at[0, 0]
        return up_hbm.at[0, 0, piece - steps - 1]

    load_rhs = pltpu.make_async_copy(rhs_hbm.at[0, 0], raw_rhs, load_sems.at[pieces])
    load_urem = pltpu.make_async_copy(urem_hbm.at[0, 0], raw_urem, load_sems.at[pieces + 1])
    load_dinv = pltpu.make_async_copy(dinv_hbm.at[0, 0], raw_dinv, load_sems.at[pieces + 2])
    load_rhs.start()
    pltpu.make_async_copy(piece_source(0), raw.at[0], load_sems.at[0]).start()

    def start_loads():
        for piece in range(1, steps + 1):
            pltpu.make_async_copy(piece_source(piece), raw.at[piece], load_sems.at[piece]).start()
        load_dinv.start()
        load_urem.start()
        for piece in range(steps + 1, pieces):
            pltpu.make_async_copy(piece_source(piece), raw.at[piece], load_sems.at[piece]).start()

    barrier = pltpu.get_barrier_semaphore()

    def greet(step, _):
        peer = lax.rem(me + step, parts)

        @pl.when(level > 0)
        def _():
            pl.semaphore_signal(barrier, inc=1, device_id=(level - 1, peer), device_id_type=MESH)

        @pl.when(level < levels - 1)
        def _():
            pl.semaphore_signal(barrier, inc=1, device_id=(level + 1, peer), device_id_type=MESH)

        return 0

    lax.fori_loop(0, parts, greet, 0)

    low_half8 = lax.broadcasted_iota(jnp.int32, (8, 128), 1) < BS
    top_half8 = lax.broadcasted_iota(jnp.int32, (8, 128), 0) < 4
    zero8 = jnp.zeros((8, 128), F32)

    def interleave(slot, first, second):
        first_turned = pltpu.roll(first, BS, 1)
        second_turned = pltpu.roll(second, BS, 1)
        mixed[slot, pl.ds(0, 8, stride=2), :] = jnp.where(low_half8, first, second_turned)
        mixed[slot, pl.ds(1, 8, stride=2), :] = jnp.where(low_half8, first_turned, second)

    def lines_of(source, first, quarter):
        lanes = slice(quarter * 1024, quarter * 1024 + 1024)
        part = source[pl.ds(pl.multiple_of(first, 16), 16), lanes]
        return part.astype(F32).reshape(16, 8, 128)

    def await_piece(piece):
        pltpu.make_async_copy(lrem_hbm.at[0, 0], raw.at[piece], load_sems.at[piece]).wait()

    def flatten_piece(piece, target):
        await_piece(piece)

        def body(step, _):
            for quarter in range(4):
                lines = [lines_of(raw.at[piece, couple], step * 16, quarter) for couple in range(3)]
                for slot in range(16):
                    interleave(quarter * 32 + slot, lines[0][slot], lines[1][slot])
                    third = lines[2][slot]
                    turned = pltpu.roll(third, BS, 1)
                    at = quarter * 32 + 16 + slot
                    mixed[at, pl.ds(0, 8, stride=2), :] = third
                    mixed[at, pl.ds(1, 8, stride=2), :] = turned
                for slot in range(16):
                    group = target * groups + step * GROUP + slot // GROUP
                    row = (slot % GROUP) * BS + quarter * 16
                    flat[group, row : row + 16, 0:128] = mixed[quarter * 32 + slot].astype(BF16)
                    flat[group, row : row + 16, 128:DEPTH] = mixed[
                        quarter * 32 + 16 + slot, :, : DEPTH - 128
                    ].astype(BF16)
            return 0

        lax.fori_loop(0, blocks // 16, body, 0)

    def turned(rows):
        return dot_rows(identity[: rows.shape[1], : rows.shape[1]], rows).astype(BF16)

    def prepare_lower(piece, _):
        flatten_piece(piece, 0)

        def body(group, _):
            mats[piece * groups + group] = turned(flat[group, :, :DEPTH])
            return 0

        lax.fori_loop(0, groups, body, 0, unroll=groups)
        return 0

    member_lane = lax.broadcasted_iota(jnp.int32, (BS, GROUP * BS), 1) // BS

    def prepare_upper(color, _):
        piece = steps + 1 + color
        flatten_piece(piece, 0)

        def body(group, _):
            inverses = w_dinv[color * groups + group]
            apart = [
                jnp.where(member_lane == member, inverses, jnp.zeros_like(inverses))
                for member in range(GROUP)
            ]
            product = dot_rows(turned(flat[group, :, :DEPTH]), jnp.concatenate(apart, axis=0))
            mats[piece * groups + group] = product.astype(BF16)
            return 0

        lax.fori_loop(0, groups, body, 0, unroll=4)
        return 0

    def prepare_rhs():
        load_rhs.wait()
        start_loads()

        def body(step, _):
            color, first = step // (blocks // 8), lax.rem(step, blocks // 8) * 8
            lines = raw_rhs[color, pl.ds(pl.multiple_of(first, 8), 8), :].reshape(8, 8, 128)
            for slot in range(8):
                line = lines[slot]
                turn = pltpu.roll(line, BS, 1)
                even = jnp.where(low_half8, line, turn)
                odd = pltpu.roll(jnp.where(low_half8, turn, line), 4, 0)
                rhs[0, color, first + slot] = jnp.where(top_half8, even, odd)
                rhs[1, color, first + slot] = jnp.where(top_half8, odd, even)
            return 0

        lax.fori_loop(0, colors * blocks // 8, body, 0, unroll=8)

    def prepare_sums():
        load_dinv.wait()

        def dinv_body(step, _):
            color, first = step // (blocks // 16), lax.rem(step, blocks // 16) * 16
            for quarter in range(4):
                lines = lines_of(raw_dinv.at[color], first, quarter)
                for pair in range(8):
                    interleave(quarter * 8 + pair, lines[2 * pair], lines[2 * pair + 1])
                for pair in range(8):
                    group = color * groups + first // GROUP + pair // 2
                    lanes = slice((pair % 2) * 128, (pair % 2) * 128 + 128)
                    value = mixed[quarter * 8 + pair].astype(BF16)
                    w_dinv[group, quarter * 16 : quarter * 16 + 16, lanes] = value
            return 0

        lax.fori_loop(0, colors * blocks // 16, dinv_body, 0)

        def dinv_turn(group, _):
            inverses = w_dinv[group]
            mat_dinv[group] = turned(jnp.concatenate([inverses, inverses], axis=0))
            return 0

        lax.fori_loop(0, colors * groups, dinv_turn, 0, unroll=groups)
        load_urem.wait()

        def urem_body(step, _):
            for quarter in range(4):
                for couple in range(3):
                    lines = lines_of(raw_urem.at[couple], step * 16, quarter)
                    for pair in range(8):
                        interleave(quarter * 24 + couple * 8 + pair, lines[2 * pair], lines[2 * pair + 1])
                    for pair in range(8):
                        group = step * GROUP + pair // 2
                        lanes = slice((pair % 2) * 128, (pair % 2) * 128 + 128)
                        value = mixed[quarter * 24 + couple * 8 + pair].astype(BF16)
                        row = couple * BS + quarter * 16
                        flat[group, row : row + 16, lanes] = value
                        if couple == 2:
                            flat[group, row + BS : row + BS + 16, lanes] = value
            return 0

        lax.fori_loop(0, blocks // 16, urem_body, 0)

        def urem_turn(group, _):
            mat_urem[group] = turned(flat[group])
            return 0

        lax.fori_loop(0, groups, urem_turn, 0, unroll=groups)

        lane = lax.broadcasted_iota(jnp.int32, (8, 128), 1)

        def spell(number_of):
            code = jnp.zeros((8, 128), jnp.int32)
            for within in range(16):
                code = jnp.where(lane // 8 == within, number_of(within), code)
            return code

        per_term = blocks // 16
        for parity, couples in enumerate(((0, 1, 2), (1, 0, 2))):
            for vector in range(3 * per_term):
                couple, first = couples[vector // per_term], vector % per_term * 16
                slot = spell(lambda within: slot_idx[0, couple, 0, first + within])
                place = jnp.where(slot % 2 == parity, slot // 2 * 8 + lane % 8, -1)
                edge_code[parity, :, vector * 128 : vector * 128 + 128] = place
            for vector in range(owner_code.shape[2] // 128):
                pairs = per_peer // 2

                def owner(within):
                    at = vector * 16 + within
                    return send_idx[at % pairs * 2 + parity, at // pairs]

                place = spell(owner) * 8 + lane % 8
                owner_code[parity, :, vector * 128 : vector * 128 + 128] = place

        def hot(target, codes):
            def body(chunk, _):
                rows = lax.broadcasted_iota(jnp.int32, (64, target.shape[1]), 0) + chunk * 64
                target[pl.ds(pl.multiple_of(chunk * 64, 64), 64), :] = jnp.where(
                    rows == codes[0:1, :], 1.0, 0.0
                ).astype(BF16)
                return 0

            lax.fori_loop(0, target.shape[0] // 64, body, 0)

        for parity in range(2):
            hot(edge_hot.at[parity], edge_code.at[parity])

        @pl.when(level < levels - 1)
        def _():
            for parity in range(2):
                hot(owner_hot.at[parity], owner_code.at[parity])

    def gathered(indices, source, group):
        firsts, thirds = [], []
        for member in range(GROUP):
            first, second, third = [source[at] for at in indices(group * GROUP + member)]
            firsts.append(jnp.where(low_half8, first, second))
            thirds.append(third)
        third = jnp.concatenate(thirds, axis=0)[:, :BS]
        return jnp.concatenate([jnp.concatenate(firsts, axis=0), third], axis=1).astype(BF16)

    def own_block(product, member):
        lanes = slice((member // 2) * 128, (member // 2) * 128 + 128)
        piece = product[member * 8 : member * 8 + 8, lanes]
        turn = pltpu.roll(piece, BS, 1)
        if member % 2 == 0:
            return jnp.where(low_half8, piece, turn)
        return jnp.where(low_half8, turn, piece)

    def spread(source, group):
        members = []
        for member in range(GROUP):
            value = source[group * GROUP + member]
            if member % 2 == 0:
                kept = jnp.where(low_half8, value, zero8)
            else:
                kept = jnp.where(low_half8, zero8, value)
            pair = [kept, zero8] if member < 2 else [zero8, kept]
            members.append(jnp.concatenate(pair, axis=1))
        return jnp.concatenate(members, axis=0).astype(BF16)

    def forward_step(multiply, indices, source, half, color):
        def body(group, _):
            product = multiply(gathered(indices, source, group), group)
            for member in range(GROUP):
                block = group * GROUP + member
                reduced[block] = rhs[half, color, block] - own_block(product, member)
            return 0

        lax.fori_loop(0, groups, body, 0, unroll=groups)
        solved[half, color] = reduced[...]

    def by_piece(piece):
        return lambda rows, group: jnp.dot(
            rows, mats[piece * groups + group], preferred_element_type=F32
        )

    def remote_indices(block):
        return [slot_idx[0, couple, 0, block] for couple in range(3)]

    def lower_indices(color):
        return lambda block: [low_idx[0, color - 1, couple, 0, block] for couple in range(3)]

    prepare_rhs()

    @pl.when(level == 0)
    def _():
        flatten_piece(0, 0)

    identity[...] = jnp.where(
        lax.broadcasted_iota(jnp.int32, (256, 256), 0) == lax.broadcasted_iota(jnp.int32, (256, 256), 1),
        1.0,
        0.0,
    ).astype(BF16)

    ahead = jnp.where(level == 0, 0, jnp.where(level == levels - 1, pieces, steps + 1))
    lax.fori_loop(0, ahead, prepare_lower, 0)

    @pl.when(level >= 2)
    def _():
        prepare_sums()

    pl.semaphore_wait(
        barrier, parts * ((level > 0).astype(jnp.int32) + (level < levels - 1).astype(jnp.int32))
    )

    def peer_rows(peer):
        return pl.ds(pl.multiple_of(peer * rows_per_peer, 16), rows_per_peer)

    def forward_half(half, _):
        @pl.when(level == 0)
        def _():
            solved[half, 0] = rhs[half, 0]

            def color_body(color, _):
                @pl.when((half == 0) & (color > 1))
                def _():
                    flatten_piece(color - 1, color - 1)

                forward_step(
                    lambda rows, group: dot_rows(rows, flat[(color - 1) * groups + group, :, :DEPTH]),
                    lower_indices(color),
                    solved.at[half, color - 1],
                    half,
                    color,
                )
                return 0

            lax.fori_loop(1, colors, color_body, 0)

        @pl.when(level > 0)
        def _():
            pltpu.make_async_copy(recv_f.at[half], recv_f.at[half], sems.at[2 + half]).wait()

            def body(pair, _):
                both = recv_f[half, pl.ds(pl.multiple_of(pair * 16, 16), 16), :].astype(F32)
                for side in range(2):
                    line = both[side * 8 : side * 8 + 8]
                    turn = pltpu.roll(line, BS, 1)
                    rtable[pair * 4 + side * 2] = jnp.where(low_half8, line, turn)
                    rtable[pair * 4 + side * 2 + 1] = jnp.where(low_half8, turn, line)
                return 0

            lax.fori_loop(0, recv_f.shape[1] // 16, body, 0, unroll=8)
            forward_step(by_piece(remote_piece), remote_indices, rtable, half, 0)

            def color_body(color, _):
                forward_step(
                    by_piece(color - 1), lower_indices(color), solved.at[half, color - 1], half, color
                )
                return 0

            lax.fori_loop(1, colors, color_body, 0)

        @pl.when(level < levels - 1)
        def _():
            for peer in peers:
                lines = []
                for pair in range(per_peer // 2):
                    even, odd = reduced[send_idx[pair * 2, peer]], reduced[send_idx[pair * 2 + 1, peer]]
                    lines.append(jnp.where(low_half8, even, odd))
                send_f[half, peer_rows(peer), :] = jnp.concatenate(lines, axis=0).astype(BF16)
                pltpu.make_async_remote_copy(
                    src_ref=send_f.at[half, peer_rows(peer)],
                    dst_ref=recv_f.at[half, peer_rows(me)],
                    send_sem=sems.at[half],
                    recv_sem=sems.at[2 + half],
                    device_id=(level + 1, peer),
                    device_id_type=MESH,
                ).start()

        return 0

    lax.fori_loop(0, 2, forward_half, 0)

    @pl.when(level == 0)
    def _():
        await_piece(remote_piece)

    @pl.when(level < 2)
    def _():
        prepare_sums()

    lax.fori_loop(0, jnp.where(level == levels - 1, 0, steps), prepare_upper, 0)

    def scale(color, source, put):
        def body(group, _):
            product = jnp.dot(
                spread(source, group), mat_dinv[color * groups + group], preferred_element_type=F32
            )
            for member in range(GROUP):
                put(group * GROUP + member, product[member * 8 : member * 8 + 8])
            return 0

        lax.fori_loop(0, groups, body, 0, unroll=groups)

    def scale_solved(at, _):
        half, color = at // steps, lax.rem(at, steps)

        def put(block, value):
            rhs[half, color, block] = value

        scale(color, solved.at[half, color], put)
        return 0

    @pl.when(level < levels - 1)
    def _():
        lax.fori_loop(0, 2 * steps, scale_solved, 0)

    @pl.when(level == levels - 1)
    def _():
        for half in range(2):
            for color in range(steps):
                rhs[half, color] = solved[half, color]


    def store_out(color):
        for first in range(0, blocks, 16):
            values = []
            for slot in range(16):
                zero_half, one_half = table[0, color, first + slot], table[1, color, first + slot]
                even = jnp.where(top_half8, zero_half, one_half)
                odd = pltpu.roll(jnp.where(top_half8, one_half, zero_half), 4, 0)
                values.append(jnp.where(low_half8, even, odd)[None])
            rows = jnp.concatenate(values, axis=0).reshape(16, 16 * BS)
            out[color, first : first + 16, :] = rows.astype(BF16)

    low_lanes = lax.broadcasted_iota(jnp.int32, upward.shape, 1) < BS
    low_sums = lax.broadcasted_iota(jnp.int32, send_b.shape[1:], 1) < BS

    def backward_half(half, _):
        @pl.when(level == levels - 1)
        def _():
            reduced[...] = solved[half, colors - 1]

        @pl.when(level < levels - 1)
        def _():
            pltpu.make_async_copy(recv_b.at[half], recv_b.at[half], sems.at[6 + half]).wait()
            even = jnp.dot(owner_hot[0], recv_b[half], preferred_element_type=F32)
            odd = jnp.dot(owner_hot[1], recv_b[half], preferred_element_type=F32)
            upward[...] = jnp.where(low_lanes, even, odd)

            def last_color(block, _):
                parts_of = upward[pl.ds(pl.multiple_of(block * 8, 8), 8), :]
                reduced[block] = solved[half, colors - 1, block] - (parts_of + pltpu.roll(parts_of, BS, 1))
                return 0

            lax.fori_loop(0, blocks, last_color, 0, unroll=blocks)

        def put_last(block, value):
            table[half, colors - 1, block] = value

        scale(colors - 1, reduced, put_last)

        def back_color(step, _):
            color = colors - 2 - step
            source = table.at[half, color + 1]
            store_out(color + 1)
            multiply = by_piece(steps + 1 + color)

            def indices(block):
                return [up_idx[0, color, couple, 0, block] for couple in range(3)]

            def body(group, _):
                product = multiply(gathered(indices, source, group), group)
                for member in range(GROUP):
                    block = group * GROUP + member
                    reduced[block] = rhs[half, color, block] - own_block(product, member)
                return 0

            lax.fori_loop(0, groups, body, 0, unroll=groups)

            @pl.when(level < levels - 1)
            def _():
                table[half, color] = reduced[...]

            @pl.when(level == levels - 1)
            def _():
                def put(block, value):
                    table[half, color, block] = value

                scale(color, reduced, put)

            return 0

        lax.fori_loop(0, steps, back_color, 0)

        @pl.when(level > 0)
        def _():
            def body(group, _):
                product = jnp.dot(
                    spread(table.at[half, 0], group), mat_urem[group], preferred_element_type=F32
                )
                both, third = product[:, :128], product[:, 128:]
                for term, value in enumerate((both, pltpu.roll(both, BS, 1), third)):
                    at = term * blocks * 8 + group * GROUP * 8
                    terms[pl.ds(pl.multiple_of(at, GROUP * 8), GROUP * 8), :] = value.astype(BF16)
                return 0

            lax.fori_loop(0, groups, body, 0, unroll=groups)
            even = jnp.dot(edge_hot[0], terms[...], preferred_element_type=F32)
            odd = jnp.dot(edge_hot[1], terms[...], preferred_element_type=F32)
            send_b[half] = jnp.where(low_sums, even, odd).astype(BF16)
            for peer in peers:
                pltpu.make_async_remote_copy(
                    src_ref=send_b.at[half, peer_rows(peer)],
                    dst_ref=recv_b.at[half, peer_rows(me)],
                    send_sem=sems.at[4 + half],
                    recv_sem=sems.at[6 + half],
                    device_id=(level - 1, peer),
                    device_id_type=MESH,
                ).start()

        return 0

    lax.fori_loop(0, 2, backward_half, 0)
    store_out(0)

    for half in range(2):

        @pl.when(level > 0)
        def _():
            pltpu.make_async_copy(send_b.at[half], send_b.at[half], sems.at[4 + half]).wait()

        @pl.when(level < levels - 1)
        def _():
            pltpu.make_async_copy(send_f.at[half], send_f.at[half], sems.at[half]).wait()


def per_device(
    levels,
    parts,
    rhs,
    dinv,
    lower_local,
    lower_nbrs,
    upper_local,
    upper_nbrs,
    lower_remote,
    upper_remote,
    remote_slots,
    send_list,
):
    colors, blocks, features = rhs.shape[2:]
    entries = dinv.shape[-1]
    steps, pieces = colors - 1, 2 * colors - 1
    groups = blocks // GROUP
    slots = parts * send_list.shape[-1]

    smem = pl.BlockSpec(memory_space=pltpu.SMEM)
    vmem = pl.BlockSpec(memory_space=pltpu.VMEM)
    hbm = pl.BlockSpec(memory_space=pl.ANY)
    answer = pl.pallas_call(
        functools.partial(kernel, levels, parts),
        out_shape=jax.ShapeDtypeStruct((colors, blocks, features), BF16),
        in_specs=[smem] * 4 + [hbm] * 6,
        out_specs=vmem,
        scratch_shapes=[
            pltpu.VMEM((colors, blocks, features), F32),
            pltpu.VMEM((pieces, 3, blocks, entries), BF16),
            pltpu.VMEM((3, blocks, entries), BF16),
            pltpu.VMEM((colors, blocks, entries), BF16),
            pltpu.VMEM((steps * groups, GROUP * BS, 256), BF16),
            pltpu.VMEM((pieces * groups, DEPTH, GROUP * BS), BF16),
            pltpu.VMEM((groups, GROUP * BS, 256), BF16),
            pltpu.VMEM((colors * groups, BS, GROUP * BS), BF16),
            pltpu.VMEM((colors * groups, GROUP * BS, 2 * BS), BF16),
            pltpu.VMEM((256, 256), BF16),
            pltpu.VMEM((2, colors, blocks, 8, 128), F32),
            pltpu.VMEM((128, 16, 128), F32),
            pltpu.VMEM((2, colors, blocks, 8, 128), F32),
            pltpu.VMEM((blocks, 8, 128), F32),
            pltpu.VMEM((2, colors, blocks, 8, 128), F32),
            pltpu.VMEM((slots, 8, 128), F32),
            pltpu.VMEM((blocks * 8, 128), F32),
            pltpu.VMEM((blocks * 24, 128), BF16),
            pltpu.VMEM((2, 8, blocks * 24), jnp.int32),
            pltpu.VMEM((2, 8, slots * 4), jnp.int32),
            pltpu.VMEM((2, slots * 4, blocks * 24), BF16),
            pltpu.VMEM((2, blocks * 8, slots * 4), BF16),
            pltpu.VMEM((2, slots * 4, 128), BF16),
            pltpu.VMEM((2, slots * 4, 128), BF16),
            pltpu.VMEM((2, slots * 4, 128), BF16),
            pltpu.VMEM((2, slots * 4, 128), BF16),
            pltpu.SemaphoreType.DMA((8,)),
            pltpu.SemaphoreType.DMA((pieces + 3,)),
        ],
        compiler_params=pltpu.CompilerParams(
            collective_id=0, has_side_effects=True, vmem_limit_bytes=60 * 1024 * 1024
        ),
        name="sweeps",
    )(
        jnp.transpose(lower_nbrs, (0, 2, 4, 1, 3)),
        jnp.transpose(upper_nbrs, (0, 2, 4, 1, 3)),
        jnp.transpose(remote_slots, (0, 3, 1, 2)),
        jnp.swapaxes(send_list[0, 0], 0, 1),
        rhs,
        jnp.swapaxes(lower_local, 3, 4),
        jnp.swapaxes(upper_local, 3, 4),
        jnp.swapaxes(lower_remote, 2, 3),
        jnp.swapaxes(upper_remote, 2, 3),
        dinv,
    )
    return answer[None, None]


def solution(mesh):
    levels, parts = mesh.shape["level"], mesh.shape["dom"]
    return jax.shard_map(
        functools.partial(per_device, levels, parts),
        mesh=mesh,
        in_specs=(
            P("level", "dom", None, None, None),
            P("level", "dom", None, None, None),
            P("level", "dom", None, None, None, None),
            P("level", "dom", None, None, None),
            P("level", "dom", None, None, None, None),
            P("level", "dom", None, None, None),
            P("level", "dom", None, None, None),
            P("level", "dom", None, None, None),
            P("level", "dom", None, None),
            P("level", "dom", None, None),
        ),
        out_specs=P("level", "dom", None, None, None),
        check_vma=False,
    )
```

```python
import functools

import jax
import jax.numpy as jnp
from jax import lax
from jax.experimental import pallas as pl
from jax.experimental.pallas import tpu as pltpu
from jax.sharding import PartitionSpec as P

BS = 64
GROUP = 4
DEPTH = 3 * BS
MESH = pl.DeviceIdType.MESH
BF16 = jnp.bfloat16
F32 = jnp.float32


def dot_rows(left, right):
    return lax.dot_general(left, right, (((1,), (1,)), ((), ())), preferred_element_type=F32)


def far_first(parts):
    if parts != 32:
        return [(0, 0, step) for step in range(parts)], (1, 1, parts)
    hops = lambda step: min(step, 4 - step)
    steps = [(z, y, core) for z in range(4) for y in range(4) for core in range(2)]
    steps.sort(key=lambda at: -(hops(at[0]) + hops(at[1]) + 0.5 * at[2]))
    return steps, (4, 4, 2)


def kernel(
    levels,
    parts,
    low_idx,
    up_idx,
    slot_idx,
    send_idx,
    rhs_hbm,
    low_hbm,
    up_hbm,
    lrem_hbm,
    urem_hbm,
    dinv_hbm,
    out,
    raw_rhs,
    raw,
    raw_urem,
    raw_dinv,
    flat,
    mats,
    mat_urem,
    w_dinv,
    mat_dinv,
    identity,
    rhs,
    mixed,
    solved,
    reduced,
    table,
    rtable,
    upward,
    terms,
    edge_code,
    owner_code,
    edge_hot,
    owner_hot,
    send_f,
    recv_f,
    send_b,
    recv_b,
    sems,
    load_sems,
):
    level = lax.axis_index("level")
    me = lax.axis_index("dom")
    colors, blocks = solved.shape[1], solved.shape[2]
    steps = colors - 1
    groups = blocks // GROUP
    per_peer = send_idx.shape[0]
    rows_per_peer = send_f.shape[1] // parts
    offsets, sides = far_first(parts)
    at_z, at_y, at_core = me // (sides[1] * sides[2]), lax.rem(me // sides[2], sides[1]), lax.rem(me, sides[2])
    peers = [
        (lax.rem(at_z + z, sides[0]) * sides[1] + lax.rem(at_y + y, sides[1])) * sides[2]
        + lax.rem(at_core + core, sides[2])
        for z, y, core in offsets
    ]
    remote_piece = steps
    pieces = 2 * steps + 1

    def piece_source(piece):
        if piece < steps:
            return low_hbm.at[0, 0, piece]
        if piece == steps:
            return lrem_hbm.at[0, 0]
        return up_hbm.at[0, 0, piece - steps - 1]

    load_rhs = pltpu.make_async_copy(rhs_hbm.at[0, 0], raw_rhs, load_sems.at[pieces])
    load_urem = pltpu.make_async_copy(urem_hbm.at[0, 0], raw_urem, load_sems.at[pieces + 1])
    load_dinv = pltpu.make_async_copy(dinv_hbm.at[0, 0], raw_dinv, load_sems.at[pieces + 2])
    load_rhs.start()
    pltpu.make_async_copy(piece_source(0), raw.at[0], load_sems.at[0]).start()

    def start_loads():
        for piece in range(1, steps + 1):
            pltpu.make_async_copy(piece_source(piece), raw.at[piece], load_sems.at[piece]).start()
        load_dinv.start()
        load_urem.start()
        for piece in range(steps + 1, pieces):
            pltpu.make_async_copy(piece_source(piece), raw.at[piece], load_sems.at[piece]).start()

    barrier = pltpu.get_barrier_semaphore()

    def greet(step, _):
        peer = lax.rem(me + step, parts)

        @pl.when(level > 0)
        def _():
            pl.semaphore_signal(barrier, inc=1, device_id=(level - 1, peer), device_id_type=MESH)

        @pl.when(level < levels - 1)
        def _():
            pl.semaphore_signal(barrier, inc=1, device_id=(level + 1, peer), device_id_type=MESH)

        return 0

    lax.fori_loop(0, parts, greet, 0)

    low_half8 = lax.broadcasted_iota(jnp.int32, (8, 128), 1) < BS
    top_half8 = lax.broadcasted_iota(jnp.int32, (8, 128), 0) < 4
    zero8 = jnp.zeros((8, 128), F32)

    def interleave(slot, first, second):
        first_turned = pltpu.roll(first, BS, 1)
        second_turned = pltpu.roll(second, BS, 1)
        mixed[slot, pl.ds(0, 8, stride=2), :] = jnp.where(low_half8, first, second_turned)
        mixed[slot, pl.ds(1, 8, stride=2), :] = jnp.where(low_half8, first_turned, second)

    def lines_of(source, first, quarter):
        lanes = slice(quarter * 1024, quarter * 1024 + 1024)
        part = source[pl.ds(pl.multiple_of(first, 16), 16), lanes]
        return part.astype(F32).reshape(16, 8, 128)

    def await_piece(piece):
        pltpu.make_async_copy(lrem_hbm.at[0, 0], raw.at[piece], load_sems.at[piece]).wait()

    def flatten_piece(piece, target):
        await_piece(piece)

        def body(step, _):
            for quarter in range(4):
                lines = [lines_of(raw.at[piece, couple], step * 16, quarter) for couple in range(3)]
                for slot in range(16):
                    interleave(quarter * 32 + slot, lines[0][slot], lines[1][slot])
                    third = lines[2][slot]
                    turned = pltpu.roll(third, BS, 1)
                    at = quarter * 32 + 16 + slot
                    mixed[at, pl.ds(0, 8, stride=2), :] = third
                    mixed[at, pl.ds(1, 8, stride=2), :] = turned
                for slot in range(16):
                    group = target * groups + step * GROUP + slot // GROUP
                    row = (slot % GROUP) * BS + quarter * 16
                    flat[group, row : row + 16, 0:128] = mixed[quarter * 32 + slot].astype(BF16)
                    flat[group, row : row + 16, 128:DEPTH] = mixed[
                        quarter * 32 + 16 + slot, :, : DEPTH - 128
                    ].astype(BF16)
            return 0

        lax.fori_loop(0, blocks // 16, body, 0, unroll=4)

    def turned(rows):
        return dot_rows(identity[: rows.shape[1], : rows.shape[1]], rows).astype(BF16)

    def prepare_lower(piece, _):
        flatten_piece(piece, 0)

        def body(group, _):
            mats[piece * groups + group] = turned(flat[group, :, :DEPTH])
            return 0

        lax.fori_loop(0, groups, body, 0, unroll=groups)
        return 0

    member_lane = lax.broadcasted_iota(jnp.int32, (BS, GROUP * BS), 1) // BS

    def prepare_upper(color, _):
        piece = steps + 1 + color
        flatten_piece(piece, 0)

        def body(group, _):
            inverses = w_dinv[color * groups + group]
            apart = [
                jnp.where(member_lane == member, inverses, jnp.zeros_like(inverses))
                for member in range(GROUP)
            ]
            product = dot_rows(turned(flat[group, :, :DEPTH]), jnp.concatenate(apart, axis=0))
            mats[piece * groups + group] = product.astype(BF16)
            return 0

        lax.fori_loop(0, groups, body, 0, unroll=4)
        return 0

    def prepare_rhs():
        load_rhs.wait()
        start_loads()

        def body(step, _):
            color, first = step // (blocks // 8), lax.rem(step, blocks // 8) * 8
            lines = raw_rhs[color, pl.ds(pl.multiple_of(first, 8), 8), :].reshape(8, 8, 128)
            for slot in range(8):
                line = lines[slot]
                turn = pltpu.roll(line, BS, 1)
                even = jnp.where(low_half8, line, turn)
                odd = pltpu.roll(jnp.where(low_half8, turn, line), 4, 0)
                rhs[0, color, first + slot] = jnp.where(top_half8, even, odd)
                rhs[1, color, first + slot] = jnp.where(top_half8, odd, even)
            return 0

        lax.fori_loop(0, colors * blocks // 8, body, 0, unroll=8)

    def prepare_sums():
        load_dinv.wait()

        def dinv_body(step, _):
            color, first = step // (blocks // 16), lax.rem(step, blocks // 16) * 16
            for quarter in range(4):
                lines = lines_of(raw_dinv.at[color], first, quarter)
                for pair in range(8):
                    interleave(quarter * 8 + pair, lines[2 * pair], lines[2 * pair + 1])
                for pair in range(8):
                    group = color * groups + first // GROUP + pair // 2
                    lanes = slice((pair % 2) * 128, (pair % 2) * 128 + 128)
                    value = mixed[quarter * 8 + pair].astype(BF16)
                    w_dinv[group, quarter * 16 : quarter * 16 + 16, lanes] = value
            return 0

        lax.fori_loop(0, colors * blocks // 16, dinv_body, 0)

        def dinv_turn(group, _):
            inverses = w_dinv[group]
            mat_dinv[group] = turned(jnp.concatenate([inverses, inverses], axis=0))
            return 0

        lax.fori_loop(0, colors * groups, dinv_turn, 0, unroll=groups)
        load_urem.wait()

        def urem_body(step, _):
            for quarter in range(4):
                for couple in range(3):
                    lines = lines_of(raw_urem.at[couple], step * 16, quarter)
                    for pair in range(8):
                        interleave(quarter * 24 + couple * 8 + pair, lines[2 * pair], lines[2 * pair + 1])
                    for pair in range(8):
                        group = step * GROUP + pair // 2
                        lanes = slice((pair % 2) * 128, (pair % 2) * 128 + 128)
                        value = mixed[quarter * 24 + couple * 8 + pair].astype(BF16)
                        row = couple * BS + quarter * 16
                        flat[group, row : row + 16, lanes] = value
                        if couple == 2:
                            flat[group, row + BS : row + BS + 16, lanes] = value
            return 0

        lax.fori_loop(0, blocks // 16, urem_body, 0)

        def urem_turn(group, _):
            mat_urem[group] = turned(flat[group])
            return 0

        lax.fori_loop(0, groups, urem_turn, 0, unroll=groups)

        lane = lax.broadcasted_iota(jnp.int32, (8, 128), 1)

        def spell(number_of):
            code = jnp.zeros((8, 128), jnp.int32)
            for within in range(16):
                code = jnp.where(lane // 8 == within, number_of(within), code)
            return code

        per_term = blocks // 16
        for parity, couples in enumerate(((0, 1, 2), (1, 0, 2))):
            for vector in range(3 * per_term):
                couple, first = couples[vector // per_term], vector % per_term * 16
                slot = spell(lambda within: slot_idx[0, couple, 0, first + within])
                place = jnp.where(slot % 2 == parity, slot // 2 * 8 + lane % 8, -1)
                edge_code[parity, :, vector * 128 : vector * 128 + 128] = place
            for vector in range(owner_code.shape[2] // 128):
                pairs = per_peer // 2

                def owner(within):
                    at = vector * 16 + within
                    return send_idx[at % pairs * 2 + parity, at // pairs]

                place = spell(owner) * 8 + lane % 8
                owner_code[parity, :, vector * 128 : vector * 128 + 128] = place

        def hot(target, codes):
            def body(chunk, _):
                rows = lax.broadcasted_iota(jnp.int32, (64, target.shape[1]), 0) + chunk * 64
                target[pl.ds(pl.multiple_of(chunk * 64, 64), 64), :] = jnp.where(
                    rows == codes[0:1, :], 1.0, 0.0
                ).astype(BF16)
                return 0

            lax.fori_loop(0, target.shape[0] // 64, body, 0)

        for parity in range(2):
            hot(edge_hot.at[parity], edge_code.at[parity])

        @pl.when(level < levels - 1)
        def _():
            for parity in range(2):
                hot(owner_hot.at[parity], owner_code.at[parity])

    def gathered(indices, source, group):
        firsts, thirds = [], []
        for member in range(GROUP):
            first, second, third = [source[at] for at in indices(group * GROUP + member)]
            firsts.append(jnp.where(low_half8, first, second))
            thirds.append(third)
        third = jnp.concatenate(thirds, axis=0)[:, :BS]
        return jnp.concatenate([jnp.concatenate(firsts, axis=0), third], axis=1).astype(BF16)

    def own_block(product, member):
        lanes = slice((member // 2) * 128, (member // 2) * 128 + 128)
        piece = product[member * 8 : member * 8 + 8, lanes]
        turn = pltpu.roll(piece, BS, 1)
        if member % 2 == 0:
            return jnp.where(low_half8, piece, turn)
        return jnp.where(low_half8, turn, piece)

    def spread(source, group):
        members = []
        for member in range(GROUP):
            value = source[group * GROUP + member]
            if member % 2 == 0:
                kept = jnp.where(low_half8, value, zero8)
            else:
                kept = jnp.where(low_half8, zero8, value)
            pair = [kept, zero8] if member < 2 else [zero8, kept]
            members.append(jnp.concatenate(pair, axis=1))
        return jnp.concatenate(members, axis=0).astype(BF16)

    def forward_step(multiply, indices, source, half, color):
        def body(group, _):
            product = multiply(gathered(indices, source, group), group)
            for member in range(GROUP):
                block = group * GROUP + member
                reduced[block] = rhs[half, color, block] - own_block(product, member)
            return 0

        lax.fori_loop(0, groups, body, 0, unroll=groups)
        solved[half, color] = reduced[...]

    def by_piece(piece):
        return lambda rows, group: jnp.dot(
            rows, mats[piece * groups + group], preferred_element_type=F32
        )

    def remote_indices(block):
        return [slot_idx[0, couple, 0, block] for couple in range(3)]

    def lower_indices(color):
        return lambda block: [low_idx[0, color - 1, couple, 0, block] for couple in range(3)]

    prepare_rhs()

    @pl.when(level == 0)
    def _():
        flatten_piece(0, 0)

    identity[...] = jnp.where(
        lax.broadcasted_iota(jnp.int32, (256, 256), 0) == lax.broadcasted_iota(jnp.int32, (256, 256), 1),
        1.0,
        0.0,
    ).astype(BF16)

    ahead = jnp.where(level == 0, 0, jnp.where(level == levels - 1, pieces, steps + 1))
    lax.fori_loop(0, ahead, prepare_lower, 0)

    @pl.when(level >= 2)
    def _():
        prepare_sums()

    pl.semaphore_wait(
        barrier, parts * ((level > 0).astype(jnp.int32) + (level < levels - 1).astype(jnp.int32))
    )

    def peer_rows(peer):
        return pl.ds(pl.multiple_of(peer * rows_per_peer, 16), rows_per_peer)

    def forward_half(half, _):
        @pl.when(level == 0)
        def _():
            solved[half, 0] = rhs[half, 0]

            def color_body(color, _):
                @pl.when((half == 0) & (color > 1))
                def _():
                    flatten_piece(color - 1, color - 1)

                forward_step(
                    lambda rows, group: dot_rows(rows, flat[(color - 1) * groups + group, :, :DEPTH]),
                    lower_indices(color),
                    solved.at[half, color - 1],
                    half,
                    color,
                )
                return 0

            lax.fori_loop(1, colors, color_body, 0)

        @pl.when(level > 0)
        def _():
            pltpu.make_async_copy(recv_f.at[half], recv_f.at[half], sems.at[2 + half]).wait()

            def body(pair, _):
                both = recv_f[half, pl.ds(pl.multiple_of(pair * 16, 16), 16), :].astype(F32)
                for side in range(2):
                    line = both[side * 8 : side * 8 + 8]
                    turn = pltpu.roll(line, BS, 1)
                    rtable[pair * 4 + side * 2] = jnp.where(low_half8, line, turn)
                    rtable[pair * 4 + side * 2 + 1] = jnp.where(low_half8, turn, line)
                return 0

            lax.fori_loop(0, recv_f.shape[1] // 16, body, 0, unroll=8)
            forward_step(by_piece(remote_piece), remote_indices, rtable, half, 0)

            def color_body(color, _):
                forward_step(
                    by_piece(color - 1), lower_indices(color), solved.at[half, color - 1], half, color
                )
                return 0

            lax.fori_loop(1, colors, color_body, 0)

        @pl.when(level < levels - 1)
        def _():
            for peer in peers:
                lines = []
                for pair in range(per_peer // 2):
                    even, odd = reduced[send_idx[pair * 2, peer]], reduced[send_idx[pair * 2 + 1, peer]]
                    lines.append(jnp.where(low_half8, even, odd))
                send_f[half, peer_rows(peer), :] = jnp.concatenate(lines, axis=0).astype(BF16)
                pltpu.make_async_remote_copy(
                    src_ref=send_f.at[half, peer_rows(peer)],
                    dst_ref=recv_f.at[half, peer_rows(me)],
                    send_sem=sems.at[half],
                    recv_sem=sems.at[2 + half],
                    device_id=(level + 1, peer),
                    device_id_type=MESH,
                ).start()

        return 0

    lax.fori_loop(0, 2, forward_half, 0)

    @pl.when(level == 0)
    def _():
        await_piece(remote_piece)

    @pl.when(level < 2)
    def _():
        prepare_sums()

    lax.fori_loop(0, jnp.where(level == levels - 1, 0, steps), prepare_upper, 0)

    def scale(color, source, put):
        def body(group, _):
            product = jnp.dot(
                spread(source, group), mat_dinv[color * groups + group], preferred_element_type=F32
            )
            for member in range(GROUP):
                put(group * GROUP + member, product[member * 8 : member * 8 + 8])
            return 0

        lax.fori_loop(0, groups, body, 0, unroll=groups)

    def scale_solved(at, _):
        half, color = at // steps, lax.rem(at, steps)

        def put(block, value):
            rhs[half, color, block] = value

        scale(color, solved.at[half, color], put)
        return 0

    @pl.when(level < levels - 1)
    def _():
        lax.fori_loop(0, 2 * steps, scale_solved, 0)

    @pl.when(level == levels - 1)
    def _():
        for half in range(2):
            for color in range(steps):
                rhs[half, color] = solved[half, color]


    def store_out(color):
        for first in range(0, blocks, 16):
            values = []
            for slot in range(16):
                zero_half, one_half = table[0, color, first + slot], table[1, color, first + slot]
                even = jnp.where(top_half8, zero_half, one_half)
                odd = pltpu.roll(jnp.where(top_half8, one_half, zero_half), 4, 0)
                values.append(jnp.where(low_half8, even, odd)[None])
            rows = jnp.concatenate(values, axis=0).reshape(16, 16 * BS)
            out[color, first : first + 16, :] = rows.astype(BF16)

    low_lanes = lax.broadcasted_iota(jnp.int32, upward.shape, 1) < BS
    low_sums = lax.broadcasted_iota(jnp.int32, send_b.shape[1:], 1) < BS

    def backward_half(half, _):
        @pl.when(level == levels - 1)
        def _():
            reduced[...] = solved[half, colors - 1]

        @pl.when(level < levels - 1)
        def _():
            pltpu.make_async_copy(recv_b.at[half], recv_b.at[half], sems.at[6 + half]).wait()
            even = jnp.dot(owner_hot[0], recv_b[half], preferred_element_type=F32)
            odd = jnp.dot(owner_hot[1], recv_b[half], preferred_element_type=F32)
            upward[...] = jnp.where(low_lanes, even, odd)

            def last_color(block, _):
                parts_of = upward[pl.ds(pl.multiple_of(block * 8, 8), 8), :]
                reduced[block] = solved[half, colors - 1, block] - (parts_of + pltpu.roll(parts_of, BS, 1))
                return 0

            lax.fori_loop(0, blocks, last_color, 0, unroll=blocks)

        def put_last(block, value):
            table[half, colors - 1, block] = value

        scale(colors - 1, reduced, put_last)

        def back_color(step, _):
            color = colors - 2 - step
            source = table.at[half, color + 1]
            store_out(color + 1)
            multiply = by_piece(steps + 1 + color)

            def indices(block):
                return [up_idx[0, color, couple, 0, block] for couple in range(3)]

            def body(group, _):
                product = multiply(gathered(indices, source, group), group)
                for member in range(GROUP):
                    block = group * GROUP + member
                    reduced[block] = rhs[half, color, block] - own_block(product, member)
                return 0

            lax.fori_loop(0, groups, body, 0, unroll=groups)

            @pl.when(level < levels - 1)
            def _():
                table[half, color] = reduced[...]

            @pl.when(level == levels - 1)
            def _():
                def put(block, value):
                    table[half, color, block] = value

                scale(color, reduced, put)

            return 0

        lax.fori_loop(0, steps, back_color, 0)

        @pl.when(level > 0)
        def _():
            def body(group, _):
                product = jnp.dot(
                    spread(table.at[half, 0], group), mat_urem[group], preferred_element_type=F32
                )
                both, third = product[:, :128], product[:, 128:]
                for term, value in enumerate((both, pltpu.roll(both, BS, 1), third)):
                    at = term * blocks * 8 + group * GROUP * 8
                    terms[pl.ds(pl.multiple_of(at, GROUP * 8), GROUP * 8), :] = value.astype(BF16)
                return 0

            lax.fori_loop(0, groups, body, 0, unroll=groups)
            even = jnp.dot(edge_hot[0], terms[...], preferred_element_type=F32)
            odd = jnp.dot(edge_hot[1], terms[...], preferred_element_type=F32)
            send_b[half] = jnp.where(low_sums, even, odd).astype(BF16)
            for peer in peers:
                pltpu.make_async_remote_copy(
                    src_ref=send_b.at[half, peer_rows(peer)],
                    dst_ref=recv_b.at[half, peer_rows(me)],
                    send_sem=sems.at[4 + half],
                    recv_sem=sems.at[6 + half],
                    device_id=(level - 1, peer),
                    device_id_type=MESH,
                ).start()

        return 0

    lax.fori_loop(0, 2, backward_half, 0)
    store_out(0)

    for half in range(2):

        @pl.when(level > 0)
        def _():
            pltpu.make_async_copy(send_b.at[half], send_b.at[half], sems.at[4 + half]).wait()

        @pl.when(level < levels - 1)
        def _():
            pltpu.make_async_copy(send_f.at[half], send_f.at[half], sems.at[half]).wait()


def per_device(
    levels,
    parts,
    rhs,
    dinv,
    lower_local,
    lower_nbrs,
    upper_local,
    upper_nbrs,
    lower_remote,
    upper_remote,
    remote_slots,
    send_list,
):
    colors, blocks, features = rhs.shape[2:]
    entries = dinv.shape[-1]
    steps, pieces = colors - 1, 2 * colors - 1
    groups = blocks // GROUP
    slots = parts * send_list.shape[-1]

    smem = pl.BlockSpec(memory_space=pltpu.SMEM)
    vmem = pl.BlockSpec(memory_space=pltpu.VMEM)
    hbm = pl.BlockSpec(memory_space=pl.ANY)
    answer = pl.pallas_call(
        functools.partial(kernel, levels, parts),
        out_shape=jax.ShapeDtypeStruct((colors, blocks, features), BF16),
        in_specs=[smem] * 4 + [hbm] * 6,
        out_specs=vmem,
        scratch_shapes=[
            pltpu.VMEM((colors, blocks, features), F32),
            pltpu.VMEM((pieces, 3, blocks, entries), BF16),
            pltpu.VMEM((3, blocks, entries), BF16),
            pltpu.VMEM((colors, blocks, entries), BF16),
            pltpu.VMEM((steps * groups, GROUP * BS, 256), BF16),
            pltpu.VMEM((pieces * groups, DEPTH, GROUP * BS), BF16),
            pltpu.VMEM((groups, GROUP * BS, 256), BF16),
            pltpu.VMEM((colors * groups, BS, GROUP * BS), BF16),
            pltpu.VMEM((colors * groups, GROUP * BS, 2 * BS), BF16),
            pltpu.VMEM((256, 256), BF16),
            pltpu.VMEM((2, colors, blocks, 8, 128), F32),
            pltpu.VMEM((128, 16, 128), F32),
            pltpu.VMEM((2, colors, blocks, 8, 128), F32),
            pltpu.VMEM((blocks, 8, 128), F32),
            pltpu.VMEM((2, colors, blocks, 8, 128), F32),
            pltpu.VMEM((slots, 8, 128), F32),
            pltpu.VMEM((blocks * 8, 128), F32),
            pltpu.VMEM((blocks * 24, 128), BF16),
            pltpu.VMEM((2, 8, blocks * 24), jnp.int32),
            pltpu.VMEM((2, 8, slots * 4), jnp.int32),
            pltpu.VMEM((2, slots * 4, blocks * 24), BF16),
            pltpu.VMEM((2, blocks * 8, slots * 4), BF16),
            pltpu.VMEM((2, slots * 4, 128), BF16),
            pltpu.VMEM((2, slots * 4, 128), BF16),
            pltpu.VMEM((2, slots * 4, 128), BF16),
            pltpu.VMEM((2, slots * 4, 128), BF16),
            pltpu.SemaphoreType.DMA((8,)),
            pltpu.SemaphoreType.DMA((pieces + 3,)),
        ],
        compiler_params=pltpu.CompilerParams(
            collective_id=0, has_side_effects=True, vmem_limit_bytes=60 * 1024 * 1024
        ),
        name="sweeps",
    )(
        jnp.transpose(lower_nbrs, (0, 2, 4, 1, 3)),
        jnp.transpose(upper_nbrs, (0, 2, 4, 1, 3)),
        jnp.transpose(remote_slots, (0, 3, 1, 2)),
        jnp.swapaxes(send_list[0, 0], 0, 1),
        rhs,
        jnp.swapaxes(lower_local, 3, 4),
        jnp.swapaxes(upper_local, 3, 4),
        jnp.swapaxes(lower_remote, 2, 3),
        jnp.swapaxes(upper_remote, 2, 3),
        dinv,
    )
    return answer[None, None]


def solution(mesh):
    levels, parts = mesh.shape["level"], mesh.shape["dom"]
    return jax.shard_map(
        functools.partial(per_device, levels, parts),
        mesh=mesh,
        in_specs=(
            P("level", "dom", None, None, None),
            P("level", "dom", None, None, None),
            P("level", "dom", None, None, None, None),
            P("level", "dom", None, None, None),
            P("level", "dom", None, None, None, None),
            P("level", "dom", None, None, None),
            P("level", "dom", None, None, None),
            P("level", "dom", None, None, None),
            P("level", "dom", None, None),
            P("level", "dom", None, None),
        ),
        out_specs=P("level", "dom", None, None, None),
        check_vma=False,
    )
```
